32 devices in a mesh: blk: 16 (over z, y, x), rep: 2 (over core).
Axes of the slice: x: 2, y: 2, z: 4, core: 2. Of those that a mesh axis runs over, the one named last changes fastest.
Arguments:
- patches: bfloat16 [2, 16384, 768], P('rep', 'blk'), may hold values from -6 to 6
- latents: bfloat16 [2, 512, 768], P('rep', 'blk'), may hold values from -6 to 6
- norm_gain: bfloat16 [5, 768], replicated, may hold values from 0.099609375 to 1.8984375
- norm_bias: bfloat16 [5, 768], replicated, may hold values from -1.75 to 1.75
- read_in: bfloat16 [3, 768, 768], replicated, may hold values from -0.21875 to 0.21875
- read_out: bfloat16 [768, 768], replicated, may hold values from -1.75 to 1.75
- self_in: bfloat16 [3, 768, 768], replicated, may hold values from -0.21875 to 0.21875
- self_out: bfloat16 [768, 768], replicated, may hold values from -2 to 2
- write_in: bfloat16 [3, 768, 768], replicated, may hold values from -0.21875 to 0.21875
- write_out: bfloat16 [768, 768], replicated, may hold values from -0.3125 to 0.3125
- feed_up: bfloat16 [768, 3072], replicated, may hold values from -0.21875 to 0.21875
- feed_down: bfloat16 [3072, 768], replicated, may hold values from -0.109375 to 0.109375
- group_image: int32 [2, 64], P('rep'), may hold values from 0 to 63, as said below
- cot_patches: bfloat16 [2, 16384, 768], P('rep', 'blk'), may hold values from -6 to 6
- cot_latents: bfloat16 [2, 512, 768], P('rep', 'blk'), may hold values from -6 to 6
Outputs:
- out_patches: bfloat16 [2, 16384, 768], P('rep', 'blk')
- out_latents: bfloat16 [2, 512, 768], P('rep', 'blk')
- gradient_patches: bfloat16 [2, 16384, 768], P('rep', 'blk')
- gradient_latents: bfloat16 [2, 512, 768], P('rep', 'blk')
- gradient_gain: float32 [5, 768], P(None, 'blk')
- gradient_bias: float32 [5, 768], P(None, 'blk')
- gradient_read_in: float32 [3, 768, 768], P(None, 'blk')
- gradient_read_out: float32 [768, 768], P('blk')
- gradient_self_in: float32 [3, 768, 768], P(None, 'blk')
- gradient_self_out: float32 [768, 768], P('blk')
- gradient_write_in: float32 [3, 768, 768], P(None, 'blk')
- gradient_write_out: float32 [768, 768], P('blk')
- gradient_up: float32 [768, 3072], P('blk')
- gradient_down: float32 [3072, 768], P('blk')
The draws below stay inside these ranges and needn't reach their ends.
Inputs may be any that keep to these rules, and one draw needn't show every extreme that they name: `group_image`: along each row ids never fall and the groups of one image are contiguous; an image's id is the index of its last group. Group 0 is an image of its own, and one image runs from one of the first 4 groups to one of the last 4 groups of its row.
All inputs are finite; a program needn't handle non-finite values.
Results may differ from the reference program's by a relative error of at most 0.025.
Values may be sent and summed in bfloat16 or wider, within the bound.
No kernel may reach another device: no remote copies, remote signals or barrier semaphores. Data moves between devices by JAX's collectives and lax.ppermute only.
A program may use at most 192 MiB of HBM per device.

```python
import jax
import jax.numpy as jnp
from jax import lax

D = 768
HEADS = 12
HEAD = 64
FF = 3072
GROUP = 256
LAT = 8
GPD = 4
TOK_ROW = 16384
LAT_ROW = 512
N_BLK = 16
N_REP = 2


def draw_group_image(key, part):
    key = jax.random.fold_in(key, 7)
    groups = GPD * N_BLK
    key_first, key_last, key_bits = jax.random.split(key, 3)
    first_group = jax.random.randint(key_first, (N_REP, 1), 1, GPD)
    last_group = jax.random.randint(key_last, (N_REP, 1), groups - GPD, groups)
    indices = jnp.arange(groups, dtype=jnp.int32)[None, :]
    random_bits = jax.random.randint(key_bits, (N_REP, groups), 0, 2)
    inside = (indices >= first_group) & (indices < last_group)
    endings = (indices == first_group - 1) | (indices == last_group) | (indices == groups - 1) | (indices == 0)
    boundary = jnp.where(endings, 1, jnp.where(inside, 0, random_bits))
    marks = jnp.where(boundary == 1, indices, groups)
    return lax.cummin(marks, axis=1, reverse=True).astype(jnp.int32)


def levels(own_key, shape, cuts, low, high):
    level = 1.0
    for position, shards_of in cuts:
        heights = jax.random.uniform(jax.random.fold_in(jax.random.fold_in(own_key, 6), position), (shards_of,), jnp.float32, low / len(cuts), high / len(cuts))
        level = level * jnp.repeat(jnp.exp(heights), shape[position] // shards_of).reshape((-1,) + (1,) * (len(shape) - 1 - position))
    return level


def gaussian(own_key, dims, scale, most, cuts=(), kind=jnp.bfloat16):
    values = jax.random.normal(own_key, dims, jnp.float32) * scale
    if len(cuts) > 0:
        values = levels(own_key, dims, cuts, -0.22, 0.18) * values
    return jnp.clip(values, min=-most, max=most).astype(kind)


def setup_inputs(seed: int = 0) -> dict:
    keys = jax.random.split(jax.random.key(seed), 16)
    patches = gaussian(keys[0], (N_REP, TOK_ROW, D), 1.0, 6.0, ((0, 2), (1, 16)))
    latents = gaussian(keys[1], (N_REP, LAT_ROW, D), 1.0, 6.0, ((0, 2), (1, 16)))
    norm_gain = jnp.clip(1.0 + 0.18 * jax.random.normal(keys[2], (5, D), jnp.float32), 0.099609375, 1.8984375).astype(jnp.bfloat16)
    norm_bias = gaussian(keys[3], (5, D), 0.3, 1.75)
    read_in = gaussian(keys[4], (3, D, D), D ** -0.5, 0.21875)
    read_out = gaussian(keys[5], (D, D), (max(1, 4 * D // GROUP)) ** -0.5, 1.75)
    self_in = gaussian(keys[6], (3, D, D), D ** -0.5, 0.21875)
    self_out = gaussian(keys[7], (D, D), (max(8, 4 * D // (LAT * GPD * N_BLK))) ** -0.5, 2.0)
    write_in = gaussian(keys[8], (3, D, D), D ** -0.5, 0.21875)
    write_out = gaussian(keys[9], (D, D), (4 * D // LAT) ** -0.5, 0.3125)
    feed_up = gaussian(keys[10], (D, FF), D ** -0.5, 0.21875)
    feed_down = gaussian(keys[11], (FF, D), FF ** -0.5, 0.109375)
    group_image = draw_group_image(jax.random.fold_in(keys[15], 71), 0)
    cot_patches = gaussian(keys[13], (N_REP, TOK_ROW, D), 1.0, 6.0, ((0, 2), (1, 16)))
    cot_latents = gaussian(keys[14], (N_REP, LAT_ROW, D), 1.0, 6.0, ((0, 2), (1, 16)))
    return dict(patches=patches, latents=latents, norm_gain=norm_gain, norm_bias=norm_bias, read_in=read_in, read_out=read_out, self_in=self_in, self_out=self_out, write_in=write_in, write_out=write_out, feed_up=feed_up, feed_down=feed_down, group_image=group_image, cot_patches=cot_patches, cot_latents=cot_latents)


@jax.custom_vjp
def low(v):
    return lax.optimization_barrier(v.astype(jnp.bfloat16)).astype(jnp.float32)

@jax.custom_vjp
def low_back(v):
    return v

def low_keep(v):
    return (low(v), None)

def low_pass(kept, grad):
    return (grad,)

def back_keep(v):
    return (v, None)

def back_low(kept, grad):
    return (low(grad),)
low.defvjp(low_keep, low_pass)
low_back.defvjp(back_keep, back_low)

def product(left, right):
    return jnp.dot(left, right, precision=lax.Precision.HIGHEST, preferred_element_type=jnp.float32)

def rounded(tensor):
    return low(low_back(tensor))

def layer_norm(tensor, scale_row, shift_row):
    center = tensor - lax.optimization_barrier(jnp.mean(tensor, axis=-1, keepdims=True))
    spread = lax.optimization_barrier(jnp.mean(center * center, axis=-1, keepdims=True))
    return center * lax.rsqrt(spread + 1e-06) * scale_row + shift_row

def gelu_value(tensor):
    return 0.5 * tensor * (1.0 + lax.erf(tensor * 0.7071067811865476))

def split_heads(tensor, blocks):
    return tensor.reshape(blocks, -1, HEADS, HEAD)

def attention(queries, key_rows, values, allowed):
    factor = HEAD ** (-0.5)
    scores = low_back(jnp.einsum('bqhe,bkhe->bhqk', queries, key_rows, precision=lax.Precision.HIGHEST) * factor)
    if allowed is not None:
        scores = jnp.where(allowed, scores, -1e+30)
    highest = lax.optimization_barrier(jnp.max(scores, axis=-1, keepdims=True))
    powers = jnp.exp(scores - highest)
    shares = low(powers / lax.optimization_barrier(jnp.sum(powers, axis=-1, keepdims=True)))
    return jnp.einsum('bhqk,bkhe->bqhe', shares, values, precision=lax.Precision.HIGHEST)

def row_forward(patch_rows, latent_rows, images, gain, shift, read_in, read_out, self_in, self_out, write_in, write_out, feed_up, feed_down):
    groups = images.shape[0]
    lat_total = latent_rows.shape[0]
    tok_total = patch_rows.shape[0]
    query_src = low(layer_norm(latent_rows, gain[0], shift[0]))
    patch_src = low(layer_norm(patch_rows, gain[1], shift[1]))
    queries = rounded(product(query_src, read_in[0]))
    key_rows = rounded(product(patch_src, read_in[1]))
    values = rounded(product(patch_src, read_in[2]))
    mixture = attention(split_heads(queries, groups), split_heads(key_rows, groups), split_heads(values, groups), None)
    mixture = rounded(mixture.reshape(lat_total, D))
    after_read = latent_rows + low_back(product(mixture, read_out))
    latent_src = low(layer_norm(after_read, gain[2], shift[2]))
    queries = rounded(product(latent_src, self_in[0]))
    key_rows = rounded(product(latent_src, self_in[1]))
    values = rounded(product(latent_src, self_in[2]))
    owners = jnp.repeat(images, LAT)
    allowed = (owners[:, None] == owners[None, :])[None, None]
    mixture = attention(split_heads(queries, 1), split_heads(key_rows, 1), split_heads(values, 1), allowed)
    mixture = rounded(mixture.reshape(lat_total, D))
    after_self = after_read + low_back(product(mixture, self_out))
    latent_src = low(layer_norm(after_self, gain[3], shift[3]))
    queries = rounded(product(patch_src, write_in[0]))
    key_rows = rounded(product(latent_src, write_in[1]))
    values = rounded(product(latent_src, write_in[2]))
    mixture = attention(split_heads(queries, groups), split_heads(key_rows, groups), split_heads(values, groups), None)
    mixture = rounded(mixture.reshape(tok_total, D))
    written = patch_rows + low_back(product(mixture, write_out))
    hidden_src = low(layer_norm(written, gain[4], shift[4]))
    hidden = low_back(product(hidden_src, feed_up))
    active = low(gelu_value(hidden))
    result = written + low_back(product(active, feed_down))
    return (result, after_self)

def reference(patches, latents, norm_gain, norm_bias, read_in, read_out, self_in, self_out, write_in, write_out, feed_up, feed_down, group_image, cot_patches, cot_latents):
    weights = tuple((item.astype(jnp.float32) for item in (norm_gain, norm_bias, read_in, read_out, self_in, self_out, write_in, write_out, feed_up, feed_down)))

    def row_step(totals, row_data):
        patch_row, latent_row, image_row, cot_patch, cot_latent = row_data

        def forward(patch_in, latent_in, *params):
            return row_forward(patch_in, latent_in, image_row, *params)
        results, pullback = jax.vjp(forward, patch_row.astype(jnp.float32), latent_row.astype(jnp.float32), *weights)
        gradients = pullback((cot_patch.astype(jnp.float32), cot_latent.astype(jnp.float32)))
        totals = tuple((total + part for total, part in zip(totals, gradients[2:])))
        return (totals, (results[0].astype(jnp.bfloat16), results[1].astype(jnp.bfloat16), gradients[0].astype(jnp.bfloat16), gradients[1].astype(jnp.bfloat16)))
    zeros = tuple((jnp.zeros_like(item) for item in weights))
    totals, stacked = lax.scan(row_step, zeros, (patches, latents, group_image, cot_patches, cot_latents))
    return (stacked[0], stacked[1], stacked[2], stacked[3], totals[0], totals[1], totals[2], totals[3], totals[4], totals[5], totals[6], totals[7], totals[8], totals[9])
```

```python
import functools

import jax
import jax.numpy as jnp
from jax import lax
from jax.experimental import pallas as pl
from jax.experimental.pallas import tpu as pltpu
from jax.sharding import PartitionSpec as P

D = 768
HEADS = 12
HEAD = 64
LAT = 8
FACTOR = HEAD ** (-0.5)
HL = HEADS * LAT
BF = jnp.bfloat16
F32 = jnp.float32
VMEM_LIMIT = 60 * 1024 * 1024


def narrow(tensor):
    return tensor.astype(BF)


def mm(left, right):
    return lax.dot_general(left, right, (((1,), (0,)), ((), ())), preferred_element_type=F32)


def mm_tn(left, right):
    return lax.dot_general(left, right, (((0,), (0,)), ((), ())), preferred_element_type=F32)


def mm_nt(left, right):
    return lax.dot_general(left, right, (((1,), (1,)), ((), ())), preferred_element_type=F32)


def norm_parts(tensor):
    center = tensor - jnp.mean(tensor, axis=-1, keepdims=True)
    spread = jnp.mean(center * center, axis=-1, keepdims=True)
    inverse = lax.rsqrt(spread + 1e-06)
    return center * inverse, inverse


def norm_forward(tensor, gain, shift):
    unit, _ = norm_parts(tensor)
    return unit * gain + shift


def norm_back(unit, inverse, gain, upstream):
    scaled = upstream * gain
    return inverse * (
        scaled
        - jnp.mean(scaled, axis=-1, keepdims=True)
        - unit * jnp.mean(scaled * unit, axis=-1, keepdims=True)
    )


def fold_rows(tensor):
    rows, cols = tensor.shape
    return jnp.sum(tensor.reshape(rows // 8, 8, cols), axis=0)


def head_mask():
    head = lax.broadcasted_iota(jnp.int32, (HEADS, 1, D), 0)
    feature = lax.broadcasted_iota(jnp.int32, (HEADS, 1, D), 2)
    return (feature >= head * HEAD) & (feature < head * HEAD + HEAD)


def expand(rows):
    count = rows.shape[0]
    return narrow(jnp.where(head_mask(), rows[None], 0.0).reshape(HEADS * count, D))


def collapse(rows):
    count = rows.shape[0] // HEADS
    return jnp.sum(jnp.where(head_mask(), rows.reshape(HEADS, count, D), 0.0), axis=0)


def whole(shape):
    return pl.BlockSpec(shape, lambda *_: (0,) * len(shape), pipeline_mode=pl.Buffered(1))


def rows_of(shape):
    return pl.BlockSpec(shape, lambda g: (g,) + (0,) * (len(shape) - 1))


def one_of(index):
    return pl.BlockSpec(
        (None, D, D), lambda *_: (index, 0, 0), pipeline_mode=pl.Buffered(1)
    )


def shaped(shape, dtype):
    return jax.ShapeDtypeStruct(shape, dtype)


def call(body, grid, in_specs, out_specs, out_shape, flops, moved, scratch=()):
    return pl.pallas_call(
        body,
        grid=grid,
        in_specs=in_specs,
        out_specs=out_specs,
        out_shape=out_shape,
        scratch_shapes=scratch,
        compiler_params=pltpu.CompilerParams(
            vmem_limit_bytes=VMEM_LIMIT, dimension_semantics=("arbitrary",) * len(grid)
        ),
        cost_estimate=pl.CostEstimate(
            flops=int(flops), bytes_accessed=int(moved), transcendentals=0
        ),
    )


def read_forward_kernel(
    x_ref, z_ref, norm_ref, in_ref, out_w_ref,
    a1_ref, q1_ref, b1_ref, k1_ref, v1_ref, p1_ref, o1_ref, z1_ref, a2_ref,
    mix_ref,
):
    step = pl.program_id(0)
    last = pl.num_programs(0) - 1

    @pl.when(step == 0)
    def _():
        a1 = narrow(norm_forward(z_ref[...].astype(F32), norm_ref[0:1], norm_ref[5:6]))
        a1_ref[...] = a1
        q1_ref[...] = narrow(mm(a1, in_ref[0])).astype(F32)

    b1 = narrow(norm_forward(x_ref[...].astype(F32), norm_ref[1:2], norm_ref[6:7]))
    b1_ref[...] = b1
    k1 = narrow(mm(b1, in_ref[1]))
    v1 = narrow(mm(b1, in_ref[2]))
    k1_ref[...] = k1
    v1_ref[...] = v1
    own = pl.ds(pl.multiple_of(step * LAT, LAT), LAT)
    scores = mm_nt(expand(q1_ref[own, :]), k1) * FACTOR
    powers = jnp.exp(scores - jnp.max(scores, axis=-1, keepdims=True))
    shares = powers / jnp.sum(powers, axis=-1, keepdims=True)
    p1_ref[...] = shares
    mix_ref[own, :] = collapse(mm(narrow(shares), v1))

    @pl.when(step == last)
    def _():
        o1 = narrow(mix_ref[...])
        o1_ref[...] = o1
        z1 = z_ref[...].astype(F32) + mm(o1, out_w_ref[...])
        z1_ref[...] = z1
        a2_ref[...] = narrow(norm_forward(z1, norm_ref[2:3], norm_ref[7:8]))


def self_forward_kernel(
    all_ref, a2_ref, z1_ref, key_own_ref, query_own_ref, norm_ref, in_ref, out_w_ref, wk_ref, wv_ref,
    k2_ref, v2_ref, p2_ref, l2_ref, o2_ref, z2_ref, out_ref, b3_ref, k3_ref, v3_ref,
):
    k2 = narrow(mm(all_ref[...], in_ref[1]))
    v2 = narrow(mm(all_ref[...], in_ref[2]))
    k2_ref[...] = k2
    v2_ref[...] = v2
    q2 = narrow(mm(a2_ref[...], in_ref[0])).astype(F32)
    scores = mm_nt(k2, expand(q2)) * FACTOR
    allowed = key_own_ref[...] == query_own_ref[...]
    scores = jnp.where(allowed, scores, -1e30)
    highest = jnp.max(scores, axis=0, keepdims=True)
    powers = jnp.exp(scores - highest)
    totals = jnp.sum(powers, axis=0, keepdims=True)
    shares = powers / totals
    p2_ref[...] = shares
    l2_ref[...] = highest + jnp.log(totals)
    o2 = narrow(collapse(mm_tn(narrow(shares), v2)))
    o2_ref[...] = o2
    z2 = z1_ref[...] + mm(o2, out_w_ref[...])
    z2_ref[...] = z2
    out_ref[...] = narrow(z2)
    b3 = narrow(norm_forward(z2, norm_ref[3:4], norm_ref[8:9]))
    b3_ref[...] = b3
    k3_ref[...] = narrow(mm(b3, wk_ref[...])).astype(F32)
    v3_ref[...] = narrow(mm(b3, wv_ref[...])).astype(F32)


ROOT_HALF = 0.7071067811865476
DENSITY = 0.3989422804014327


def patch_kernel(
    chunk, x_ref, q3_ref, cot_ref, k3_ref, v3_ref, norm_ref, wo_ref, up_ref, down_ref,
    out_ref, h_ref, g_ref, du_ref, o3_ref, e3_ref, dq3_ref, dx1_ref, dk3_ref, dv3_ref,
    gain_ref, shift_ref,
):
    step = pl.program_id(0)
    own = pl.ds(pl.multiple_of(step * LAT, LAT), LAT)
    kx = expand(k3_ref[own, :])
    vx = expand(v3_ref[own, :])
    q3 = q3_ref[...]
    tokens = q3.shape[0]
    scores = (mm_nt(kx, q3) * FACTOR).reshape(HEADS, LAT, tokens)
    powers = jnp.exp(scores - jnp.max(scores, axis=1, keepdims=True))
    shares = powers / jnp.sum(powers, axis=1, keepdims=True)
    shares_low = narrow(shares.reshape(HL, tokens))
    o3 = narrow(mm_tn(shares_low, vx))
    o3_ref[...] = o3
    x1 = x_ref[...].astype(F32) + mm(o3, wo_ref[...])
    unit, inverse = norm_parts(x1)
    gain = norm_ref[4:5]
    h = narrow(unit * gain + norm_ref[9:10])
    h_ref[...] = h
    e4 = cot_ref[...]
    x2 = x1
    dh = jnp.zeros((tokens, D), F32)
    hidden = up_ref.shape[1]
    for start in range(0, hidden, chunk):
        part = slice(start, start + chunk)
        u = mm(h, up_ref[:, part])
        cdf = 0.5 + 0.5 * lax.erf(u * ROOT_HALF)
        g = narrow(u * cdf)
        g_ref[:, part] = g
        x2 = x2 + mm(g, down_ref[part, :])
        slope = cdf + u * (jnp.exp(-0.5 * u * u) * DENSITY)
        du = narrow(mm_nt(e4, down_ref[part, :]) * slope)
        du_ref[:, part] = du
        dh = dh + mm_nt(du, up_ref[:, part])
    out_ref[...] = narrow(x2)

    @pl.when(step == 0)
    def _():
        gain_ref[...] = jnp.zeros_like(gain_ref)
        shift_ref[...] = jnp.zeros_like(shift_ref)

    gain_ref[...] += fold_rows(dh * unit)
    shift_ref[...] += fold_rows(dh)
    dx1 = e4.astype(F32) + norm_back(unit, inverse, gain, dh)
    dx1_ref[...] = dx1
    e3 = narrow(dx1)
    e3_ref[...] = e3
    do3 = narrow(mm_nt(e3, wo_ref[...]))
    dshares = mm_nt(vx, do3).reshape(HEADS, LAT, tokens)
    inner = jnp.sum(shares * dshares, axis=1, keepdims=True)
    dscores = narrow((shares * (dshares - inner)).reshape(HL, tokens))
    dq3_ref[...] = narrow(mm_tn(dscores, kx) * FACTOR)
    dv3_ref[...] = collapse(mm(shares_low, do3))
    dk3_ref[...] = collapse(mm(dscores, q3)) * FACTOR


def latent_back_kernel(
    dk3_ref, dv3_ref, z2_ref, cot_ref, k2_ref, v2_ref, p2_ref, norm_ref, wk_ref, wv_ref, out_w_ref,
    dk3_low_ref, dv3_low_ref, dz2_ref, e2_ref, do2_ref, inner_ref, dq2_ref, gain_ref, shift_ref,
):
    dk3 = narrow(dk3_ref[...])
    dv3 = narrow(dv3_ref[...])
    dk3_low_ref[...] = dk3
    dv3_low_ref[...] = dv3
    upstream = mm_nt(dk3, wk_ref[...]) + mm_nt(dv3, wv_ref[...])
    unit, inverse = norm_parts(z2_ref[...])
    gain_ref[...] = fold_rows(upstream * unit)
    shift_ref[...] = fold_rows(upstream)
    dz2 = cot_ref[...].astype(F32) + norm_back(unit, inverse, norm_ref[3:4], upstream)
    dz2_ref[...] = dz2
    e2 = narrow(dz2)
    e2_ref[...] = e2
    do2 = narrow(mm_nt(e2, out_w_ref[...]))
    do2_ref[...] = do2
    shares = p2_ref[...]
    dshares = mm_nt(v2_ref[...], expand(do2.astype(F32)))
    inner = jnp.sum(shares * dshares, axis=0, keepdims=True)
    inner_ref[...] = inner
    dscores = narrow(shares * (dshares - inner))
    dq2_ref[...] = narrow(collapse(mm_tn(dscores, k2_ref[...])) * FACTOR)


def self_back_kernel(
    q_all_ref, do_all_ref, l_ref, inner_ref, key_own_ref, query_own_ref, k2_ref, v2_ref,
    dq2_ref, z1_ref, dz2_ref, norm_ref, in_ref, out_w_ref,
    dk2_ref, dv2_ref, dz1_ref, e1_ref, do1_ref, gain_ref, shift_ref,
):
    count = k2_ref.shape[0]
    total = q_all_ref.shape[0]
    q_all = q_all_ref[...]
    do_all = do_all_ref[...]
    scores = mm_nt(expand(k2_ref[...].astype(F32)), q_all) * FACTOR
    allowed = key_own_ref[...] == query_own_ref[...]
    log_total = jnp.broadcast_to(l_ref[...], (HEADS, count, total)).reshape(HEADS * count, total)
    shares = jnp.where(allowed, jnp.exp(jnp.where(allowed, scores - log_total, 0.0)), 0.0)
    dv2 = narrow(collapse(mm(narrow(shares), do_all)))
    dshares = mm_nt(expand(v2_ref[...].astype(F32)), do_all)
    inner = jnp.broadcast_to(inner_ref[...], (HEADS, count, total)).reshape(HEADS * count, total)
    dscores = narrow(shares * (dshares - inner))
    dk2 = narrow(collapse(mm(dscores, q_all)) * FACTOR)
    dk2_ref[...] = dk2
    dv2_ref[...] = dv2
    upstream = mm_nt(dq2_ref[...], in_ref[0]) + mm_nt(dk2, in_ref[1]) + mm_nt(dv2, in_ref[2])
    unit, inverse = norm_parts(z1_ref[...])
    gain_ref[...] = fold_rows(upstream * unit)
    shift_ref[...] = fold_rows(upstream)
    dz1 = dz2_ref[...] + norm_back(unit, inverse, norm_ref[2:3], upstream)
    dz1_ref[...] = dz1
    e1 = narrow(dz1)
    e1_ref[...] = e1
    do1_ref[...] = narrow(mm_nt(e1, out_w_ref[...])).astype(F32)


def read_back_kernel(
    do1_ref, q1_ref, p1_ref, k1_ref, v1_ref,
    dq1_ref, dk1_ref, dv1_ref,
):
    step = pl.program_id(0)
    own = pl.ds(pl.multiple_of(step * LAT, LAT), LAT)
    qx = expand(q1_ref[own, :])
    dox = expand(do1_ref[own, :])
    shares = p1_ref[...]
    dshares = mm_nt(dox, v1_ref[...])
    inner = jnp.sum(shares * dshares, axis=-1, keepdims=True)
    dscores = narrow(shares * (dshares - inner))
    dv1_ref[...] = narrow(mm_tn(narrow(shares), dox))
    dk1_ref[...] = narrow(mm_tn(dscores, qx) * FACTOR)
    dq1_ref[...] = collapse(mm(dscores, k1_ref[...])) * FACTOR


def input_back_kernel(
    x_ref, dx1_ref, dq3_ref, dk1_ref, dv1_ref, z_ref, dz1_ref, dq1_ref, norm_ref, in_ref, wq_ref,
    dx_ref, dz_ref, gain_ref, shift_ref, gain_zero_ref, shift_zero_ref,
):
    step = pl.program_id(0)

    @pl.when(step == 0)
    def _():
        gain_ref[...] = jnp.zeros_like(gain_ref)
        shift_ref[...] = jnp.zeros_like(shift_ref)
        upstream = mm_nt(dq1_ref[...], in_ref[0])
        unit, inverse = norm_parts(z_ref[...].astype(F32))
        gain_zero_ref[...] = fold_rows(upstream * unit)
        shift_zero_ref[...] = fold_rows(upstream)
        dz_ref[...] = narrow(dz1_ref[...] + norm_back(unit, inverse, norm_ref[0:1], upstream))

    upstream = (
        mm_nt(dq3_ref[...], wq_ref[...])
        + mm_nt(dk1_ref[...], in_ref[1])
        + mm_nt(dv1_ref[...], in_ref[2])
    )
    unit, inverse = norm_parts(x_ref[...].astype(F32))
    gain_ref[...] += fold_rows(upstream * unit)
    shift_ref[...] += fold_rows(upstream)
    dx_ref[...] = narrow(dx1_ref[...] + norm_back(unit, inverse, norm_ref[1:2], upstream))


def bits_of(count):
    bits = count.bit_length() - 1
    if 1 << bits != count:
        raise ValueError("axis size")
    return bits


def swap(tensor, axis, bit, count):
    return lax.ppermute(tensor, axis, [(i, i ^ (1 << bit)) for i in range(count)])


def own_bit(bit, axis="blk"):
    return (lax.axis_index(axis) >> bit) & 1


def doubled(tensor, bit, place, count):
    other = swap(tensor, "blk", bit, count)
    mine_first = own_bit(bit) == 0
    return jnp.stack(
        [jnp.where(mine_first, tensor, other), jnp.where(mine_first, other, tensor)], place
    )


def gather_rows(tensor, count):
    bits = bits_of(count)
    rows, cols = tensor.shape
    for place, bit in enumerate(range(bits - 1, 1, -1)):
        tensor = doubled(tensor, bit, place, count)
    lead = max(bits - 2, 0)
    if bits < 2:
        for bit in range(bits - 1, -1, -1):
            tensor = doubled(tensor, bit, 0, count)
        return tensor.reshape(count, rows, cols)
    left, right = tensor[..., : cols // 2], tensor[..., cols // 2 :]
    left = doubled(left, 1, lead, count)
    right = doubled(right, 0, lead, count)
    left = doubled(left, 0, lead + 1, count)
    right = doubled(right, 1, lead, count)
    return jnp.concatenate([left, right], -1).reshape(count, rows, cols)


def scatter_orders(bits):
    high = list(range(2, bits))
    if bits < 3:
        base = list(range(bits))
        return [base, base[::-1], base]
    return [[0, 1] + high, [1] + high[:1] + [0] + high[1:], high[:1] + [0, 1] + high[1:]]


def scatter_sum(tensor, order, count):
    bits = bits_of(count)
    rows, cols = tensor.shape[1:]
    tensor = tensor.reshape((2,) * bits + (rows, cols))
    left = list(range(bits - 1, -1, -1))
    for bit in order:
        place = left.index(bit)
        left.pop(place)
        mine = own_bit(bit)
        send = lax.dynamic_index_in_dim(tensor, 1 - mine, place, keepdims=False)
        keep = lax.dynamic_index_in_dim(tensor, mine, place, keepdims=False)
        got = swap(send, "blk", bit, count)
        tensor = narrow(keep.astype(F32) + got.astype(F32))
    return tensor


def half_columns(tensor, which):
    width = tensor.shape[1] // 2
    return lax.dynamic_slice_in_dim(tensor, which * width, width, 1)


def weight_halves(left, right, core, count):
    def half(which):
        grad = narrow(mm_tn(left, half_columns(right, which)))
        return grad.reshape(count, -1, grad.shape[1])

    return half(1 - core), half(core)


def make_body(n_blk, n_rep):
    rep_bits = bits_of(n_rep)
    orders = scatter_orders(bits_of(n_blk))

    def merge_core(pairs):
        other = jnp.concatenate([pair[0] for pair in pairs], 1) if len(pairs) > 1 else pairs[0][0]
        mine = jnp.concatenate([pair[1] for pair in pairs], 1) if len(pairs) > 1 else pairs[0][1]
        got = swap(other, "rep", 0, n_rep)
        return narrow(mine.astype(F32) + got.astype(F32))

    def finish(tensor, core):
        for bit in range(1, rep_bits):
            tensor = narrow(tensor.astype(F32) + swap(tensor, "rep", bit, n_rep).astype(F32))
        return tensor

    def body(
        patches, latents, norm_gain, norm_bias, read_in, read_out, self_in, self_out,
        write_in, write_out, feed_up, feed_down, group_image, cot_patches, cot_latents,
    ):
        x, z, cot, cot_z = patches[0], latents[0], cot_patches[0], cot_latents[0]
        tokens, lat = x.shape[0], z.shape[0]
        groups = lat // LAT
        size = tokens // groups
        total = lat * n_blk
        hidden = feed_up.shape[1]
        core = lax.axis_index("rep") & 1
        norms = jnp.concatenate(
            [norm_gain, norm_bias, jnp.zeros((6, D), BF)], 0
        ).astype(F32)
        norm_spec = whole((16, D))
        square = whole((D, D))
        three = whole((3, D, D))
        lat_spec = whole((lat, D))
        patch_spec = rows_of((size, D))
        grid = (groups,)
        unit_flops = 2 * tokens * D * D

        a1, q1, b1, k1, v1, p1, o1, z1, a2 = call(
            read_forward_kernel, grid,
            [patch_spec, lat_spec, norm_spec, three, square],
            [lat_spec, lat_spec, patch_spec, patch_spec, patch_spec,
             pl.BlockSpec((None, HL, size), lambda g: (g, 0, 0)), lat_spec, lat_spec, lat_spec],
            [shaped((lat, D), BF), shaped((lat, D), F32)] + [shaped((tokens, D), BF)] * 3
            + [shaped((groups, HL, size), F32), shaped((lat, D), BF), shaped((lat, D), F32), shaped((lat, D), BF)],
            2 * unit_flops, 12 * tokens * D,
            [pltpu.VMEM((lat, D), F32)],
        )(x, z, norms, read_in, read_out)

        a2_all = gather_rows(a2, n_blk).reshape(total, D)
        q3 = narrow(mm(b1, write_in[0]))

        owners = jnp.repeat(group_image[0], LAT)
        own = lax.dynamic_slice_in_dim(owners, lax.axis_index("blk") * lat, lat, 0)
        own_heads = jnp.tile(own, HEADS)
        hl2 = HEADS * lat
        k2, v2, p2, l2, o2, z2, out_latents, b3, k3, v3 = call(
            self_forward_kernel, (1,),
            [whole((total, D)), lat_spec, lat_spec, whole((total, 1)), whole((1, hl2)), norm_spec, three, square,
             one_of(1), one_of(2)],
            [whole((total, D)), whole((total, D)), whole((total, hl2)), whole((1, hl2))] + [lat_spec] * 6,
            [shaped((total, D), BF), shaped((total, D), BF), shaped((total, hl2), F32), shaped((1, hl2), F32),
             shaped((lat, D), BF), shaped((lat, D), F32), shaped((lat, D), BF), shaped((lat, D), BF),
             shaped((lat, D), F32), shaped((lat, D), F32)],
            unit_flops * 2, 10 * D * D * 2,
        )(a2_all, a2, z1, owners[:, None], own_heads[None, :], norms, self_in, self_out, write_in, write_in)

        out_patches, h, g, du, o3, e3, dq3, dx1, dk3, dv3, gain4, shift4 = call(
            functools.partial(patch_kernel, D), grid,
            [patch_spec, patch_spec, patch_spec, lat_spec, lat_spec, norm_spec, square,
             whole((D, hidden)), whole((hidden, D))],
            [patch_spec, patch_spec, rows_of((size, hidden)), rows_of((size, hidden)), patch_spec, patch_spec,
             patch_spec, patch_spec, rows_of((LAT, D)), rows_of((LAT, D)), whole((8, D)), whole((8, D))],
            [shaped((tokens, D), BF), shaped((tokens, D), BF), shaped((tokens, hidden), BF), shaped((tokens, hidden), BF),
             shaped((tokens, D), BF), shaped((tokens, D), BF), shaped((tokens, D), BF), shaped((tokens, D), F32),
             shaped((lat, D), F32), shaped((lat, D), F32), shaped((8, D), F32), shaped((8, D), F32)],
            unit_flops * 20, 40 * tokens * D,
        )(x, q3, cot, k3, v3, norms, write_out, feed_up, feed_down)

        dk3, dv3, dz2, e2, do2, inner2, dq2, gain3, shift3 = call(
            latent_back_kernel, (1,),
            [lat_spec] * 4 + [whole((total, D))] * 2 + [whole((total, hl2)), norm_spec, one_of(1), one_of(2), square],
            [lat_spec] * 5 + [whole((1, hl2)), lat_spec, whole((8, D)), whole((8, D))],
            [shaped((lat, D), BF), shaped((lat, D), BF), shaped((lat, D), F32), shaped((lat, D), BF), shaped((lat, D), BF),
             shaped((1, hl2), F32), shaped((lat, D), BF), shaped((8, D), F32), shaped((8, D), F32)],
            unit_flops, 10 * D * D,
        )(dk3, dv3, z2, cot_z, k2, v2, p2, norms, write_in, write_in, self_out)

        stats = jnp.concatenate([l2, inner2], 0)
        stats_top = narrow(stats)
        rest = stats - stats_top.astype(F32)
        stats_mid = narrow(rest)
        stats_low = narrow(rest - stats_mid.astype(F32))
        extra = jnp.concatenate([stats_top, stats_mid, stats_low], 0).reshape(-1, D)
        extra_rows = extra.shape[0]
        pad = -(lat + extra_rows) % 16
        payload = jnp.concatenate([do2, extra, jnp.zeros((pad, D), BF)], 0)
        spread = gather_rows(payload, n_blk)
        do_all = spread[:, :lat].reshape(total, D)
        stats_all = spread[:, lat : lat + extra_rows].reshape(n_blk, 3, 2, HEADS, lat).astype(F32)
        stats_all = jnp.sum(stats_all, axis=1).transpose(1, 2, 0, 3).reshape(2, HEADS, 1, total)
        q2_all = narrow(mm(a2_all, self_in[0]))

        up_part = merge_core([weight_halves(h, du, core, n_blk)])
        up_sum = scatter_sum(up_part, orders[0], n_blk)
        down_part = merge_core([weight_halves(g, cot, core, n_blk)])
        down_sum = scatter_sum(down_part, orders[1], n_blk)
        mid_part = merge_core(
            [weight_halves(o3, e3, core, n_blk), weight_halves(b1, dq3, core, n_blk),
             weight_halves(b3, dk3, core, n_blk), weight_halves(b3, dv3, core, n_blk),
             weight_halves(o2, e2, core, n_blk)]
        )
        mid_sum = scatter_sum(mid_part, orders[2], n_blk)

        place = lax.axis_index("blk") * lat
        k2_own = lax.dynamic_slice_in_dim(k2, place, lat, 0)
        v2_own = lax.dynamic_slice_in_dim(v2, place, lat, 0)
        dk2, dv2, dz1, e1, do1, gain2, shift2 = call(
            self_back_kernel, (1,),
            [whole((total, D))] * 2 + [whole((HEADS, 1, total))] * 2 + [whole((hl2, 1)), whole((1, total))]
            + [lat_spec] * 5 + [norm_spec, three, square],
            [lat_spec] * 5 + [whole((8, D)), whole((8, D))],
            [shaped((lat, D), BF), shaped((lat, D), BF), shaped((lat, D), F32), shaped((lat, D), BF), shaped((lat, D), F32),
             shaped((8, D), F32), shaped((8, D), F32)],
            unit_flops, 10 * D * D,
        )(q2_all, do_all, stats_all[0], stats_all[1], own_heads[:, None], owners[None, :], k2_own, v2_own,
          dq2, z1, dz2, norms, self_in, read_out)

        dq1, dk1, dv1 = call(
            read_back_kernel, grid,
            [lat_spec, lat_spec, pl.BlockSpec((None, HL, size), lambda g: (g, 0, 0)), patch_spec, patch_spec],
            [rows_of((LAT, D)), patch_spec, patch_spec],
            [shaped((lat, D), F32), shaped((tokens, D), BF), shaped((tokens, D), BF)],
            unit_flops / 2, 10 * tokens * D,
        )(do1, q1, p1, k1, v1)
        dq1 = narrow(dq1)

        dx, dz, gain1, shift1, gain0, shift0 = call(
            input_back_kernel, grid,
            [patch_spec] * 5 + [lat_spec] * 3 + [norm_spec, three, one_of(0)],
            [patch_spec, lat_spec] + [whole((8, D))] * 4,
            [shaped((tokens, D), BF), shaped((lat, D), BF)] + [shaped((8, D), F32)] * 4,
            unit_flops * 3, 14 * tokens * D,
        )(x, dx1, dq3, dk1, dv1, z, dz1, dq1, norms, read_in, write_in)

        late_self = scatter_sum(
            merge_core([weight_halves(a2, dq2, core, n_blk), weight_halves(a2, dk2, core, n_blk),
                        weight_halves(a2, dv2, core, n_blk)]),
            orders[0], n_blk)
        late_read = scatter_sum(
            merge_core([weight_halves(b1, dk1, core, n_blk), weight_halves(b1, dv1, core, n_blk)]),
            orders[1], n_blk)
        gains = jnp.sum(jnp.stack([gain0, gain1, gain2, gain3, gain4]), 1)
        shifts = jnp.sum(jnp.stack([shift0, shift1, shift2, shift3, shift4]), 1)
        norm_rows = D // n_blk

        def norm_block(which):
            block = narrow(jnp.where(which == 0, gains, shifts)).reshape(5, n_blk, norm_rows)
            block = block.transpose(1, 0, 2).reshape(n_blk, 5 * norm_rows)
            block = jnp.pad(block, ((0, 0), (0, 16 * (D // 2) - 5 * norm_rows)))
            return block.reshape(n_blk, 16, D // 2)

        late_mix = scatter_sum(
            merge_core([weight_halves(a1, dq1, core, n_blk), weight_halves(o1, e1, core, n_blk),
                        (norm_block(1 - core), norm_block(core))]),
            orders[2], n_blk)

        rows = D // n_blk
        up_rows = up_sum.reshape(rows, 2, -1, D // 2) if False else up_sum
        flat = jnp.concatenate([mid_sum, late_self, late_read, late_mix, down_sum], 0)
        up_flat = jnp.concatenate(
            [up_rows[:, i * (D // 2) : (i + 1) * (D // 2)] for i in range(hidden // D)], 0
        )
        flat = finish(jnp.concatenate([flat, up_flat], 0), core)
        partner = swap(flat, "rep", 0, n_rep)
        low = jnp.where(core == 0, flat, partner).astype(F32)
        high = jnp.where(core == 0, partner, flat).astype(F32)
        pieces = []
        start = 0
        for index in range(12):
            part = slice(start, start + rows)
            pieces.append(jnp.concatenate([low[part], high[part]], 1))
            start += rows
            if index == 11:
                norm_low, norm_high = low[start : start + 16], high[start : start + 16]
                start += 16
        wo_g, wq_g, wk_g, wv_g, so_g, sq_g, sk_g, sv_g, rk_g, rv_g, rq_g, ro_g = pieces
        down_g = jnp.concatenate(
            [low[start : start + hidden // n_blk], high[start : start + hidden // n_blk]], 1
        )
        start += hidden // n_blk
        up_low, up_high = [], []
        for _ in range(hidden // D):
            up_low.append(low[start : start + rows])
            up_high.append(high[start : start + rows])
            start += rows
        up_g = jnp.concatenate(up_low + up_high, 1)
        gain_g = norm_low.reshape(-1)[: 5 * norm_rows].reshape(5, norm_rows)
        shift_g = norm_high.reshape(-1)[: 5 * norm_rows].reshape(5, norm_rows)
        return (
            out_patches[None], out_latents[None], dx[None], dz[None], gain_g, shift_g,
            jnp.stack([rq_g, rk_g, rv_g]), ro_g,
            jnp.stack([sq_g, sk_g, sv_g]), so_g,
            jnp.stack([wq_g, wk_g, wv_g]), wo_g,
            up_g, down_g,
        )

    return body


def solution(mesh):
    return jax.shard_map(
        make_body(mesh.shape["blk"], mesh.shape["rep"]),
        mesh=mesh,
        in_specs=(
            P("rep", "blk", None), P("rep", "blk", None), P(), P(), P(), P(), P(), P(), P(), P(), P(), P(),
            P("rep", None), P("rep", "blk", None), P("rep", "blk", None),
        ),
        out_specs=(
            P("rep", "blk", None), P("rep", "blk", None), P("rep", "blk", None), P("rep", "blk", None),
            P(None, "blk"), P(None, "blk"), P(None, "blk", None), P("blk", None), P(None, "blk", None),
            P("blk", None), P(None, "blk", None), P("blk", None), P("blk", None), P("blk", None),
        ),
        check_vma=False,
    )
```

```python
import functools

import jax
import jax.numpy as jnp
from jax import lax
from jax.experimental import pallas as pl
from jax.experimental.pallas import tpu as pltpu
from jax.sharding import PartitionSpec as P

D = 768
HEADS = 12
HEAD = 64
LAT = 8
FACTOR = HEAD ** (-0.5)
HL = HEADS * LAT
BF = jnp.bfloat16
F32 = jnp.float32


def narrow(tensor):
    return tensor.astype(BF)


def mm(left, right):
    return lax.dot_general(left, right, (((1,), (0,)), ((), ())), preferred_element_type=F32)


def mm_tn(left, right):
    return lax.dot_general(left, right, (((0,), (0,)), ((), ())), preferred_element_type=F32)


def mm_nt(left, right):
    return lax.dot_general(left, right, (((1,), (1,)), ((), ())), preferred_element_type=F32)


def norm_parts(tensor):
    center = tensor - jnp.mean(tensor, axis=-1, keepdims=True)
    spread = jnp.mean(center * center, axis=-1, keepdims=True)
    inverse = lax.rsqrt(spread + 1e-06)
    return center * inverse, inverse


def norm_forward(tensor, gain, shift):
    unit, _ = norm_parts(tensor)
    return unit * gain + shift


def norm_back(unit, inverse, gain, upstream):
    scaled = upstream * gain
    return inverse * (
        scaled
        - jnp.mean(scaled, axis=-1, keepdims=True)
        - unit * jnp.mean(scaled * unit, axis=-1, keepdims=True)
    )


def fold_rows(tensor):
    rows, cols = tensor.shape
    return jnp.sum(tensor.reshape(rows // 8, 8, cols), axis=0)


def head_mask():
    head = lax.broadcasted_iota(jnp.int32, (HEADS, 1, D), 0)
    feature = lax.broadcasted_iota(jnp.int32, (HEADS, 1, D), 2)
    return (feature >= head * HEAD) & (feature < head * HEAD + HEAD)


def expand(rows):
    count = rows.shape[0]
    return narrow(jnp.where(head_mask(), rows[None], 0.0).reshape(HEADS * count, D))


def collapse(rows):
    count = rows.shape[0] // HEADS
    return jnp.sum(jnp.where(head_mask(), rows.reshape(HEADS, count, D), 0.0), axis=0)


def whole(shape):
    return pl.BlockSpec(shape, lambda *_: (0,) * len(shape), pipeline_mode=pl.Buffered(1))


def rows_of(shape):
    return pl.BlockSpec(shape, lambda g: (g,) + (0,) * (len(shape) - 1))


def one_of(index):
    return pl.BlockSpec(
        (None, D, D), lambda *_: (index, 0, 0), pipeline_mode=pl.Buffered(1)
    )


def shaped(shape, dtype):
    return jax.ShapeDtypeStruct(shape, dtype)


def in_hbm(tensor):
    return pltpu.with_memory_space_constraint(tensor, pltpu.HBM)


def image_marks(image_ref, places_ref, shape, axis, rows):
    index = lax.broadcasted_iota(jnp.int32, shape, axis)
    marks = jnp.zeros(shape, jnp.int32)
    for group in range(shape[axis] // rows):
        inside = (index >= group * rows) & (index < (group + 1) * rows)
        marks = jnp.where(inside, image_ref[0, places_ref[group]], marks)
    return marks


def gathered(refs):
    pieces = [ref[...] for ref in refs]
    return jnp.concatenate([piece.reshape(-1, piece.shape[-1]) for piece in pieces], 0)


def call(body, grid, in_specs, out_specs, out_shape, flops, moved, scratch=(), vmem=20):
    return pl.pallas_call(
        body,
        grid=grid,
        in_specs=in_specs,
        out_specs=out_specs,
        out_shape=out_shape,
        scratch_shapes=scratch,
        compiler_params=pltpu.CompilerParams(
            vmem_limit_bytes=vmem << 20, dimension_semantics=("arbitrary",) * len(grid)
        ),
        cost_estimate=pl.CostEstimate(
            flops=int(flops), bytes_accessed=int(moved), transcendentals=0
        ),
    )


def read_forward_kernel(
    x_ref, z_ref, norm_ref, in_ref, out_w_ref,
    a1_ref, q1_ref, b1_ref, k1_ref, v1_ref, p1_ref, o1_ref, z1_ref, a2_ref,
    mix_ref,
):
    step = pl.program_id(0)
    last = pl.num_programs(0) - 1

    @pl.when(step == 0)
    def _():
        a1 = narrow(norm_forward(z_ref[...].astype(F32), norm_ref[0:1], norm_ref[5:6]))
        a1_ref[...] = a1
        q1_ref[...] = narrow(mm(a1, in_ref[0])).astype(F32)

    b1 = narrow(norm_forward(x_ref[...].astype(F32), norm_ref[1:2], norm_ref[6:7]))
    b1_ref[...] = b1
    k1 = narrow(mm(b1, in_ref[1]))
    v1 = narrow(mm(b1, in_ref[2]))
    k1_ref[...] = k1
    v1_ref[...] = v1
    own = pl.ds(pl.multiple_of(step * LAT, LAT), LAT)
    scores = mm_nt(expand(q1_ref[own, :]), k1) * FACTOR
    powers = jnp.exp(scores - jnp.max(scores, axis=-1, keepdims=True))
    shares = powers / jnp.sum(powers, axis=-1, keepdims=True)
    p1_ref[...] = shares
    mix_ref[own, :] = collapse(mm(narrow(shares), v1))

    @pl.when(step == last)
    def _():
        o1 = narrow(mix_ref[...])
        o1_ref[...] = o1
        z1 = z_ref[...].astype(F32) + mm(o1, out_w_ref[...])
        z1_ref[...] = z1
        a2_ref[...] = narrow(norm_forward(z1, norm_ref[2:3], norm_ref[7:8]))


def self_forward_kernel(
    image_ref, places_ref, own_at_ref, piece0_ref, piece1_ref, piece2_ref, piece3_ref,
    a2_ref, z1_ref, norm_ref, in_ref, out_w_ref, wk_ref, wv_ref,
    all_ref, allowed_ref, k2_ref, v2_ref, p2_ref, l2_ref, o2_ref, z2_ref, out_ref, b3_ref, k3_ref, v3_ref,
):
    everyone = gathered((piece0_ref, piece1_ref, piece2_ref, piece3_ref))
    all_ref[...] = everyone
    k2 = narrow(mm(everyone, in_ref[1]))
    v2 = narrow(mm(everyone, in_ref[2]))
    k2_ref[...] = k2
    v2_ref[...] = v2
    q2 = narrow(mm(a2_ref[...], in_ref[0])).astype(F32)
    scores = mm_nt(expand(q2), k2) * FACTOR
    total, count = everyone.shape[0], q2.shape[0]
    owners = image_marks(image_ref, places_ref, (1, total), 1, LAT)
    own = jnp.concatenate([image_marks(image_ref, own_at_ref, (count, 1), 0, LAT)] * HEADS, 0)
    allowed = own == owners
    allowed_ref[...] = jnp.where(allowed, 1.0, 0.0)
    scores = jnp.where(allowed, scores, -1e30)
    highest = jnp.max(scores, axis=-1, keepdims=True)
    powers = jnp.exp(scores - highest)
    totals = jnp.sum(powers, axis=-1, keepdims=True)
    shares = powers / totals
    p2_ref[...] = shares
    l2_ref[...] = highest + jnp.log(totals)
    o2 = narrow(collapse(mm(narrow(shares), v2)))
    o2_ref[...] = o2
    z2 = z1_ref[...] + mm(o2, out_w_ref[...])
    z2_ref[...] = z2
    out_ref[...] = narrow(z2)
    b3 = narrow(norm_forward(z2, norm_ref[3:4], norm_ref[8:9]))
    b3_ref[...] = b3
    k3_ref[...] = narrow(mm(b3, wk_ref[...])).astype(F32)
    v3_ref[...] = narrow(mm(b3, wv_ref[...])).astype(F32)


ROOT_HALF = 0.7071067811865476
DENSITY = 0.3989422804014327


def patch_kernel(
    chunk, x_ref, q3_ref, cot_ref, k3_ref, v3_ref, norm_ref, wo_ref, up_ref, down_ref,
    out_ref, he_ref, gd_ref, o3_ref, e3_ref, dq3_ref, dx1_ref, dk3_ref, dv3_ref,
    gain_ref, shift_ref,
):
    step = pl.program_id(0)
    own = pl.ds(pl.multiple_of(step * LAT, LAT), LAT)
    kx = expand(k3_ref[own, :])
    vx = expand(v3_ref[own, :])
    q3 = q3_ref[...]
    tokens = q3.shape[0]
    scores = (mm_nt(kx, q3) * FACTOR).reshape(HEADS, LAT, tokens)
    powers = jnp.exp(scores - jnp.max(scores, axis=1, keepdims=True))
    shares = powers / jnp.sum(powers, axis=1, keepdims=True)
    shares_low = narrow(shares.reshape(HL, tokens))
    o3 = narrow(mm_tn(shares_low, vx))
    o3_ref[...] = o3
    x1 = x_ref[...].astype(F32) + mm(o3, wo_ref[...])
    unit, inverse = norm_parts(x1)
    gain = norm_ref[4:5]
    h = narrow(unit * gain + norm_ref[9:10])
    e4 = cot_ref[...]
    he_ref[0] = h
    he_ref[1] = e4
    x2 = x1
    dh = jnp.zeros((tokens, D), F32)
    hidden = up_ref.shape[1]
    for start in range(0, hidden, chunk):
        part = slice(start, start + chunk)
        u = mm(h, up_ref[:, part])
        cdf = 0.5 + 0.5 * lax.erf(u * ROOT_HALF)
        g = narrow(u * cdf)
        gd_ref[1, :, part] = g
        x2 = x2 + mm(g, down_ref[part, :])
        slope = cdf + u * (jnp.exp(-0.5 * u * u) * DENSITY)
        du = narrow(mm_nt(e4, down_ref[part, :]) * slope)
        gd_ref[0, :, part] = du
        dh = dh + mm_nt(du, up_ref[:, part])
    out_ref[...] = narrow(x2)

    @pl.when(step == 0)
    def _():
        gain_ref[...] = jnp.zeros_like(gain_ref)
        shift_ref[...] = jnp.zeros_like(shift_ref)

    gain_ref[...] += fold_rows(dh * unit)
    shift_ref[...] += fold_rows(dh)
    dx1 = e4.astype(F32) + norm_back(unit, inverse, gain, dh)
    dx1_ref[...] = dx1
    e3 = narrow(dx1)
    e3_ref[...] = e3
    do3 = narrow(mm_nt(e3, wo_ref[...]))
    dshares = mm_nt(vx, do3).reshape(HEADS, LAT, tokens)
    inner = jnp.sum(shares * dshares, axis=1, keepdims=True)
    dscores = narrow((shares * (dshares - inner)).reshape(HL, tokens))
    dq3_ref[...] = narrow(mm_tn(dscores, kx) * FACTOR)
    dv3_ref[...] = collapse(mm(shares_low, do3))
    dk3_ref[...] = collapse(mm(dscores, q3)) * FACTOR


STAT = 2 * HEADS


def latent_back_kernel(
    dk3_ref, dv3_ref, z2_ref, cot_ref, k2_ref, v2_ref, p2_ref, l2_ref, norm_ref, wk_ref, wv_ref, out_w_ref,
    dk3_low_ref, dv3_low_ref, dz2_ref, e2_ref, send_ref, dq2_ref, gain_ref, shift_ref,
):
    dk3 = narrow(dk3_ref[...])
    dv3 = narrow(dv3_ref[...])
    dk3_low_ref[...] = dk3
    dv3_low_ref[...] = dv3
    upstream = mm_nt(dk3, wk_ref[...]) + mm_nt(dv3, wv_ref[...])
    unit, inverse = norm_parts(z2_ref[...])
    gain_ref[...] = fold_rows(upstream * unit)
    shift_ref[...] = fold_rows(upstream)
    dz2 = cot_ref[...].astype(F32) + norm_back(unit, inverse, norm_ref[3:4], upstream)
    dz2_ref[...] = dz2
    e2 = narrow(dz2)
    e2_ref[...] = e2
    do2 = narrow(mm_nt(e2, out_w_ref[...]))
    send_ref[:, :D] = do2
    shares = p2_ref[...]
    dshares = mm_nt(expand(do2.astype(F32)), v2_ref[...])
    inner = jnp.sum(shares * dshares, axis=-1, keepdims=True)
    count = do2.shape[0]
    lane = lax.broadcasted_iota(jnp.int32, (count, 128), 1)
    stats = jnp.zeros((count, 128), F32)
    for slot, columns in ((0, l2_ref[...]), (HEADS, inner)):
        for head in range(HEADS):
            place = slot + head
            chosen = (lane == place) | (lane == place + STAT) | (lane == place + 2 * STAT)
            stats = jnp.where(chosen, columns[head * count : (head + 1) * count], stats)
    top = narrow(stats)
    rest = stats - top.astype(F32)
    middle = narrow(rest)
    bottom = narrow(rest - middle.astype(F32))
    send_ref[:, D:] = narrow(
        jnp.where(lane < STAT, top.astype(F32), jnp.where(lane < 2 * STAT, middle.astype(F32), bottom.astype(F32)))
    )
    dscores = narrow(shares * (dshares - inner))
    dq2_ref[...] = narrow(collapse(mm(dscores, k2_ref[...])) * FACTOR)


def spread_stat(stats, slot, count):
    shape = (HEADS * count, 128)
    place = lax.broadcasted_iota(jnp.int32, shape, 1)
    column = lax.broadcasted_iota(jnp.int32, shape, 0)
    chosen = jnp.zeros(shape, jnp.bool_)
    for term in range(3):
        head = place - (slot + term * STAT)
        chosen |= (head >= 0) & (head < HEADS) & (column >= head * count) & (column < (head + 1) * count)
    return mm_nt(narrow(jnp.where(chosen, 1.0, 0.0)), stats)


def put_units(core_ref, other_ref, mine_ref, units):
    count = mine_ref.shape[0]
    rows = D // count
    for core in range(2):
        @pl.when(core_ref[0] == core)
        def _():
            for ref, pairs in ((other_ref, units[1 - core]), (mine_ref, units[core])):
                for index, (left, right) in enumerate(pairs):
                    grad = narrow(mm_tn(left[...], right[...]).reshape(count, rows, D))
                    ref[:, index * rows : (index + 1) * rows, :] = grad


def early_kernel(
    core_ref, o3_ref, e3_ref, b1_ref, dq3_ref, b3_ref, dk3_ref, dv3_ref, other_ref, mine_ref
):
    put_units(core_ref, other_ref, mine_ref,
              [[(o3_ref, e3_ref), (b3_ref, dk3_ref)], [(b1_ref, dq3_ref), (b3_ref, dv3_ref)]])


def late_kernel(
    core_ref, b1_ref, dk1_ref, dv1_ref, a1_ref, dq1_ref, o1_ref, e1_ref, a2_ref, dq2_ref, o2_ref, e2_ref,
    dk2_ref, dv2_ref, other_ref, mine_ref,
):
    put_units(core_ref, other_ref, mine_ref,
              [[(b1_ref, dk1_ref), (a1_ref, dq1_ref), (a2_ref, dq2_ref), (o2_ref, e2_ref)],
               [(b1_ref, dv1_ref), (o1_ref, e1_ref), (a2_ref, dk2_ref), (a2_ref, dv2_ref)]])


def stage_kernel(parts, pick_ref, *refs):
    for index in range(parts):
        keep_ref, got_ref = refs[2 * index : 2 * index + 2]
        send_ref, stay_ref = refs[2 * parts + 2 * index : 2 * parts + 2 * index + 2]
        mine = pick_ref[index]
        send_ref[...] = narrow(keep_ref[1 - mine].astype(F32) + got_ref[1 - mine].astype(F32))
        stay_ref[...] = narrow(keep_ref[mine].astype(F32) + got_ref[mine].astype(F32))


def last_stage_kernel(parts, pick_ref, *refs):
    send_ref, stay_ref = refs[2 * parts :]
    mine = pick_ref[0]
    start = 0
    for index in range(parts):
        keep_ref, got_ref = refs[2 * index : 2 * index + 2]
        rows = keep_ref.shape[1]
        span = slice(start, start + rows)
        send_ref[span] = narrow(keep_ref[1 - mine].astype(F32) + got_ref[1 - mine].astype(F32))
        stay_ref[span] = narrow(keep_ref[mine].astype(F32) + got_ref[mine].astype(F32))
        start += rows


def sum_kernel(keep_ref, got_ref, out_ref):
    out_ref[...] = narrow(keep_ref[...].astype(F32) + got_ref[...].astype(F32))


def early_out_kernel(core_ref, mine_ref, partner_ref, up_ref, down_ref, wo_ref, in_ref):
    rows = wo_ref.shape[0]
    feed_rows = down_ref.shape[0]
    for core in range(2):
        @pl.when(core_ref[0] == core)
        def _():
            zero, one = (mine_ref, partner_ref) if core == 0 else (partner_ref, mine_ref)
            for index in range(feed_rows // rows):
                up_ref[:, index * D : (index + 1) * D] = zero[index * rows : (index + 1) * rows].astype(F32)
            down_ref[...] = one[:feed_rows].astype(F32)
            wo_ref[...] = zero[feed_rows : feed_rows + rows].astype(F32)
            in_ref[0] = one[feed_rows : feed_rows + rows].astype(F32)
            in_ref[1] = zero[feed_rows + rows :].astype(F32)
            in_ref[2] = one[feed_rows + rows :].astype(F32)


def late_out_kernel(core_ref, mine_ref, partner_ref, read_in_ref, read_out_ref, self_in_ref, self_out_ref):
    rows = read_out_ref.shape[0]
    for core in range(2):
        @pl.when(core_ref[0] == core)
        def _():
            zero, one = (mine_ref, partner_ref) if core == 0 else (partner_ref, mine_ref)

            def unit(ref, index):
                return ref[index * rows : (index + 1) * rows].astype(F32)

            read_in_ref[0] = unit(zero, 1)
            read_in_ref[1] = unit(zero, 0)
            read_in_ref[2] = unit(one, 0)
            read_out_ref[...] = unit(one, 1)
            self_in_ref[0] = unit(zero, 2)
            self_in_ref[1] = unit(one, 2)
            self_in_ref[2] = unit(one, 3)
            self_out_ref[...] = unit(zero, 3)


def feed_kernel(which_ref, gd_ref, he_ref, out_ref):
    part = pl.program_id(0)
    count, rows, _ = out_ref.shape
    slab = D // count

    @pl.when(which_ref[0] == 0)
    def _():
        grad = narrow(mm_tn(he_ref[...], gd_ref[...]).reshape(count, slab, D))
        out_ref[:, pl.ds(pl.multiple_of(part * slab, 8), slab), :] = grad

    @pl.when(which_ref[0] == 1)
    def _():
        grad = narrow(mm_tn(gd_ref[...], he_ref[...]).reshape(D // rows, rows, D))
        out_ref[pl.ds(part * (D // rows), D // rows)] = grad


def inner_back_kernel(
    piece0_ref, piece1_ref, piece2_ref, piece3_ref, q_all_ref, allowed_ref, k2_ref, v2_ref,
    dq2_ref, z1_ref, dz2_ref, norm_ref, in_ref, out_w_ref, q1_ref, p1_ref, k1_ref, v1_ref,
    dk2_ref, dv2_ref, dz1_ref, e1_ref, gain_ref, shift_ref, dq1_ref, dk1_ref, dv1_ref,
    do1_ref,
):
    step = pl.program_id(0)

    @pl.when(step == 0)
    def _():
        count = dq2_ref.shape[0]
        half, total = count // 2, q_all_ref.shape[0]

        def own_rows(ref):
            return jnp.concatenate([ref[:half], ref[total // 2 : total // 2 + half]], 0).astype(F32)

        q_all = q_all_ref[...]
        spread = gathered((piece0_ref, piece1_ref, piece2_ref, piece3_ref))
        do_all = spread[:, :D]
        stats = spread[:, D:]
        scores = mm_nt(expand(own_rows(k2_ref)), q_all) * FACTOR
        allowed = allowed_ref[...] > 0.5
        log_total = spread_stat(stats, 0, count)
        shares = jnp.where(allowed, jnp.exp(jnp.where(allowed, scores - log_total, 0.0)), 0.0)
        dv2 = narrow(collapse(mm(narrow(shares), do_all)))
        dshares = mm_nt(expand(own_rows(v2_ref)), do_all)
        dscores = narrow(shares * (dshares - spread_stat(stats, HEADS, count)))
        dk2 = narrow(collapse(mm(dscores, q_all)) * FACTOR)
        dk2_ref[...] = dk2
        dv2_ref[...] = dv2
        upstream = mm_nt(dq2_ref[...], in_ref[0]) + mm_nt(dk2, in_ref[1]) + mm_nt(dv2, in_ref[2])
        unit, inverse = norm_parts(z1_ref[...])
        gain_ref[...] = fold_rows(upstream * unit)
        shift_ref[...] = fold_rows(upstream)
        dz1 = dz2_ref[...] + norm_back(unit, inverse, norm_ref[2:3], upstream)
        dz1_ref[...] = dz1
        e1 = narrow(dz1)
        e1_ref[...] = e1
        do1_ref[...] = narrow(mm_nt(e1, out_w_ref[...])).astype(F32)

    own = pl.ds(pl.multiple_of(step * LAT, LAT), LAT)
    qx = expand(q1_ref[own, :])
    dox = expand(do1_ref[own, :])
    shares = p1_ref[...]
    dshares = mm_nt(dox, v1_ref[...])
    inner = jnp.sum(shares * dshares, axis=-1, keepdims=True)
    dscores = narrow(shares * (dshares - inner))
    dv1_ref[...] = narrow(mm_tn(narrow(shares), dox))
    dk1_ref[...] = narrow(mm_tn(dscores, qx) * FACTOR)
    dq1_ref[own, :] = collapse(mm(dscores, k1_ref[...])) * FACTOR


def input_back_kernel(
    x_ref, dx1_ref, dq3_ref, dk1_ref, dv1_ref, z_ref, dz1_ref, dq1_ref, norm_ref, in_ref, wq_ref,
    gain2_ref, shift2_ref, gain3_ref, shift3_ref, gain4_ref, shift4_ref,
    dx_ref, dz_ref, sums_ref, gain_ref, shift_ref,
):
    step = pl.program_id(0)

    def total(tensor):
        return jnp.sum(tensor, axis=0, keepdims=True)

    @pl.when(step == 0)
    def _():
        gain_ref[...] = jnp.zeros_like(gain_ref)
        shift_ref[...] = jnp.zeros_like(shift_ref)
        upstream = mm_nt(narrow(dq1_ref[...]), in_ref[0])
        unit, inverse = norm_parts(z_ref[...].astype(F32))
        sums_ref[...] = jnp.zeros_like(sums_ref)
        sums_ref[0:1] = total(upstream * unit)
        sums_ref[5:6] = total(upstream)
        for index, ref in enumerate((gain2_ref, gain3_ref, gain4_ref)):
            sums_ref[2 + index : 3 + index] = total(ref[...])
        for index, ref in enumerate((shift2_ref, shift3_ref, shift4_ref)):
            sums_ref[7 + index : 8 + index] = total(ref[...])
        dz_ref[...] = narrow(dz1_ref[...] + norm_back(unit, inverse, norm_ref[0:1], upstream))

    upstream = (
        mm_nt(dq3_ref[...], wq_ref[...])
        + mm_nt(dk1_ref[...], in_ref[1])
        + mm_nt(dv1_ref[...], in_ref[2])
    )
    unit, inverse = norm_parts(x_ref[...].astype(F32))
    gain_ref[...] += fold_rows(upstream * unit)
    shift_ref[...] += fold_rows(upstream)
    dx_ref[...] = narrow(dx1_ref[...] + norm_back(unit, inverse, norm_ref[1:2], upstream))

    @pl.when(step == pl.num_programs(0) - 1)
    def _():
        sums_ref[1:2] = total(gain_ref[...])
        sums_ref[6:7] = total(shift_ref[...])


def bits_of(count):
    bits = count.bit_length() - 1
    if 1 << bits != count:
        raise ValueError("axis size")
    return bits


def swap(tensor, axis, bit, count):
    return lax.ppermute(tensor, axis, [(i, i ^ (1 << bit)) for i in range(count)])


def own_bit(bit, axis="blk"):
    return (lax.axis_index(axis) >> bit) & 1


def gather_rows(tensor, count, line, fill):
    bits = bits_of(count)
    step = 0
    for bit in range(bits - 1, 1, -1):
        other = swap(line.gate(tensor), "blk", bit, count)
        beside = fill(step)
        line.note((other, beside) if beside is not None else other)
        tensor = jnp.stack([tensor, other], step)
        step += 1
    rows = tensor.shape[-2]
    left, right = tensor[..., : rows // 2, :], tensor[..., rows // 2 :, :]
    for bit_left, bit_right in ((1, 0), (0, 1)):
        got_left = swap(line.gate(left), "blk", bit_left, count)
        got_right = swap(line.gate(right), "blk", bit_right, count)
        beside = fill(step)
        line.note((got_left, got_right) + (() if beside is None else (beside,)))
        if bit_left == 1:
            left = jnp.stack([left, got_left], step)
            right = jnp.stack([right, got_right], step)
        step += 1
    return [piece.reshape(count // 2, -1, piece.shape[-1]) for piece in (left, got_left, right, got_right)]


def gather_places(count, groups):
    bits = bits_of(count)

    def spans(order):
        distances = [0]
        for bit in order:
            distances = [d | (on << bit) for d in distances for on in (0, 1)]
        return distances

    high = list(range(bits - 1, 1, -1))
    distance, place = [], []
    half = groups // 2
    for order, last, first in ((high + [1], 0, 0), (high + [0], 1, half)):
        for on in (0, 1):
            for d in spans(order):
                for group in range(first, first + half):
                    distance.append(d | (on << last))
                    place.append(group)
    return distance, place


def scatter_orders(bits):
    if bits < 3:
        return [list(range(bits))] * 3
    low, high = [0, 1], list(range(2, bits))
    return [
        low + high,
        [1] + high[:1] + [0] + high[1:],
        high[:1] + low + high[1:],
    ]


class Line:
    def __init__(self):
        self.last = None

    def gate(self, tensors):
        if self.last is None:
            return tensors
        tensors, _ = lax.optimization_barrier((tensors, self.last))
        return tensors

    def note(self, tensor):
        self.last = tensor


class Scatter:
    def __init__(self, line, count, orders):
        self.line, self.count, self.orders = line, count, orders
        self.left = [list(range(bits_of(count) - 1, -1, -1)) for _ in orders]
        self.step = 0

    def begin(self, parts):
        self.parts = parts
        self.send()

    def send(self):
        if self.step == len(self.orders[0]) - 1 and len({order[-1] for order in self.orders}) == 1:
            self.send_last()
            return
        lead = (self.count >> self.step) // 2
        picks, in_specs, operands, out_specs, out_shape, bits = [], [], [], [], [], []
        for (kept, got, rows, block), left, order in zip(self.parts, self.left, self.orders):
            bit = order[self.step]
            place = left.index(bit)
            left.pop(place)
            inner = lead >> place
            picks.append(own_bit(bit))
            bits.append(bit)
            spec = pl.BlockSpec(
                (None, 2, None, rows, D),
                lambda i, inner=inner, block=block: (i // inner, 0, i % inner, block, 0),
            )
            in_specs += [spec, spec]
            operands += [t.reshape(lead // inner, 2, inner, -1, D) for t in (kept, got)]
            out_specs += [pl.BlockSpec((None, rows, D), lambda i: (i, 0, 0))] * 2
            out_shape += [shaped((lead, rows, D), BF)] * 2
        moved = sum(3 * 4 * lead * part[2] * D for part in self.parts)
        out = call(
            functools.partial(stage_kernel, len(self.parts)), (lead,),
            [pl.BlockSpec(memory_space=pltpu.SMEM)] + in_specs, out_specs, out_shape, 0, moved, vmem=10,
        )(*self.line.gate((jnp.stack(picks).astype(jnp.int32), *operands)))
        self.line.note(out)
        got = [swap(sent, "blk", bit, self.count) for sent, bit in zip(out[::2], bits)]
        self.parts = [
            (stay, arrived, part[2], 0) for stay, arrived, part in zip(out[1::2], got, self.parts)
        ]
        self.step += 1

    def send_last(self):
        bit = self.orders[0][-1]
        rows = [part[2] for part in self.parts]
        operands = [t for kept, got, _, _ in self.parts for t in (kept, got)]
        shape = (sum(rows), D)
        send, stay = call(
            functools.partial(last_stage_kernel, len(rows)), (1,),
            [pl.BlockSpec(memory_space=pltpu.SMEM)] + [whole(t.shape) for t in operands], [whole(shape)] * 2,
            [shaped(shape, BF)] * 2, 0, 12 * shape[0] * D,
        )(*self.line.gate((own_bit(bit).reshape(1).astype(jnp.int32), *operands)))
        self.line.note(stay)
        self.parts = [(stay, swap(send, "blk", bit, self.count), shape[0], 0)]
        self.step += 1

    def flying(self):
        return [part[1] for part in self.parts]

    def result(self):
        ((stay, got, rows, _),) = self.parts
        return call(
            sum_kernel, (1,), [whole((rows, D))] * 2, whole((rows, D)), shaped((rows, D), BF), 0, 6 * rows * D,
        )(*self.line.gate((stay, got)))


def make_body(n_blk, n_rep):
    rep_bits = bits_of(n_rep)
    orders = scatter_orders(bits_of(n_blk))
    rows = D // n_blk

    def body(
        patches, latents, norm_gain, norm_bias, read_in, read_out, self_in, self_out,
        write_in, write_out, feed_up, feed_down, group_image, cot_patches, cot_latents,
    ):
        x, z, cot, cot_z = patches[0], latents[0], cot_patches[0], cot_latents[0]
        tokens, lat = x.shape[0], z.shape[0]
        groups = lat // LAT
        size = tokens // groups
        total = lat * n_blk
        hidden = feed_up.shape[1]
        feed_rows = hidden // n_blk
        core = lax.axis_index("rep") & 1
        core_at = core.reshape(1).astype(jnp.int32)
        other_at = 1 - core_at
        norms = jnp.concatenate([norm_gain, norm_bias, jnp.zeros((6, D), BF)], 0).astype(F32)
        norm_spec = whole((16, D))
        square = whole((D, D))
        three = whole((3, D, D))
        lat_spec = whole((lat, D))
        fold_spec = whole((8, D))
        patch_spec = rows_of((size, D))
        smem = pl.BlockSpec(memory_space=pltpu.SMEM)
        share_spec = pl.BlockSpec((None, HL, size), lambda g: (g, 0, 0))
        grid = (groups,)
        unit_flops = 2 * tokens * D * D
        low_lat, full_lat, fold = shaped((lat, D), BF), shaped((lat, D), F32), shaped((8, D), F32)
        low_patch = shaped((tokens, D), BF)
        line = Line()

        a1, q1, b1, k1, v1, p1, o1, z1, a2 = call(
            read_forward_kernel, grid,
            [patch_spec, lat_spec, norm_spec, three, square],
            [lat_spec, lat_spec, patch_spec, patch_spec, patch_spec, share_spec, lat_spec, lat_spec, lat_spec],
            [low_lat, full_lat, low_patch, low_patch, low_patch, shaped((groups, HL, size), F32),
             low_lat, full_lat, low_lat],
            2 * unit_flops, 12 * tokens * D,
            [pltpu.VMEM((lat, D), F32)],
        )(in_hbm(x), z, norms, in_hbm(read_in), in_hbm(read_out))

        q3 = []

        def fill_first(step):
            if step == 0:
                q3.append(narrow(mm(b1, write_in[0])))
                return q3[0]
            return None

        pieces = gather_rows(a2, n_blk, line, fill_first)
        q3 = q3[0]

        me = lax.axis_index("blk")
        distance, place = gather_places(n_blk, groups)
        places = (me ^ jnp.array(distance, jnp.int32)) * groups + jnp.array(place, jnp.int32)
        own_at = me * groups + jnp.arange(groups, dtype=jnp.int32)
        piece_shape = (n_blk // 2, lat // 2)
        hl2 = HEADS * lat
        a2_all, allowed, k2, v2, p2, l2, o2, z2, out_latents, b3, k3, v3 = call(
            self_forward_kernel, (1,),
            [smem] * 3 + [whole(piece_shape + (D,))] * 4 + [lat_spec, lat_spec, norm_spec, three, square,
             one_of(1), one_of(2)],
            [whole((total, D)), whole((hl2, total)), whole((total, D)), whole((total, D)), whole((hl2, total)),
             whole((hl2, 1))] + [lat_spec] * 6,
            [shaped((total, D), BF), shaped((hl2, total), F32), shaped((total, D), BF), shaped((total, D), BF),
             shaped((hl2, total), F32), shaped((hl2, 1), F32),
             low_lat, full_lat, low_lat, low_lat, full_lat, full_lat],
            unit_flops * 2, 10 * D * D * 2,
        )(group_image, places, own_at, *pieces, a2, z1, norms, self_in, self_out, write_in, write_in)

        pair_spec = pl.BlockSpec((2, size, D), lambda g: (0, g, 0))
        out_patches, he, gd, o3, e3, dq3, dx1, dk3, dv3, gain4, shift4 = call(
            functools.partial(patch_kernel, D), grid,
            [patch_spec, patch_spec, patch_spec, lat_spec, lat_spec, norm_spec, square,
             whole((D, hidden)), whole((hidden, D))],
            [patch_spec, pair_spec, pl.BlockSpec((2, size, hidden), lambda g: (0, g, 0)), patch_spec, patch_spec,
             patch_spec, patch_spec, rows_of((LAT, D)), rows_of((LAT, D)), fold_spec, fold_spec],
            [low_patch, shaped((2, tokens, D), BF), shaped((2, tokens, hidden), BF),
             low_patch, low_patch, low_patch, shaped((tokens, D), F32), full_lat, full_lat, fold, fold],
            unit_flops * 20, 40 * tokens * D, vmem=40,
        )(in_hbm(x), in_hbm(q3), in_hbm(cot), k3, v3, norms, write_out, feed_up, feed_down)

        width = D + 128
        dk3, dv3, dz2, e2, payload, dq2, gain3, shift3 = call(
            latent_back_kernel, (1,),
            [lat_spec] * 4 + [whole((total, D))] * 2
            + [whole((hl2, total)), whole((hl2, 1)), norm_spec, one_of(1), one_of(2), square],
            [lat_spec] * 4 + [whole((lat, width)), lat_spec, fold_spec, fold_spec],
            [low_lat, low_lat, full_lat, low_lat, shaped((lat, width), BF), low_lat, fold, fold],
            unit_flops, 10 * D * D,
        )(dk3, dv3, z2, cot_z, k2, v2, p2, l2, norms, write_in, write_in, self_out)
        line.note(payload)

        def feed_grad(which):
            return pl.pallas_call(
                feed_kernel,
                grid_spec=pltpu.PrefetchScalarGridSpec(
                    num_scalar_prefetch=1,
                    grid=(hidden // D,),
                    in_specs=[
                        pl.BlockSpec((None, tokens, D), lambda j, w: (w[0], 0, j)),
                        pl.BlockSpec((None, tokens, D), lambda j, w: (w[0], 0, 0), pipeline_mode=pl.Buffered(1)),
                    ],
                    out_specs=pl.BlockSpec((n_blk, feed_rows, D), lambda j, w: (0, 0, 0), pipeline_mode=pl.Buffered(1)),
                ),
                out_shape=shaped((n_blk, feed_rows, D), BF),
                compiler_params=pltpu.CompilerParams(
                    vmem_limit_bytes=20 << 20, dimension_semantics=("arbitrary",)
                ),
                cost_estimate=pl.CostEstimate(
                    flops=unit_flops * 4, bytes_accessed=20 * tokens * D, transcendentals=0
                ),
            )(*line.gate((which, in_hbm(gd), in_hbm(he))))

        whole_patch = whole((tokens, D))

        def unit_grads(kernel, patch_sized, lat_sized, count):
            return call(
                kernel, (1,),
                [smem] + [whole_patch] * len(patch_sized) + [lat_spec] * len(lat_sized),
                [whole((n_blk, count * rows, D))] * 2, [shaped((n_blk, count * rows, D), BF)] * 2,
                unit_flops, 8 * tokens * D,
            )(*line.gate((core_at, *patch_sized, *lat_sized)))

        def core_swap(tensor):
            return swap(line.gate(tensor), "rep", 0, n_rep)

        early = {}
        first = Scatter(line, n_blk, orders)

        def fill_second(step):
            if step == 0:
                early["feed_other"] = feed_grad(other_at)
                return early["feed_other"]
            if step == 1:
                early["feed_got"] = core_swap(early["feed_other"])
                early["feed_mine"] = feed_grad(core_at)
                return early["feed_mine"], early["feed_got"]
            if step == 2:
                early["other"], early["mine"] = unit_grads(early_kernel, (o3, e3, b1, dq3), (b3, dk3, dv3), 2)
                return early["mine"]
            early["got"] = core_swap(early["other"])
            early["q2_all"] = narrow(mm(line.gate(a2_all), self_in[0]))
            return early["q2_all"], early["got"]

        spread_pieces = gather_rows(payload, n_blk, line, fill_second)
        half = feed_rows // 2
        first.begin([
            (early["feed_mine"], early["feed_got"], half, 0),
            (early["feed_mine"], early["feed_got"], half, 1),
            (early["mine"], early["got"], 2 * rows, 0),
        ])

        dk2, dv2, dz1, e1, gain2, shift2, dq1, dk1, dv1 = call(
            inner_back_kernel, grid,
            [whole(piece_shape + (width,))] * 4 + [whole((total, D)), whole((hl2, total))]
            + [whole((total, D))] * 2 + [lat_spec] * 3 + [norm_spec, three, square, lat_spec, share_spec]
            + [patch_spec] * 2,
            [lat_spec] * 4 + [fold_spec] * 2 + [lat_spec] + [patch_spec] * 2,
            [low_lat, low_lat, full_lat, low_lat, fold, fold, full_lat, low_patch, low_patch],
            2 * unit_flops, 10 * tokens * D,
            [pltpu.VMEM((lat, D), F32)],
        )(*line.gate((*spread_pieces, early["q2_all"], allowed, k2, v2,
                      dq2, z1, dz2, norms, self_in, read_out, q1, in_hbm(p1), in_hbm(k1), in_hbm(v1))))
        line.note((dk1, first.flying()))
        first.send()

        late_other, late_mine = unit_grads(
            late_kernel, (b1, dk1, dv1), (a1, narrow(dq1), o1, e1, a2, dq2, o2, e2, dk2, dv2), 4
        )
        line.note((late_mine, first.flying()))
        late_got = core_swap(late_other)
        first.send()

        dx, dz, norm_grads = call(
            input_back_kernel, grid,
            [patch_spec] * 5 + [lat_spec] * 3 + [norm_spec, three, one_of(0)] + [fold_spec] * 6,
            [patch_spec, lat_spec, norm_spec],
            [low_patch, low_lat, shaped((16, D), F32)],
            unit_flops * 3, 14 * tokens * D,
            [pltpu.VMEM((8, D), F32)] * 2,
        )(*line.gate((in_hbm(x), in_hbm(dx1), in_hbm(dq3), dk1, dv1, z, dz1, dq1, norms, read_in, write_in,
                      gain2, shift2, gain3, shift3, gain4, shift4)))
        norm_got = swap(norm_grads, "rep", 0, n_rep)
        line.note((dx, late_got, first.flying()))
        last = Scatter(line, n_blk, orders)
        last_rows = 4 * rows // 3
        last.begin([(late_mine, late_got, last_rows, i) for i in range(3)])
        first.send()
        norm_grads = norm_grads + norm_got
        for bit in range(1, rep_bits):
            norm_grads = norm_grads + swap(line.gate(norm_grads), "rep", bit, n_rep)
        bits = bits_of(n_blk)

        def finish(flat):
            for bit in range(1, rep_bits):
                flat = narrow(flat.astype(F32) + swap(flat, "rep", bit, n_rep).astype(F32))
            return flat, swap(flat, "rep", 0, n_rep)

        def outputs(kernel, flat, partner, shapes):
            return call(
                kernel, (1,), [smem, whole(flat.shape), whole(flat.shape)], [whole(t) for t in shapes],
                [shaped(t, F32) for t in shapes], 0, 12 * flat.shape[0] * D,
            )(*line.gate((core_at, flat, partner)))

        for step in range(bits):
            got = swap(line.gate(norm_grads), "blk", step, n_blk)
            if step == 0:
                line.note((last.flying(), first.flying(), got))
            elif step == 1:
                last.send()
                while first.step < bits:
                    line.note(first.flying())
                    first.send()
                flat, partner = finish(first.result())
                up, down, wo, write_in_grad = outputs(
                    early_out_kernel, flat, partner, [(rows, hidden), (feed_rows, D), (rows, D), (3, rows, D)]
                )
                line.note((last.flying(), got, up))
            else:
                if last.step < bits:
                    last.send()
                line.note((last.flying(), got))
            norm_grads = norm_grads + got
        while last.step < bits:
            last.send()
            line.note(last.flying())
        flat, partner = finish(last.result())
        read_in_grad, read_out_grad, self_in_grad, self_out_grad = outputs(
            late_out_kernel, flat, partner, [(3, rows, D), (rows, D), (3, rows, D), (rows, D)]
        )
        norm_own = lax.dynamic_slice_in_dim(norm_grads, lax.axis_index("blk") * rows, rows, 1)
        return (
            out_patches[None], out_latents[None], dx[None], dz[None], norm_own[:5], norm_own[5:10],
            read_in_grad, read_out_grad, self_in_grad, self_out_grad, write_in_grad, wo, up, down,
        )

    return body


def solution(mesh):
    return jax.shard_map(
        make_body(mesh.shape["blk"], mesh.shape["rep"]),
        mesh=mesh,
        in_specs=(
            P("rep", "blk", None), P("rep", "blk", None), P(), P(), P(), P(), P(), P(), P(), P(), P(), P(),
            P("rep", None), P("rep", "blk", None), P("rep", "blk", None),
        ),
        out_specs=(
            P("rep", "blk", None), P("rep", "blk", None), P("rep", "blk", None), P("rep", "blk", None),
            P(None, "blk"), P(None, "blk"), P(None, "blk", None), P("blk", None), P(None, "blk", None),
            P("blk", None), P(None, "blk", None), P("blk", None), P("blk", None), P("blk", None),
        ),
        check_vma=False,
    )
```

```python
import functools

import jax
import jax.numpy as jnp
from jax import lax
from jax.experimental import pallas as pl
from jax.experimental.pallas import tpu as pltpu
from jax.sharding import PartitionSpec as P

D = 768
HEADS = 12
HEAD = 64
LAT = 8
FACTOR = HEAD ** (-0.5)
HL = HEADS * LAT
BF = jnp.bfloat16
F32 = jnp.float32


def narrow(tensor):
    return tensor.astype(BF)


def mm(left, right):
    return lax.dot_general(left, right, (((1,), (0,)), ((), ())), preferred_element_type=F32)


def mm_tn(left, right):
    return lax.dot_general(left, right, (((0,), (0,)), ((), ())), preferred_element_type=F32)


def mm_nt(left, right):
    return lax.dot_general(left, right, (((1,), (1,)), ((), ())), preferred_element_type=F32)


def norm_parts(tensor):
    center = tensor - jnp.mean(tensor, axis=-1, keepdims=True)
    spread = jnp.mean(center * center, axis=-1, keepdims=True)
    inverse = lax.rsqrt(spread + 1e-06)
    return center * inverse, inverse


def norm_forward(tensor, gain, shift):
    unit, _ = norm_parts(tensor)
    return unit * gain + shift


def norm_back(unit, inverse, gain, upstream):
    scaled = upstream * gain
    return inverse * (
        scaled
        - jnp.mean(scaled, axis=-1, keepdims=True)
        - unit * jnp.mean(scaled * unit, axis=-1, keepdims=True)
    )


def fold_rows(tensor):
    rows, cols = tensor.shape
    return jnp.sum(tensor.reshape(rows // 8, 8, cols), axis=0)


def head_mask():
    head = lax.broadcasted_iota(jnp.int32, (HEADS, 1, D), 0)
    feature = lax.broadcasted_iota(jnp.int32, (HEADS, 1, D), 2)
    return (feature >= head * HEAD) & (feature < head * HEAD + HEAD)


def expand(rows):
    count = rows.shape[0]
    return narrow(jnp.where(head_mask(), rows[None], 0.0).reshape(HEADS * count, D))


def collapse(rows):
    count = rows.shape[0] // HEADS
    return jnp.sum(jnp.where(head_mask(), rows.reshape(HEADS, count, D), 0.0), axis=0)


def whole(shape):
    return pl.BlockSpec(shape, lambda *_: (0,) * len(shape), pipeline_mode=pl.Buffered(1))


def rows_of(shape):
    return pl.BlockSpec(shape, lambda g: (g,) + (0,) * (len(shape) - 1))


def one_of(index):
    return pl.BlockSpec(
        (None, D, D), lambda *_: (index, 0, 0), pipeline_mode=pl.Buffered(1)
    )


def shaped(shape, dtype):
    return jax.ShapeDtypeStruct(shape, dtype)


def in_hbm(tensor):
    return pltpu.with_memory_space_constraint(tensor, pltpu.HBM)


def image_marks(image_ref, places_ref, shape, axis, rows):
    index = lax.broadcasted_iota(jnp.int32, shape, axis)
    marks = jnp.zeros(shape, jnp.int32)
    for group in range(shape[axis] // rows):
        inside = (index >= group * rows) & (index < (group + 1) * rows)
        marks = jnp.where(inside, image_ref[0, places_ref[group]], marks)
    return marks


def gathered(refs):
    pieces = [ref[...] for ref in refs]
    return jnp.concatenate([piece.reshape(-1, piece.shape[-1]) for piece in pieces], 0)


def call(body, grid, in_specs, out_specs, out_shape, flops, moved, scratch=(), vmem=20):
    return pl.pallas_call(
        body,
        grid=grid,
        in_specs=in_specs,
        out_specs=out_specs,
        out_shape=out_shape,
        scratch_shapes=scratch,
        compiler_params=pltpu.CompilerParams(
            vmem_limit_bytes=vmem << 20, dimension_semantics=("arbitrary",) * len(grid)
        ),
        cost_estimate=pl.CostEstimate(
            flops=int(flops), bytes_accessed=int(moved), transcendentals=0
        ),
    )


def read_forward_kernel(
    x_ref, z_ref, norm_ref, in_ref, out_w_ref,
    a1_ref, q1_ref, b1_ref, k1_ref, v1_ref, p1_ref, o1_ref, z1_ref, a2_ref,
    mix_ref,
):
    step = pl.program_id(0)
    last = pl.num_programs(0) - 1

    @pl.when(step == 0)
    def _():
        a1 = narrow(norm_forward(z_ref[...].astype(F32), norm_ref[0:1], norm_ref[5:6]))
        a1_ref[...] = a1
        q1_ref[...] = narrow(mm(a1, in_ref[0])).astype(F32)

    b1 = narrow(norm_forward(x_ref[...].astype(F32), norm_ref[1:2], norm_ref[6:7]))
    b1_ref[...] = b1
    k1 = narrow(mm(b1, in_ref[1]))
    v1 = narrow(mm(b1, in_ref[2]))
    k1_ref[...] = k1
    v1_ref[...] = v1
    own = pl.ds(pl.multiple_of(step * LAT, LAT), LAT)
    scores = mm_nt(expand(q1_ref[own, :]), k1) * FACTOR
    powers = jnp.exp(scores - jnp.max(scores, axis=-1, keepdims=True))
    shares = powers / jnp.sum(powers, axis=-1, keepdims=True)
    p1_ref[...] = shares
    mix_ref[own, :] = collapse(mm(narrow(shares), v1))

    @pl.when(step == last)
    def _():
        o1 = narrow(mix_ref[...])
        o1_ref[...] = o1
        z1 = z_ref[...].astype(F32) + mm(o1, out_w_ref[...])
        z1_ref[...] = z1
        a2_ref[...] = narrow(norm_forward(z1, norm_ref[2:3], norm_ref[7:8]))


def self_forward_kernel(
    image_ref, places_ref, own_at_ref, piece0_ref, piece1_ref, piece2_ref, piece3_ref,
    a2_ref, z1_ref, norm_ref, in_ref, out_w_ref, wk_ref, wv_ref,
    all_ref, allowed_ref, k2_ref, v2_ref, p2_ref, l2_ref, o2_ref, z2_ref, out_ref, b3_ref, k3_ref, v3_ref,
):
    everyone = gathered((piece0_ref, piece1_ref, piece2_ref, piece3_ref))
    all_ref[...] = everyone
    k2 = narrow(mm(everyone, in_ref[1]))
    v2 = narrow(mm(everyone, in_ref[2]))
    k2_ref[...] = k2
    v2_ref[...] = v2
    q2 = narrow(mm(a2_ref[...], in_ref[0])).astype(F32)
    scores = mm_nt(expand(q2), k2) * FACTOR
    total, count = everyone.shape[0], q2.shape[0]
    owners = image_marks(image_ref, places_ref, (1, total), 1, LAT)
    own = jnp.concatenate([image_marks(image_ref, own_at_ref, (count, 1), 0, LAT)] * HEADS, 0)
    allowed = own == owners
    allowed_ref[...] = jnp.where(allowed, 1.0, 0.0)
    scores = jnp.where(allowed, scores, -1e30)
    highest = jnp.max(scores, axis=-1, keepdims=True)
    powers = jnp.exp(scores - highest)
    totals = jnp.sum(powers, axis=-1, keepdims=True)
    shares = powers / totals
    p2_ref[...] = shares
    l2_ref[...] = highest + jnp.log(totals)
    o2 = narrow(collapse(mm(narrow(shares), v2)))
    o2_ref[...] = o2
    z2 = z1_ref[...] + mm(o2, out_w_ref[...])
    z2_ref[...] = z2
    out_ref[...] = narrow(z2)
    b3 = narrow(norm_forward(z2, norm_ref[3:4], norm_ref[8:9]))
    b3_ref[...] = b3
    k3_ref[...] = narrow(mm(b3, wk_ref[...])).astype(F32)
    v3_ref[...] = narrow(mm(b3, wv_ref[...])).astype(F32)


ROOT_HALF = 0.7071067811865476
DENSITY = 0.3989422804014327


def patch_kernel(
    chunk, size, core_ref, x_ref, q3_ref, cot_ref, k3_ref, v3_ref, norm_ref, wo_ref, up_ref, down_ref, b1_ref, b3_ref,
    out_ref, h_ref, gd_ref, dq3_ref, dx1_ref, dk3_ref, dv3_ref, other_ref, mine_ref,
    gain_ref, shift_ref, o3_ref, e3_ref,
):
    step = pl.program_id(0)
    tokens = x_ref.shape[0]
    each = tokens // size
    here = pl.ds(pl.multiple_of(step * tokens, tokens), tokens)
    keys, values, weights = [], [], []
    for index in range(each):
        own = pl.ds(pl.multiple_of((step * each + index) * LAT, LAT), LAT)
        kx, vx = expand(k3_ref[own, :]), expand(v3_ref[own, :])
        rows = slice(index * size, (index + 1) * size)
        scores = (mm_nt(kx, q3_ref[rows]) * FACTOR).reshape(HEADS, LAT, size)
        powers = jnp.exp(scores - jnp.max(scores, axis=1, keepdims=True))
        shares = powers / jnp.sum(powers, axis=1, keepdims=True)
        keys.append(kx)
        values.append(vx)
        weights.append(shares)
    mixed = [narrow(mm_tn(narrow(w.reshape(HL, size)), v)) for w, v in zip(weights, values)]
    o3 = jnp.concatenate(mixed, 0) if each > 1 else mixed[0]
    o3_ref[here, :] = o3
    x1 = x_ref[...].astype(F32) + mm(o3, wo_ref[...])
    unit, inverse = norm_parts(x1)
    gain = norm_ref[4:5]
    h = narrow(unit * gain + norm_ref[9:10])
    h_ref[...] = h
    e4 = cot_ref[...]
    x2 = x1
    dh = jnp.zeros((tokens, D), F32)
    hidden = up_ref.shape[1]
    for start in range(0, hidden, chunk):
        part = slice(start, start + chunk)
        u = mm(h, up_ref[:, part])
        cdf = 0.5 + 0.5 * lax.erf(u * ROOT_HALF)
        g = narrow(u * cdf)
        gd_ref[1, :, part] = g
        x2 = x2 + mm(g, down_ref[part, :])
        slope = cdf + u * (jnp.exp(-0.5 * u * u) * DENSITY)
        du = narrow(mm_nt(e4, down_ref[part, :]) * slope)
        gd_ref[0, :, part] = du
        dh = dh + mm_nt(du, up_ref[:, part])
    out_ref[...] = narrow(x2)

    @pl.when(step == 0)
    def _():
        gain_ref[...] = jnp.zeros_like(gain_ref)
        shift_ref[...] = jnp.zeros_like(shift_ref)

    gain_ref[...] += fold_rows(dh * unit)
    shift_ref[...] += fold_rows(dh)
    dx1 = e4.astype(F32) + norm_back(unit, inverse, gain, dh)
    dx1_ref[...] = dx1
    e3 = narrow(dx1)
    e3_ref[here, :] = e3
    do3 = narrow(mm_nt(e3, wo_ref[...]))
    for index in range(each):
        own = pl.ds(pl.multiple_of((step * each + index) * LAT, LAT), LAT)
        place = pl.ds(pl.multiple_of((step * each + index) * size, size), size)
        rows = slice(index * size, (index + 1) * size)
        kx, vx, shares = keys[index], values[index], weights[index]
        grad = do3[rows]
        dshares = mm_nt(vx, grad).reshape(HEADS, LAT, size)
        inner = jnp.sum(shares * dshares, axis=1, keepdims=True)
        dscores = narrow((shares * (dshares - inner)).reshape(HL, size))
        dq3_ref[place, :] = narrow(mm_tn(dscores, kx) * FACTOR)
        dv3_ref[own, :] = narrow(collapse(mm(narrow(shares.reshape(HL, size)), grad))).astype(F32)
        dk3_ref[own, :] = narrow(collapse(mm(dscores, q3_ref[rows])) * FACTOR).astype(F32)

    @pl.when(step == pl.num_programs(0) - 1)
    def _():
        b3 = b3_ref[...]
        put_units(core_ref, other_ref, mine_ref,
                  [[(o3_ref, e3_ref), (b3, narrow(dk3_ref[...]))], [(b1_ref, dq3_ref), (b3, narrow(dv3_ref[...]))]])


STAT = 2 * HEADS


def latent_back_kernel(
    dk3_ref, dv3_ref, z2_ref, cot_ref, k2_ref, v2_ref, p2_ref, l2_ref, norm_ref, wk_ref, wv_ref, out_w_ref,
    dz2_ref, e2_ref, send_ref, dq2_ref, gain_ref, shift_ref,
):
    dk3 = narrow(dk3_ref[...])
    dv3 = narrow(dv3_ref[...])
    upstream = mm_nt(dk3, wk_ref[...]) + mm_nt(dv3, wv_ref[...])
    unit, inverse = norm_parts(z2_ref[...])
    gain_ref[...] = fold_rows(upstream * unit)
    shift_ref[...] = fold_rows(upstream)
    dz2 = cot_ref[...].astype(F32) + norm_back(unit, inverse, norm_ref[3:4], upstream)
    dz2_ref[...] = dz2
    e2 = narrow(dz2)
    e2_ref[...] = e2
    do2 = narrow(mm_nt(e2, out_w_ref[...]))
    send_ref[:, :D] = do2
    shares = p2_ref[...]
    dshares = mm_nt(expand(do2.astype(F32)), v2_ref[...])
    inner = jnp.sum(shares * dshares, axis=-1, keepdims=True)
    count = do2.shape[0]
    lane = lax.broadcasted_iota(jnp.int32, (count, 128), 1)
    stats = jnp.zeros((count, 128), F32)
    for slot, columns in ((0, l2_ref[...]), (HEADS, inner)):
        for head in range(HEADS):
            place = slot + head
            chosen = (lane == place) | (lane == place + STAT) | (lane == place + 2 * STAT)
            stats = jnp.where(chosen, columns[head * count : (head + 1) * count], stats)
    top = narrow(stats)
    rest = stats - top.astype(F32)
    middle = narrow(rest)
    bottom = narrow(rest - middle.astype(F32))
    send_ref[:, D:] = narrow(
        jnp.where(lane < STAT, top.astype(F32), jnp.where(lane < 2 * STAT, middle.astype(F32), bottom.astype(F32)))
    )
    dscores = narrow(shares * (dshares - inner))
    dq2_ref[...] = narrow(collapse(mm(dscores, k2_ref[...])) * FACTOR)


def spread_stat(stats, slot, count):
    shape = (HEADS * count, 128)
    place = lax.broadcasted_iota(jnp.int32, shape, 1)
    column = lax.broadcasted_iota(jnp.int32, shape, 0)
    chosen = jnp.zeros(shape, jnp.bool_)
    for term in range(3):
        head = place - (slot + term * STAT)
        chosen |= (head >= 0) & (head < HEADS) & (column >= head * count) & (column < (head + 1) * count)
    return mm_nt(narrow(jnp.where(chosen, 1.0, 0.0)), stats)


def unit_grad(left, right, count):
    return mm_tn(left[...], right[...]).reshape(count, D // count, D)


def put_units(core_ref, other_ref, mine_ref, units):
    count = mine_ref.shape[0]
    rows = D // count
    for core in range(2):
        @pl.when(core_ref[0] == core)
        def _():
            for ref, pairs in ((other_ref, units[1 - core]), (mine_ref, units[core])):
                for index, (left, right) in enumerate(pairs):
                    ref[:, index * rows : (index + 1) * rows, :] = narrow(unit_grad(left, right, count))


def cut_kernel(bit, pick_ref, keep_ref, got_ref, send_ref, stay_ref):
    zero, one = halves(keep_ref[...].astype(F32) + got_ref[...].astype(F32), bit)
    mine = pick_ref[0] == 0
    send_ref[...] = narrow(jnp.where(mine, one, zero))
    stay_ref[...] = narrow(jnp.where(mine, zero, one))


def stage_kernel(parts, pick_ref, *refs):
    for index in range(parts):
        keep_ref, got_ref = refs[2 * index : 2 * index + 2]
        send_ref, stay_ref = refs[2 * parts + 2 * index : 2 * parts + 2 * index + 2]
        mine = pick_ref[index]
        send_ref[...] = narrow(keep_ref[1 - mine].astype(F32) + got_ref[1 - mine].astype(F32))
        stay_ref[...] = narrow(keep_ref[mine].astype(F32) + got_ref[mine].astype(F32))


def last_stage_kernel(parts, pick_ref, *refs):
    send_ref, stay_ref = refs[2 * parts :]
    mine = pick_ref[0]
    start = 0
    for index in range(parts):
        keep_ref, got_ref = refs[2 * index : 2 * index + 2]
        rows = keep_ref.shape[1]
        span = slice(start, start + rows)
        send_ref[span] = narrow(keep_ref[1 - mine].astype(F32) + got_ref[1 - mine].astype(F32))
        stay_ref[span] = narrow(keep_ref[mine].astype(F32) + got_ref[mine].astype(F32))
        start += rows


def sum_kernel(keep_ref, got_ref, out_ref):
    out_ref[...] = narrow(keep_ref[...].astype(F32) + got_ref[...].astype(F32))


def early_out_kernel(core_ref, mine_ref, partner_ref, up_ref, down_ref, wo_ref, in_ref):
    rows = wo_ref.shape[0]
    feed_rows = down_ref.shape[0]
    for core in range(2):
        @pl.when(core_ref[0] == core)
        def _():
            zero, one = (mine_ref, partner_ref) if core == 0 else (partner_ref, mine_ref)
            for index in range(feed_rows // rows):
                up_ref[:, index * D : (index + 1) * D] = zero[index * rows : (index + 1) * rows].astype(F32)
            down_ref[...] = one[:feed_rows].astype(F32)
            wo_ref[...] = zero[feed_rows : feed_rows + rows].astype(F32)
            in_ref[0] = one[feed_rows : feed_rows + rows].astype(F32)
            in_ref[1] = zero[feed_rows + rows :].astype(F32)
            in_ref[2] = one[feed_rows + rows :].astype(F32)


def late_out_kernel(core_ref, mine_ref, partner_ref, read_in_ref, read_out_ref, self_in_ref, self_out_ref):
    rows = read_out_ref.shape[0]
    for core in range(2):
        @pl.when(core_ref[0] == core)
        def _():
            zero, one = (mine_ref, partner_ref) if core == 0 else (partner_ref, mine_ref)

            def unit(ref, index):
                return ref[index * rows : (index + 1) * rows].astype(F32)

            read_in_ref[0] = unit(zero, 1)
            read_in_ref[1] = unit(zero, 0)
            read_in_ref[2] = unit(one, 0)
            read_out_ref[...] = unit(one, 1)
            self_in_ref[0] = unit(zero, 2)
            self_in_ref[1] = unit(one, 2)
            self_in_ref[2] = unit(one, 3)
            self_out_ref[...] = unit(zero, 3)


def feed_kernel(which_ref, gd_ref, h_ref, e4_ref, out_ref):
    part = pl.program_id(0)
    count, rows, _ = out_ref.shape
    slab = D // count

    @pl.when(which_ref[0] == 0)
    def _():
        grad = narrow(mm_tn(h_ref[...], gd_ref[...]).reshape(count, slab, D))
        out_ref[:, pl.ds(pl.multiple_of(part * slab, 8), slab), :] = grad

    @pl.when(which_ref[0] == 1)
    def _():
        grad = narrow(mm_tn(gd_ref[...], e4_ref[...]).reshape(D // rows, rows, D))
        out_ref[pl.ds(part * (D // rows), D // rows)] = grad


def halves(tensor, bit):
    count, rows, cols = tensor.shape
    cut = tensor.reshape(count >> (bit + 1), 2, 1 << bit, rows, cols)
    return cut[:, 0].reshape(count // 2, rows, cols), cut[:, 1].reshape(count // 2, rows, cols)


def feed_sum_kernel(
    bits, which_ref, gd_ref, h_ref, e4_ref, got_up_ref, got_down_ref, send0_ref, stay0_ref, send1_ref, stay1_ref
):
    part = pl.program_id(0)
    count, slab, _ = got_up_ref.shape
    near, rows, _ = got_down_ref.shape
    half = rows // 2
    per_part = half // slab

    def store(refs, index, value, bit):
        zero, one = halves(value, bit)
        mine = which_ref[1 + (0 if bit == bits[0] else 1)] == 0
        refs[0][index] = narrow(jnp.where(mine, one, zero))
        refs[1][index] = narrow(jnp.where(mine, zero, one))

    pairs = ((send0_ref, stay0_ref), (send1_ref, stay1_ref))

    @pl.when(which_ref[0] == 0)
    def _():
        grad = mm_tn(h_ref[...], gd_ref[...]).reshape(count, slab, D) + got_up_ref[...].astype(F32)
        for index in range(2):
            @pl.when(part // per_part == index)
            def _():
                place = pl.ds(pl.multiple_of(lax.rem(part, per_part) * slab, 8), slab)
                store(pairs[index], (slice(None), place), grad, bits[index])

    @pl.when(which_ref[0] == 1)
    def _():
        grad = mm_tn(gd_ref[...], e4_ref[...]).reshape(near, rows, D) + got_down_ref[...].astype(F32)
        for index in range(2):
            store(pairs[index], (pl.ds(part * (near // 2), near // 2),),
                  grad[:, index * half : (index + 1) * half], bits[index])


def tail_kernel(
    core_ref, piece0_ref, piece1_ref, piece2_ref, piece3_ref, everyone_ref, allowed_ref, k2_ref, v2_ref,
    dq2_ref, z1_ref, dz2_ref, norm_ref, self_in_ref, read_out_ref, q1_ref, p1_ref, k1_ref, v1_ref,
    b1_ref, a1_ref, o1_ref, a2_ref, o2_ref, e2_ref,
    other_ref, mine_ref, dk1_ref, dv1_ref, dq1_ref, dz1_ref, gain_ref, shift_ref,
    do1_ref, e1_ref, dk2_ref, dv2_ref,
):
    step = pl.program_id(0)
    last = pl.num_programs(0) - 1

    @pl.when(step == 0)
    def _():
        count = dq2_ref.shape[0]
        half, everything = count // 2, everyone_ref.shape[0]

        def own_rows(ref):
            return jnp.concatenate([ref[:half], ref[everything // 2 : everything // 2 + half]], 0).astype(F32)

        q_all = narrow(mm(everyone_ref[...], self_in_ref[0]))
        spread = gathered((piece0_ref, piece1_ref, piece2_ref, piece3_ref))
        do_all = spread[:, :D]
        stats = spread[:, D:]
        scores = mm_nt(expand(own_rows(k2_ref)), q_all) * FACTOR
        allowed = allowed_ref[...] > 0.5
        log_total = spread_stat(stats, 0, count)
        shares = jnp.where(allowed, jnp.exp(jnp.where(allowed, scores - log_total, 0.0)), 0.0)
        dv2 = narrow(collapse(mm(narrow(shares), do_all)))
        dshares = mm_nt(expand(own_rows(v2_ref)), do_all)
        dscores = narrow(shares * (dshares - spread_stat(stats, HEADS, count)))
        dk2 = narrow(collapse(mm(dscores, q_all)) * FACTOR)
        dk2_ref[...] = dk2
        dv2_ref[...] = dv2
        upstream = (
            mm_nt(dq2_ref[...], self_in_ref[0]) + mm_nt(dk2, self_in_ref[1]) + mm_nt(dv2, self_in_ref[2])
        )
        unit, inverse = norm_parts(z1_ref[...])
        gain_ref[...] = fold_rows(upstream * unit)
        shift_ref[...] = fold_rows(upstream)
        dz1 = dz2_ref[...] + norm_back(unit, inverse, norm_ref[2:3], upstream)
        dz1_ref[...] = dz1
        e1 = narrow(dz1)
        e1_ref[...] = e1
        do1_ref[...] = narrow(mm_nt(e1, read_out_ref[...])).astype(F32)

    own = pl.ds(pl.multiple_of(step * LAT, LAT), LAT)
    qx = expand(q1_ref[own, :])
    dox = expand(do1_ref[own, :])
    shares = p1_ref[...]
    dshares = mm_nt(dox, v1_ref[...])
    inner = jnp.sum(shares * dshares, axis=-1, keepdims=True)
    dscores = narrow(shares * (dshares - inner))
    size = k1_ref.shape[0]
    here = pl.ds(pl.multiple_of(step * size, size), size)
    dv1 = narrow(mm_tn(narrow(shares), dox))
    dk1 = narrow(mm_tn(dscores, qx) * FACTOR)
    dv1_ref[here, :] = dv1
    dk1_ref[here, :] = dk1
    dq1_ref[own, :] = collapse(mm(dscores, k1_ref[...])) * FACTOR

    @pl.when(step == last)
    def _():
        dq1 = narrow(dq1_ref[...])
        put_units(core_ref, other_ref, mine_ref,
                  [[(b1_ref, dk1_ref), (a1_ref, dq1), (a2_ref, dq2_ref), (o2_ref, e2_ref)],
                   [(b1_ref, dv1_ref), (o1_ref, e1_ref), (a2_ref, dk2_ref), (a2_ref, dv2_ref)]])


def input_back_kernel(
    x_ref, dx1_ref, dq3_ref, dk1_ref, dv1_ref, z_ref, dz1_ref, dq1_ref, norm_ref, in_ref, wq_ref,
    gain2_ref, shift2_ref, gain3_ref, shift3_ref, gain4_ref, shift4_ref,
    dx_ref, dz_ref, sums_ref, gain_ref, shift_ref,
):
    step = pl.program_id(0)

    def total(tensor):
        return jnp.sum(tensor, axis=0, keepdims=True)

    @pl.when(step == 0)
    def _():
        gain_ref[...] = jnp.zeros_like(gain_ref)
        shift_ref[...] = jnp.zeros_like(shift_ref)
        upstream = mm_nt(narrow(dq1_ref[...]), in_ref[0])
        unit, inverse = norm_parts(z_ref[...].astype(F32))
        sums_ref[...] = jnp.zeros_like(sums_ref)
        sums_ref[0:1] = total(upstream * unit)
        sums_ref[5:6] = total(upstream)
        for index, ref in enumerate((gain2_ref, gain3_ref, gain4_ref)):
            sums_ref[2 + index : 3 + index] = total(ref[...])
        for index, ref in enumerate((shift2_ref, shift3_ref, shift4_ref)):
            sums_ref[7 + index : 8 + index] = total(ref[...])
        dz_ref[...] = narrow(dz1_ref[...] + norm_back(unit, inverse, norm_ref[0:1], upstream))

    upstream = (
        mm_nt(dq3_ref[...], wq_ref[...])
        + mm_nt(dk1_ref[...], in_ref[1])
        + mm_nt(dv1_ref[...], in_ref[2])
    )
    unit, inverse = norm_parts(x_ref[...].astype(F32))
    gain_ref[...] += fold_rows(upstream * unit)
    shift_ref[...] += fold_rows(upstream)
    dx_ref[...] = narrow(dx1_ref[...] + norm_back(unit, inverse, norm_ref[1:2], upstream))

    @pl.when(step == pl.num_programs(0) - 1)
    def _():
        sums_ref[1:2] = total(gain_ref[...])
        sums_ref[6:7] = total(shift_ref[...])


def bits_of(count):
    bits = count.bit_length() - 1
    if 1 << bits != count:
        raise ValueError("axis size")
    return bits


def swap(tensor, axis, bit, count):
    return lax.ppermute(tensor, axis, [(i, i ^ (1 << bit)) for i in range(count)])


def own_bit(bit, axis="blk"):
    return (lax.axis_index(axis) >> bit) & 1


def gather_rows(tensor, count, line, fill):
    bits = bits_of(count)
    step = 0
    for bit in range(bits - 1, 1, -1):
        other = swap(line.gate(tensor), "blk", bit, count)
        beside = fill(step)
        line.note((other, beside) if beside is not None else other)
        tensor = jnp.stack([tensor, other], step)
        step += 1
    rows = tensor.shape[-2]
    left, right = tensor[..., : rows // 2, :], tensor[..., rows // 2 :, :]
    for bit_left, bit_right in ((1, 0), (0, 1)):
        got_left = swap(line.gate(left), "blk", bit_left, count)
        got_right = swap(line.gate(right), "blk", bit_right, count)
        beside = fill(step)
        line.note((got_left, got_right) + (() if beside is None else (beside,)))
        if bit_left == 1:
            left = jnp.stack([left, got_left], step)
            right = jnp.stack([right, got_right], step)
        step += 1
    return [piece.reshape(count // 2, -1, piece.shape[-1]) for piece in (left, got_left, right, got_right)]


def gather_places(count, groups):
    bits = bits_of(count)

    def spans(order):
        distances = [0]
        for bit in order:
            distances = [d | (on << bit) for d in distances for on in (0, 1)]
        return distances

    high = list(range(bits - 1, 1, -1))
    distance, place = [], []
    half = groups // 2
    for order, last, first in ((high + [1], 0, 0), (high + [0], 1, half)):
        for on in (0, 1):
            for d in spans(order):
                for group in range(first, first + half):
                    distance.append(d | (on << last))
                    place.append(group)
    return distance, place


def scatter_orders(bits):
    if bits < 3:
        return [list(range(bits))] * 3
    low, high = [0, 1], list(range(2, bits))
    return [
        low + high,
        [1] + high[:1] + [0] + high[1:],
        high[:1] + low + high[1:],
    ]


class Line:
    def __init__(self):
        self.last = None

    def gate(self, tensors):
        if self.last is None:
            return tensors
        tensors, _ = lax.optimization_barrier((tensors, self.last))
        return tensors

    def note(self, tensor):
        self.last = tensor


class Scatter:
    def __init__(self, line, count, orders):
        self.line, self.count, self.orders = line, count, orders
        self.left = [list(range(bits_of(count) - 1, -1, -1)) for _ in orders]
        self.step = 0

    def begin(self, parts):
        self.parts = parts
        self.send()

    def begin_cut(self, parts):
        self.parts = []
        for (sent, stay, rows), left, order in zip(parts, self.left, self.orders):
            bit = order[0]
            left.remove(bit)
            self.parts.append((stay, swap(self.line.gate(sent), "blk", bit, self.count), rows, 0))
        self.step += 1

    def send(self):
        if self.step == len(self.orders[0]) - 1 and len({order[-1] for order in self.orders}) == 1:
            self.send_last()
            return
        lead = (self.count >> self.step) // 2
        picks, in_specs, operands, out_specs, out_shape, bits = [], [], [], [], [], []
        for left, order in zip(self.left, self.orders):
            bits.append((order[self.step], left.index(order[self.step])))
            left.remove(order[self.step])
        for (kept, got, rows, block), (bit, place) in zip(self.parts, bits):
            inner = lead >> place
            picks.append(own_bit(bit))
            spec = pl.BlockSpec(
                (None, 2, None, rows, D),
                lambda i, inner=inner, block=block: (i // inner, 0, i % inner, block, 0),
            )
            in_specs += [spec, spec]
            kept, got = (t.reshape(lead // inner, 2, inner, -1, D) for t in (kept, got))
            operands += [in_hbm(kept), in_hbm(got)] if self.step == 0 else [kept, got]
            out_specs += [pl.BlockSpec((None, rows, D), lambda i: (i, 0, 0))] * 2
            out_shape += [shaped((lead, rows, D), BF)] * 2
        moved = sum(3 * 4 * lead * part[2] * D for part in self.parts)
        out = call(
            functools.partial(stage_kernel, len(self.parts)), (lead,),
            [pl.BlockSpec(memory_space=pltpu.SMEM)] + in_specs, out_specs, out_shape, 0, moved, vmem=10,
        )(*self.line.gate((jnp.stack(picks).astype(jnp.int32), *operands)))
        cut = [(sent, stay, part[2]) for sent, stay, part in zip(out[::2], out[1::2], self.parts)]
        self.line.note(out)
        self.parts = [
            (stay, swap(sent, "blk", bit, self.count), rows, 0)
            for (sent, stay, rows), (bit, _) in zip(cut, bits)
        ]
        self.step += 1

    def send_last(self):
        bit = self.orders[0][-1]
        rows = [part[2] for part in self.parts]
        operands = [t for kept, got, _, _ in self.parts for t in (kept, got)]
        shape = (sum(rows), D)
        send, stay = call(
            functools.partial(last_stage_kernel, len(rows)), (1,),
            [pl.BlockSpec(memory_space=pltpu.SMEM)] + [whole(t.shape) for t in operands], [whole(shape)] * 2,
            [shaped(shape, BF)] * 2, 0, 12 * shape[0] * D,
        )(*self.line.gate((own_bit(bit).reshape(1).astype(jnp.int32), *operands)))
        self.line.note(stay)
        self.parts = [(stay, swap(send, "blk", bit, self.count), shape[0], 0)]
        self.step += 1

    def flying(self):
        return [part[1] for part in self.parts]

    def result(self):
        ((stay, got, rows, _),) = self.parts
        return call(
            sum_kernel, (1,), [whole((rows, D))] * 2, whole((rows, D)), shaped((rows, D), BF), 0, 6 * rows * D,
        )(*self.line.gate((stay, got)))


def make_body(n_blk, n_rep):
    rep_bits = bits_of(n_rep)
    orders = scatter_orders(bits_of(n_blk))
    rows = D // n_blk

    def body(
        patches, latents, norm_gain, norm_bias, read_in, read_out, self_in, self_out,
        write_in, write_out, feed_up, feed_down, group_image, cot_patches, cot_latents,
    ):
        x, z, cot, cot_z = patches[0], latents[0], cot_patches[0], cot_latents[0]
        tokens, lat = x.shape[0], z.shape[0]
        groups = lat // LAT
        size = tokens // groups
        total = lat * n_blk
        hidden = feed_up.shape[1]
        feed_rows = hidden // n_blk
        core = lax.axis_index("rep") & 1
        core_at = core.reshape(1).astype(jnp.int32)
        other_at = 1 - core_at
        norms = jnp.concatenate([norm_gain, norm_bias, jnp.zeros((6, D), BF)], 0).astype(F32)
        norm_spec = whole((16, D))
        square = whole((D, D))
        three = whole((3, D, D))
        lat_spec = whole((lat, D))
        fold_spec = whole((8, D))
        patch_spec = rows_of((size, D))
        smem = pl.BlockSpec(memory_space=pltpu.SMEM)
        share_spec = pl.BlockSpec((None, HL, size), lambda g: (g, 0, 0))
        grid = (groups,)
        unit_flops = 2 * tokens * D * D
        low_lat, full_lat, fold = shaped((lat, D), BF), shaped((lat, D), F32), shaped((8, D), F32)
        low_patch = shaped((tokens, D), BF)
        line = Line()

        a1, q1, b1, k1, v1, p1, o1, z1, a2 = call(
            read_forward_kernel, grid,
            [patch_spec, lat_spec, norm_spec, three, square],
            [lat_spec, lat_spec, patch_spec, patch_spec, patch_spec, share_spec, lat_spec, lat_spec, lat_spec],
            [low_lat, full_lat, low_patch, low_patch, low_patch, shaped((groups, HL, size), F32),
             low_lat, full_lat, low_lat],
            2 * unit_flops, 12 * tokens * D,
            [pltpu.VMEM((lat, D), F32)],
        )(in_hbm(x), z, norms, in_hbm(read_in), in_hbm(read_out))

        q3 = []

        def fill_first(step):
            if step == 0:
                q3.append(narrow(mm(b1, write_in[0])))
                return q3[0]
            return None

        pieces = gather_rows(a2, n_blk, line, fill_first)
        q3 = q3[0]

        me = lax.axis_index("blk")
        distance, place = gather_places(n_blk, groups)
        places = (me ^ jnp.array(distance, jnp.int32)) * groups + jnp.array(place, jnp.int32)
        own_at = me * groups + jnp.arange(groups, dtype=jnp.int32)
        piece_shape = (n_blk // 2, lat // 2)
        hl2 = HEADS * lat
        a2_all, allowed, k2, v2, p2, l2, o2, z2, out_latents, b3, k3, v3 = call(
            self_forward_kernel, (1,),
            [smem] * 3 + [whole(piece_shape + (D,))] * 4 + [lat_spec, lat_spec, norm_spec, three, square,
             one_of(1), one_of(2)],
            [whole((total, D)), whole((hl2, total)), whole((total, D)), whole((total, D)), whole((hl2, total)),
             whole((hl2, 1))] + [lat_spec] * 6,
            [shaped((total, D), BF), shaped((hl2, total), F32), shaped((total, D), BF), shaped((total, D), BF),
             shaped((hl2, total), F32), shaped((hl2, 1), F32),
             low_lat, full_lat, low_lat, low_lat, full_lat, full_lat],
            unit_flops * 2, 10 * D * D * 2,
        )(group_image, places, own_at, *pieces, a2, z1, norms, self_in, self_out, write_in, write_in)

        resident = pl.BlockSpec(memory_space=pltpu.VMEM)
        pair_spec = pl.BlockSpec((2, size, D), lambda g: (0, g, 0))
        early_shape = (n_blk, 2 * rows, D)
        each = 1
        spans = rows_of((each * size, D))
        out_patches, h, gd, dq3, dx1, dk3, dv3, early_other, early_mine, gain4, shift4 = call(
            functools.partial(patch_kernel, D, size), (groups // each,),
            [smem] + [spans, spans, spans, lat_spec, lat_spec, norm_spec, square,
             resident, resident, whole((tokens, D)), lat_spec],
            [spans, spans,
             pl.BlockSpec((2, each * size, hidden), lambda g: (0, g, 0), pipeline_mode=pl.Buffered(1 if each > 1 else 2)),
             whole((tokens, D)), spans, lat_spec, lat_spec, whole(early_shape), whole(early_shape), fold_spec, fold_spec],
            [low_patch, low_patch, shaped((2, tokens, hidden), BF),
             low_patch, shaped((tokens, D), F32), full_lat, full_lat, shaped(early_shape, BF), shaped(early_shape, BF),
             fold, fold],
            unit_flops * 22, 40 * tokens * D, [pltpu.VMEM((tokens, D), BF)] * 2, vmem=46,
        )(core_at, in_hbm(x), in_hbm(q3), in_hbm(cot), k3, v3, norms, write_out, feed_up, feed_down, in_hbm(b1), b3)

        width = D + 128
        dz2, e2, payload, dq2, gain3, shift3 = call(
            latent_back_kernel, (1,),
            [lat_spec] * 4 + [whole((total, D))] * 2
            + [whole((hl2, total)), whole((hl2, 1)), norm_spec, one_of(1), one_of(2), square],
            [lat_spec] * 2 + [whole((lat, width)), lat_spec, fold_spec, fold_spec],
            [full_lat, low_lat, shaped((lat, width), BF), low_lat, fold, fold],
            unit_flops, 10 * D * D,
        )(dk3, dv3, z2, cot_z, k2, v2, p2, l2, norms, write_in, write_in, self_out)
        line.note(payload)

        feed_specs = [
            pl.BlockSpec((None, tokens, D), lambda j, w: (w[0], 0, j)),
            pl.BlockSpec((tokens, D), lambda j, w: (0, 0), pipeline_mode=pl.Buffered(1)),
            pl.BlockSpec((tokens, D), lambda j, w: (0, 0), pipeline_mode=pl.Buffered(1)),
        ]

        def feed_call(kernel, in_specs, out_specs, out_shape, operands):
            return pl.pallas_call(
                kernel,
                grid_spec=pltpu.PrefetchScalarGridSpec(
                    num_scalar_prefetch=1, grid=(hidden // D,), in_specs=in_specs, out_specs=out_specs
                ),
                out_shape=out_shape,
                compiler_params=pltpu.CompilerParams(
                    vmem_limit_bytes=24 << 20, dimension_semantics=("arbitrary",)
                ),
                cost_estimate=pl.CostEstimate(
                    flops=unit_flops * 4, bytes_accessed=20 * tokens * D, transcendentals=0
                ),
            )(*line.gate(operands))

        def once(shape):
            return pl.BlockSpec(shape, lambda j, w: (0,) * len(shape), pipeline_mode=pl.Buffered(1))

        gd, h, e4 = in_hbm(gd), in_hbm(h), in_hbm(cot)
        half = feed_rows // 2
        first = Scatter(line, n_blk, orders)
        firsts = (orders[0][0], orders[1][0])

        def feed_other():
            shape = (n_blk, feed_rows, D)
            return feed_call(feed_kernel, feed_specs, once(shape), shaped(shape, BF), (other_at, gd, h, e4))

        def feed_mine(got):
            which = jnp.stack([core, own_bit(firsts[0]), own_bit(firsts[1])]).astype(jnp.int32)
            near = D // feed_rows
            shape = (n_blk // 2, half, D)
            return feed_call(
                functools.partial(feed_sum_kernel, firsts),
                feed_specs
                + [pl.BlockSpec((n_blk, rows, D), lambda j, w: (0, j, 0)),
                   pl.BlockSpec((near, feed_rows, D), lambda j, w: (j, 0, 0))],
                [once(shape)] * 4, [shaped(shape, BF)] * 4, (which, gd, h, e4, got, got),
            )

        whole_patch = whole((tokens, D))

        def core_swap(tensor):
            return swap(line.gate(tensor), "rep", 0, n_rep)

        early = {}

        def fill_second(step):
            if step == 0:
                early["got"] = core_swap(early_other)
                early["feed_other"] = feed_other()
                return early["feed_other"], early["got"]
            if step == 1:
                early["feed_got"] = core_swap(early["feed_other"])
                bit = orders[2][0]
                shape = (n_blk // 2, 2 * rows, D)
                early["sum"] = call(
                    functools.partial(cut_kernel, bit), (1,), [smem] + [whole(early_shape)] * 2,
                    [whole(shape)] * 2, [shaped(shape, BF)] * 2, 0, 12 * tokens * D,
                )(*line.gate((own_bit(bit).reshape(1).astype(jnp.int32), early_mine, early["got"])))
                return early["sum"], early["feed_got"]
            if step == 2:
                early["feed"] = feed_mine(early["feed_got"])
                return early["feed"]
            return None

        spread_pieces = gather_rows(payload, n_blk, line, fill_second)
        feed0, feed1, feed2, feed3 = early["feed"]
        first.begin_cut([(feed0, feed1, half), (feed2, feed3, half), (*early["sum"], 2 * rows)])

        late_shape = (n_blk, 4 * rows, D)
        late_other, late_mine, dk1, dv1, dq1, dz1, gain2, shift2 = call(
            tail_kernel, grid,
            [smem] + [whole(piece_shape + (width,))] * 4
            + [whole((total, D)), whole((hl2, total)), whole((total, D)), whole((total, D))] + [lat_spec] * 3
            + [norm_spec, three, square, lat_spec, share_spec, patch_spec, patch_spec, whole_patch] + [lat_spec] * 5,
            [whole(late_shape)] * 2 + [whole_patch] * 2 + [lat_spec] * 2 + [fold_spec] * 2,
            [shaped(late_shape, BF), shaped(late_shape, BF), low_patch, low_patch, full_lat, full_lat, fold, fold],
            4 * unit_flops, 30 * tokens * D,
            [pltpu.VMEM((lat, D), F32)] + [pltpu.VMEM((lat, D), BF)] * 3,
            vmem=40,
        )(*line.gate((core_at, *spread_pieces, a2_all, allowed, k2, v2, dq2, z1, dz2, norms, self_in, read_out,
                      q1, in_hbm(p1), in_hbm(k1), in_hbm(v1), b1, a1, o1, a2, o2, e2)))
        line.note((late_other, first.flying()))
        late_got = core_swap(late_other)
        first.send()
        dx, dz, norm_grads = call(
            input_back_kernel, grid,
            [patch_spec] * 5 + [lat_spec] * 3 + [norm_spec, three, one_of(0)] + [fold_spec] * 6,
            [patch_spec, lat_spec, norm_spec],
            [low_patch, low_lat, shaped((16, D), F32)],
            unit_flops * 3, 14 * tokens * D,
            [pltpu.VMEM((8, D), F32)] * 2,
        )(*line.gate((in_hbm(x), in_hbm(dx1), in_hbm(dq3), dk1, dv1, z, dz1, dq1, norms, read_in, write_in,
                      gain2, shift2, gain3, shift3, gain4, shift4)))
        line.note((dx, late_got, first.flying()))
        first.send()
        norm_got = swap(line.gate(norm_grads), "rep", 0, n_rep)
        line.note((norm_got, first.flying()))
        norm_grads = norm_grads + norm_got
        first.send()
        last = Scatter(line, n_blk, orders)
        last_rows = 4 * rows // 3
        last.begin([(late_mine, late_got, last_rows, i) for i in range(3)])
        for bit in range(1, rep_bits):
            norm_grads = norm_grads + swap(line.gate(norm_grads), "rep", bit, n_rep)
        bits = bits_of(n_blk)

        def finish(flat):
            for bit in range(1, rep_bits):
                flat = narrow(flat.astype(F32) + swap(flat, "rep", bit, n_rep).astype(F32))
            return flat, swap(flat, "rep", 0, n_rep)

        def outputs(kernel, flat, partner, shapes):
            return call(
                kernel, (1,), [smem, whole(flat.shape), whole(flat.shape)], [whole(t) for t in shapes],
                [shaped(t, F32) for t in shapes], 0, 12 * flat.shape[0] * D,
            )(*line.gate((core_at, flat, partner)))

        for step in range(bits):
            got = swap(line.gate(norm_grads), "blk", step, n_blk)
            if step == 0:
                line.note((last.flying(), first.flying(), got))
            elif step == 1:
                last.send()
                while first.step < bits:
                    line.note(first.flying())
                    first.send()
                flat, partner = finish(first.result())
                up, down, wo, write_in_grad = outputs(
                    early_out_kernel, flat, partner, [(rows, hidden), (feed_rows, D), (rows, D), (3, rows, D)]
                )
                line.note((last.flying(), got, up))
            else:
                if last.step < bits:
                    last.send()
                line.note((last.flying(), got))
            norm_grads = norm_grads + got
        while last.step < bits:
            last.send()
            line.note(last.flying())
        flat, partner = finish(last.result())
        read_in_grad, read_out_grad, self_in_grad, self_out_grad = outputs(
            late_out_kernel, flat, partner, [(3, rows, D), (rows, D), (3, rows, D), (rows, D)]
        )
        norm_own = lax.dynamic_slice_in_dim(norm_grads, lax.axis_index("blk") * rows, rows, 1)
        return (
            out_patches[None], out_latents[None], dx[None], dz[None], norm_own[:5], norm_own[5:10],
            read_in_grad, read_out_grad, self_in_grad, self_out_grad, write_in_grad, wo, up, down,
        )

    return body


def solution(mesh):
    return jax.shard_map(
        make_body(mesh.shape["blk"], mesh.shape["rep"]),
        mesh=mesh,
        in_specs=(
            P("rep", "blk", None), P("rep", "blk", None), P(), P(), P(), P(), P(), P(), P(), P(), P(), P(),
            P("rep", None), P("rep", "blk", None), P("rep", "blk", None),
        ),
        out_specs=(
            P("rep", "blk", None), P("rep", "blk", None), P("rep", "blk", None), P("rep", "blk", None),
            P(None, "blk"), P(None, "blk"), P(None, "blk", None), P("blk", None), P(None, "blk", None),
            P("blk", None), P(None, "blk", None), P("blk", None), P("blk", None), P("blk", None),
        ),
        check_vma=False,
    )
```

```python
import functools

import jax
import jax.numpy as jnp
from jax import lax
from jax.experimental import pallas as pl
from jax.experimental.pallas import tpu as pltpu
from jax.sharding import PartitionSpec as P

D = 768
HEADS = 12
HEAD = 64
LAT = 8
FACTOR = HEAD ** (-0.5)
HL = HEADS * LAT
LANES = 768
BF = jnp.bfloat16
F32 = jnp.float32


def narrow(tensor):
    return tensor.astype(BF)


def mm(left, right):
    return lax.dot_general(left, right, (((1,), (0,)), ((), ())), preferred_element_type=F32)


def mm_tn(left, right):
    return lax.dot_general(left, right, (((0,), (0,)), ((), ())), preferred_element_type=F32)


def mm_nt(left, right):
    return lax.dot_general(left, right, (((1,), (1,)), ((), ())), preferred_element_type=F32)


def norm_parts(tensor):
    center = tensor - jnp.mean(tensor, axis=-1, keepdims=True)
    spread = jnp.mean(center * center, axis=-1, keepdims=True)
    inverse = lax.rsqrt(spread + 1e-06)
    return center * inverse, inverse


def norm_forward(tensor, gain, shift):
    unit, _ = norm_parts(tensor)
    return unit * gain + shift


def norm_back(unit, inverse, gain, upstream):
    scaled = upstream * gain
    return inverse * (
        scaled
        - jnp.mean(scaled, axis=-1, keepdims=True)
        - unit * jnp.mean(scaled * unit, axis=-1, keepdims=True)
    )


def fold_rows(tensor):
    rows, cols = tensor.shape
    return jnp.sum(tensor.reshape(rows // 8, 8, cols), axis=0)


def head_mask():
    head = lax.broadcasted_iota(jnp.int32, (HEADS, 1, D), 0)
    feature = lax.broadcasted_iota(jnp.int32, (HEADS, 1, D), 2)
    return (feature >= head * HEAD) & (feature < head * HEAD + HEAD)


def expand(rows):
    count = rows.shape[0]
    return narrow(jnp.where(head_mask(), rows[None], 0.0).reshape(HEADS * count, D))


def collapse(rows):
    count = rows.shape[0] // HEADS
    return jnp.sum(jnp.where(head_mask(), rows.reshape(HEADS, count, D), 0.0), axis=0)


def whole(shape):
    return pl.BlockSpec(shape, lambda *_: (0,) * len(shape), pipeline_mode=pl.Buffered(1))


def rows_of(shape):
    return pl.BlockSpec(shape, lambda g: (g,) + (0,) * (len(shape) - 1))


def one_of(index):
    return pl.BlockSpec(
        (None, D, D), lambda *_: (index, 0, 0), pipeline_mode=pl.Buffered(1)
    )


def shaped(shape, dtype):
    return jax.ShapeDtypeStruct(shape, dtype)


def in_hbm(tensor):
    return pltpu.with_memory_space_constraint(tensor, pltpu.HBM)


def image_marks(image_ref, places_ref, shape, axis, rows):
    index = lax.broadcasted_iota(jnp.int32, shape, axis)
    marks = jnp.zeros(shape, jnp.int32)
    for group in range(shape[axis] // rows):
        inside = (index >= group * rows) & (index < (group + 1) * rows)
        marks = jnp.where(inside, image_ref[0, places_ref[group]], marks)
    return marks


def gathered(refs):
    pieces = [ref[...] for ref in refs]
    return jnp.concatenate([piece.reshape(-1, piece.shape[-1]) for piece in pieces], 0)


def call(body, grid, in_specs, out_specs, out_shape, flops, moved, scratch=(), vmem=20):
    return pl.pallas_call(
        body,
        grid=grid,
        in_specs=in_specs,
        out_specs=out_specs,
        out_shape=out_shape,
        scratch_shapes=scratch,
        compiler_params=pltpu.CompilerParams(
            vmem_limit_bytes=vmem << 20, dimension_semantics=("arbitrary",) * len(grid)
        ),
        cost_estimate=pl.CostEstimate(
            flops=int(flops), bytes_accessed=int(moved), transcendentals=0
        ),
    )


def read_forward_kernel(
    x_ref, z_ref, norm_ref, in_ref, out_w_ref,
    a1_ref, q1_ref, b1_ref, k1_ref, v1_ref, p1_ref, o1_ref, z1_ref, a2_ref,
    mix_ref,
):
    step = pl.program_id(0)
    last = pl.num_programs(0) - 1

    @pl.when(step == 0)
    def _():
        a1 = narrow(norm_forward(z_ref[...].astype(F32), norm_ref[0:1], norm_ref[5:6]))
        a1_ref[...] = a1
        q1_ref[...] = narrow(mm(a1, in_ref[0])).astype(F32)

    b1 = narrow(norm_forward(x_ref[...].astype(F32), norm_ref[1:2], norm_ref[6:7]))
    b1_ref[...] = b1
    k1 = narrow(mm(b1, in_ref[1]))
    v1 = narrow(mm(b1, in_ref[2]))
    k1_ref[...] = k1
    v1_ref[...] = v1
    own = pl.ds(pl.multiple_of(step * LAT, LAT), LAT)
    scores = mm_nt(expand(q1_ref[own, :]), k1) * FACTOR
    powers = jnp.exp(scores - jnp.max(scores, axis=-1, keepdims=True))
    shares = powers / jnp.sum(powers, axis=-1, keepdims=True)
    p1_ref[...] = shares
    mix_ref[own, :] = collapse(mm(narrow(shares), v1))

    @pl.when(step == last)
    def _():
        o1 = narrow(mix_ref[...])
        o1_ref[...] = o1
        z1 = z_ref[...].astype(F32) + mm(o1, out_w_ref[...])
        z1_ref[...] = z1
        a2_ref[...] = narrow(norm_forward(z1, norm_ref[2:3], norm_ref[7:8]))


def self_forward_kernel(
    image_ref, places_ref, own_at_ref, piece0_ref, piece1_ref, piece2_ref, piece3_ref,
    a2_ref, z1_ref, norm_ref, in_ref, out_w_ref, wk_ref, wv_ref,
    all_ref, allowed_ref, k2_ref, v2_ref, p2_ref, l2_ref, o2_ref, z2_ref, out_ref, b3_ref, k3_ref, v3_ref,
):
    everyone = gathered((piece0_ref, piece1_ref, piece2_ref, piece3_ref))
    all_ref[...] = everyone
    k2 = narrow(mm(everyone, in_ref[1]))
    v2 = narrow(mm(everyone, in_ref[2]))
    k2_ref[...] = k2
    v2_ref[...] = v2
    q2 = narrow(mm(a2_ref[...], in_ref[0])).astype(F32)
    scores = mm_nt(expand(q2), k2) * FACTOR
    total, count = everyone.shape[0], q2.shape[0]
    owners = image_marks(image_ref, places_ref, (1, total), 1, LAT)
    own = jnp.concatenate([image_marks(image_ref, own_at_ref, (count, 1), 0, LAT)] * HEADS, 0)
    allowed = own == owners
    allowed_ref[...] = jnp.where(allowed, 1.0, 0.0)
    scores = jnp.where(allowed, scores, -1e30)
    highest = jnp.max(scores, axis=-1, keepdims=True)
    powers = jnp.exp(scores - highest)
    totals = jnp.sum(powers, axis=-1, keepdims=True)
    shares = powers / totals
    p2_ref[...] = shares
    l2_ref[...] = highest + jnp.log(totals)
    o2 = narrow(collapse(mm(narrow(shares), v2)))
    o2_ref[...] = o2
    z2 = z1_ref[...] + mm(o2, out_w_ref[...])
    z2_ref[...] = z2
    out_ref[...] = narrow(z2)
    b3 = narrow(norm_forward(z2, norm_ref[3:4], norm_ref[8:9]))
    b3_ref[...] = b3
    k3_ref[...] = narrow(mm(b3, wk_ref[...])).astype(F32)
    v3_ref[...] = narrow(mm(b3, wv_ref[...])).astype(F32)


ROOT_HALF = 0.7071067811865476
DENSITY = 0.3989422804014327


def patch_kernel(
    chunk, size, core_ref, x_ref, q3_ref, cot_ref, k3_ref, v3_ref, norm_ref, wo_ref, up_ref, down_ref, b1_ref, b3_ref,
    out_ref, h_ref, gd_ref, dq3_ref, dx1_ref, dk3_ref, dv3_ref, other_ref, mine_ref,
    gain_ref, shift_ref, o3_ref, e3_ref,
):
    step = pl.program_id(0)
    tokens = x_ref.shape[0]
    each = tokens // size
    here = pl.ds(pl.multiple_of(step * tokens, tokens), tokens)
    keys, values, weights = [], [], []
    for index in range(each):
        own = pl.ds(pl.multiple_of((step * each + index) * LAT, LAT), LAT)
        kx, vx = expand(k3_ref[own, :]), expand(v3_ref[own, :])
        rows = slice(index * size, (index + 1) * size)
        scores = (mm_nt(kx, q3_ref[rows]) * FACTOR).reshape(HEADS, LAT, size)
        powers = jnp.exp(scores - jnp.max(scores, axis=1, keepdims=True))
        shares = powers / jnp.sum(powers, axis=1, keepdims=True)
        keys.append(kx)
        values.append(vx)
        weights.append(shares)
    mixed = [narrow(mm_tn(narrow(w.reshape(HL, size)), v)) for w, v in zip(weights, values)]
    o3 = jnp.concatenate(mixed, 0) if each > 1 else mixed[0]
    o3_ref[here, :] = o3
    x1 = x_ref[...].astype(F32) + mm(o3, wo_ref[...])
    unit, inverse = norm_parts(x1)
    gain = norm_ref[4:5]
    h = narrow(unit * gain + norm_ref[9:10])
    h_ref[...] = h
    e4 = cot_ref[...]
    x2 = x1
    dh = jnp.zeros((tokens, D), F32)
    hidden = up_ref.shape[1]
    for start in range(0, hidden, chunk):
        part = slice(start, start + chunk)
        u = mm(h, up_ref[:, part])
        cdf = 0.5 + 0.5 * lax.erf(u * ROOT_HALF)
        g = narrow(u * cdf)
        gd_ref[1, :, part] = g
        x2 = x2 + mm(g, down_ref[part, :])
        slope = cdf + u * (jnp.exp(-0.5 * u * u) * DENSITY)
        du = narrow(mm_nt(e4, down_ref[part, :]) * slope)
        gd_ref[0, :, part] = du
        dh = dh + mm_nt(du, up_ref[:, part])
    out_ref[...] = narrow(x2)

    @pl.when(step == 0)
    def _():
        gain_ref[...] = jnp.zeros_like(gain_ref)
        shift_ref[...] = jnp.zeros_like(shift_ref)

    gain_ref[...] += fold_rows(dh * unit)
    shift_ref[...] += fold_rows(dh)
    dx1 = e4.astype(F32) + norm_back(unit, inverse, gain, dh)
    dx1_ref[...] = dx1
    e3 = narrow(dx1)
    e3_ref[here, :] = e3
    do3 = narrow(mm_nt(e3, wo_ref[...]))
    for index in range(each):
        own = pl.ds(pl.multiple_of((step * each + index) * LAT, LAT), LAT)
        place = pl.ds(pl.multiple_of((step * each + index) * size, size), size)
        rows = slice(index * size, (index + 1) * size)
        kx, vx, shares = keys[index], values[index], weights[index]
        grad = do3[rows]
        dshares = mm_nt(vx, grad).reshape(HEADS, LAT, size)
        inner = jnp.sum(shares * dshares, axis=1, keepdims=True)
        dscores = narrow((shares * (dshares - inner)).reshape(HL, size))
        dq3_ref[place, :] = narrow(mm_tn(dscores, kx) * FACTOR)
        dv3_ref[own, :] = narrow(collapse(mm(narrow(shares.reshape(HL, size)), grad))).astype(F32)
        dk3_ref[own, :] = narrow(collapse(mm(dscores, q3_ref[rows])) * FACTOR).astype(F32)

    @pl.when(step == pl.num_programs(0) - 1)
    def _():
        b3 = b3_ref[...]
        put_units(core_ref, other_ref, mine_ref,
                  [[(o3_ref, e3_ref), (b3, narrow(dk3_ref[...]))], [(b1_ref, dq3_ref), (b3, narrow(dv3_ref[...]))]])


STAT = 2 * HEADS


def latent_back_kernel(
    dk3_ref, dv3_ref, z2_ref, cot_ref, k2_ref, v2_ref, p2_ref, l2_ref, norm_ref, wk_ref, wv_ref, out_w_ref,
    dz2_ref, e2_ref, send_ref, dq2_ref, gain_ref, shift_ref,
):
    dk3 = narrow(dk3_ref[...])
    dv3 = narrow(dv3_ref[...])
    upstream = mm_nt(dk3, wk_ref[...]) + mm_nt(dv3, wv_ref[...])
    unit, inverse = norm_parts(z2_ref[...])
    gain_ref[...] = fold_rows(upstream * unit)
    shift_ref[...] = fold_rows(upstream)
    dz2 = cot_ref[...].astype(F32) + norm_back(unit, inverse, norm_ref[3:4], upstream)
    dz2_ref[...] = dz2
    e2 = narrow(dz2)
    e2_ref[...] = e2
    do2 = narrow(mm_nt(e2, out_w_ref[...]))
    send_ref[:, :D] = do2
    shares = p2_ref[...]
    dshares = mm_nt(expand(do2.astype(F32)), v2_ref[...])
    inner = jnp.sum(shares * dshares, axis=-1, keepdims=True)
    count = do2.shape[0]
    lane = lax.broadcasted_iota(jnp.int32, (count, 128), 1)
    stats = jnp.zeros((count, 128), F32)
    for slot, columns in ((0, l2_ref[...]), (HEADS, inner)):
        for head in range(HEADS):
            place = slot + head
            chosen = (lane == place) | (lane == place + STAT) | (lane == place + 2 * STAT)
            stats = jnp.where(chosen, columns[head * count : (head + 1) * count], stats)
    top = narrow(stats)
    rest = stats - top.astype(F32)
    middle = narrow(rest)
    bottom = narrow(rest - middle.astype(F32))
    send_ref[:, D:] = narrow(
        jnp.where(lane < STAT, top.astype(F32), jnp.where(lane < 2 * STAT, middle.astype(F32), bottom.astype(F32)))
    )
    dscores = narrow(shares * (dshares - inner))
    dq2_ref[...] = narrow(collapse(mm(dscores, k2_ref[...])) * FACTOR)


def spread_stat(stats, slot, count):
    shape = (HEADS * count, 128)
    place = lax.broadcasted_iota(jnp.int32, shape, 1)
    column = lax.broadcasted_iota(jnp.int32, shape, 0)
    chosen = jnp.zeros(shape, jnp.bool_)
    for term in range(3):
        head = place - (slot + term * STAT)
        chosen |= (head >= 0) & (head < HEADS) & (column >= head * count) & (column < (head + 1) * count)
    return mm_nt(narrow(jnp.where(chosen, 1.0, 0.0)), stats)


def unit_grad(left, right, count):
    return mm_tn(left[...], right[...]).reshape(count, D // count, D)


def put_units(core_ref, other_ref, mine_ref, units):
    count = mine_ref.shape[0]
    rows = D // count
    for core in range(2):
        @pl.when(core_ref[0] == core)
        def _():
            for ref, pairs in ((other_ref, units[1 - core]), (mine_ref, units[core])):
                for index, (left, right) in enumerate(pairs):
                    ref[:, index * rows : (index + 1) * rows, :] = narrow(unit_grad(left, right, count))


def cut_kernel(bit, pick_ref, keep_ref, got_ref, send_ref, stay_ref):
    zero, one = halves(keep_ref[...].astype(F32) + got_ref[...].astype(F32), bit)
    mine = pick_ref[0] == 0
    send_ref[...] = narrow(jnp.where(mine, one, zero))
    stay_ref[...] = narrow(jnp.where(mine, zero, one))


def stage_kernel(parts, pick_ref, *refs):
    for index in range(parts):
        keep_ref, got_ref = refs[2 * index : 2 * index + 2]
        send_ref, stay_ref = refs[2 * parts + 2 * index : 2 * parts + 2 * index + 2]
        mine = pick_ref[index]
        send_ref[...] = narrow(keep_ref[1 - mine].astype(F32) + got_ref[1 - mine].astype(F32))
        stay_ref[...] = narrow(keep_ref[mine].astype(F32) + got_ref[mine].astype(F32))


def last_stage_kernel(parts, pick_ref, *refs):
    send_ref, stay_ref = refs[2 * parts :]
    mine = pick_ref[0]
    start = 0
    for index in range(parts):
        keep_ref, got_ref = refs[2 * index : 2 * index + 2]
        rows = keep_ref.shape[1]
        span = slice(start, start + rows)
        send_ref[span] = narrow(keep_ref[1 - mine].astype(F32) + got_ref[1 - mine].astype(F32))
        stay_ref[span] = narrow(keep_ref[mine].astype(F32) + got_ref[mine].astype(F32))
        start += rows


def sum_kernel(keep_ref, got_ref, out_ref):
    out_ref[...] = narrow(keep_ref[...].astype(F32) + got_ref[...].astype(F32))


def early_out_kernel(core_ref, mine_ref, partner_ref, up_ref, down_ref, wo_ref, in_ref):
    rows = wo_ref.shape[0]
    feed_rows = down_ref.shape[0]
    for core in range(2):
        @pl.when(core_ref[0] == core)
        def _():
            zero, one = (mine_ref, partner_ref) if core == 0 else (partner_ref, mine_ref)
            for index in range(feed_rows // rows):
                up_ref[:, index * D : (index + 1) * D] = zero[index * rows : (index + 1) * rows].astype(F32)
            down_ref[...] = one[:feed_rows].astype(F32)
            wo_ref[...] = zero[feed_rows : feed_rows + rows].astype(F32)
            in_ref[0] = one[feed_rows : feed_rows + rows].astype(F32)
            in_ref[1] = zero[feed_rows + rows :].astype(F32)
            in_ref[2] = one[feed_rows + rows :].astype(F32)


def late_out_kernel(core_ref, mine_ref, partner_ref, read_in_ref, read_out_ref, self_in_ref, self_out_ref):
    rows = read_out_ref.shape[0]
    for core in range(2):
        @pl.when(core_ref[0] == core)
        def _():
            zero, one = (mine_ref, partner_ref) if core == 0 else (partner_ref, mine_ref)

            def unit(ref, index):
                return ref[index * rows : (index + 1) * rows].astype(F32)

            read_in_ref[0] = unit(zero, 1)
            read_in_ref[1] = unit(zero, 0)
            read_in_ref[2] = unit(one, 0)
            read_out_ref[...] = unit(one, 1)
            self_in_ref[0] = unit(zero, 2)
            self_in_ref[1] = unit(one, 2)
            self_in_ref[2] = unit(one, 3)
            self_out_ref[...] = unit(zero, 3)


def lane_spans():
    return [slice(start, start + LANES) for start in range(0, D, LANES)]


def feed_kernel(which_ref, gd_ref, h_ref, e4_ref, out_ref):
    part = pl.program_id(0)
    count, rows, _ = out_ref.shape
    slab = D // count
    near = D // rows

    @pl.when(which_ref[0] == 0)
    def _():
        for lanes in lane_spans():
            grad = narrow(mm_tn(h_ref[...], gd_ref[:, lanes]).reshape(count, slab, LANES))
            out_ref[:, pl.ds(pl.multiple_of(part * slab, 8), slab), lanes] = grad

    @pl.when(which_ref[0] == 1)
    def _():
        for lanes in lane_spans():
            grad = narrow(mm_tn(gd_ref[...], e4_ref[:, lanes]).reshape(near, rows, LANES))
            out_ref[pl.ds(part * near, near), :, lanes] = grad


def halves(tensor, bit):
    count, rows, cols = tensor.shape
    cut = tensor.reshape(count >> (bit + 1), 2, 1 << bit, rows, cols)
    return cut[:, 0].reshape(count // 2, rows, cols), cut[:, 1].reshape(count // 2, rows, cols)


def feed_sum_kernel(
    bits, which_ref, gd_ref, h_ref, e4_ref, got_up_ref, got_down_ref, send0_ref, stay0_ref, send1_ref, stay1_ref
):
    part = pl.program_id(0)
    count, slab, _ = got_up_ref.shape
    near, rows, _ = got_down_ref.shape
    half = rows // 2
    per_part = half // slab

    def store(index, place, value):
        zero, one = halves(value, bits[index])
        mine = which_ref[1 + index] == 0
        send, stay = ((send0_ref, stay0_ref), (send1_ref, stay1_ref))[index]
        send[place] = narrow(jnp.where(mine, one, zero))
        stay[place] = narrow(jnp.where(mine, zero, one))

    for index in range(2):
        @pl.when((which_ref[0] == 0) & (part // per_part == index))
        def _():
            rows_at = pl.ds(pl.multiple_of(lax.rem(part, per_part) * slab, 8), slab)
            for lanes in lane_spans():
                grad = mm_tn(h_ref[...], gd_ref[:, lanes]).reshape(count, slab, LANES)
                store(index, (slice(None), rows_at, lanes), grad + got_up_ref[:, :, lanes].astype(F32))

    @pl.when(which_ref[0] == 1)
    def _():
        place = pl.ds(part * (near // 2), near // 2)
        for lanes in lane_spans():
            grad = mm_tn(gd_ref[...], e4_ref[:, lanes]).reshape(near, rows, LANES)
            grad = grad + got_down_ref[:, :, lanes].astype(F32)
            for index in range(2):
                store(index, (place, slice(None), lanes), grad[:, index * half : (index + 1) * half])


def tail_kernel(
    core_ref, piece0_ref, piece1_ref, piece2_ref, piece3_ref, everyone_ref, allowed_ref, k2_ref, v2_ref,
    dq2_ref, z1_ref, dz2_ref, norm_ref, self_in_ref, read_out_ref, q1_ref, p1_ref, k1_ref, v1_ref,
    b1_ref, a1_ref, o1_ref, a2_ref, o2_ref, e2_ref,
    other_ref, mine_ref, dk1_ref, dv1_ref, dq1_ref, dz1_ref, gain_ref, shift_ref,
    do1_ref, e1_ref, dk2_ref, dv2_ref,
):
    step = pl.program_id(0)
    last = pl.num_programs(0) - 1

    @pl.when(step == 0)
    def _():
        count = dq2_ref.shape[0]
        half, everything = count // 2, everyone_ref.shape[0]

        def own_rows(ref):
            return jnp.concatenate([ref[:half], ref[everything // 2 : everything // 2 + half]], 0).astype(F32)

        q_all = narrow(mm(everyone_ref[...], self_in_ref[0]))
        spread = gathered((piece0_ref, piece1_ref, piece2_ref, piece3_ref))
        do_all = spread[:, :D]
        stats = spread[:, D:]
        scores = mm_nt(expand(own_rows(k2_ref)), q_all) * FACTOR
        allowed = allowed_ref[...] > 0.5
        log_total = spread_stat(stats, 0, count)
        shares = jnp.where(allowed, jnp.exp(jnp.where(allowed, scores - log_total, 0.0)), 0.0)
        dv2 = narrow(collapse(mm(narrow(shares), do_all)))
        dshares = mm_nt(expand(own_rows(v2_ref)), do_all)
        dscores = narrow(shares * (dshares - spread_stat(stats, HEADS, count)))
        dk2 = narrow(collapse(mm(dscores, q_all)) * FACTOR)
        dk2_ref[...] = dk2
        dv2_ref[...] = dv2
        upstream = (
            mm_nt(dq2_ref[...], self_in_ref[0]) + mm_nt(dk2, self_in_ref[1]) + mm_nt(dv2, self_in_ref[2])
        )
        unit, inverse = norm_parts(z1_ref[...])
        gain_ref[...] = fold_rows(upstream * unit)
        shift_ref[...] = fold_rows(upstream)
        dz1 = dz2_ref[...] + norm_back(unit, inverse, norm_ref[2:3], upstream)
        dz1_ref[...] = dz1
        e1 = narrow(dz1)
        e1_ref[...] = e1
        do1_ref[...] = narrow(mm_nt(e1, read_out_ref[...])).astype(F32)

    own = pl.ds(pl.multiple_of(step * LAT, LAT), LAT)
    qx = expand(q1_ref[own, :])
    dox = expand(do1_ref[own, :])
    shares = p1_ref[...]
    dshares = mm_nt(dox, v1_ref[...])
    inner = jnp.sum(shares * dshares, axis=-1, keepdims=True)
    dscores = narrow(shares * (dshares - inner))
    size = k1_ref.shape[0]
    here = pl.ds(pl.multiple_of(step * size, size), size)
    dv1 = narrow(mm_tn(narrow(shares), dox))
    dk1 = narrow(mm_tn(dscores, qx) * FACTOR)
    dv1_ref[here, :] = dv1
    dk1_ref[here, :] = dk1
    dq1_ref[own, :] = collapse(mm(dscores, k1_ref[...])) * FACTOR

    @pl.when(step == last)
    def _():
        dq1 = narrow(dq1_ref[...])
        put_units(core_ref, other_ref, mine_ref,
                  [[(b1_ref, dk1_ref), (a1_ref, dq1), (a2_ref, dq2_ref), (o2_ref, e2_ref)],
                   [(b1_ref, dv1_ref), (o1_ref, e1_ref), (a2_ref, dk2_ref), (a2_ref, dv2_ref)]])


def input_back_kernel(
    x_ref, dx1_ref, dq3_ref, dk1_ref, dv1_ref, z_ref, dz1_ref, dq1_ref, norm_ref, in_ref, wq_ref,
    gain2_ref, shift2_ref, gain3_ref, shift3_ref, gain4_ref, shift4_ref,
    dx_ref, dz_ref, sums_ref, gain_ref, shift_ref,
):
    step = pl.program_id(0)

    def total(tensor):
        return jnp.sum(tensor, axis=0, keepdims=True)

    @pl.when(step == 0)
    def _():
        gain_ref[...] = jnp.zeros_like(gain_ref)
        shift_ref[...] = jnp.zeros_like(shift_ref)
        upstream = mm_nt(narrow(dq1_ref[...]), in_ref[0])
        unit, inverse = norm_parts(z_ref[...].astype(F32))
        sums_ref[...] = jnp.zeros_like(sums_ref)
        sums_ref[0:1] = total(upstream * unit)
        sums_ref[5:6] = total(upstream)
        for index, ref in enumerate((gain2_ref, gain3_ref, gain4_ref)):
            sums_ref[2 + index : 3 + index] = total(ref[...])
        for index, ref in enumerate((shift2_ref, shift3_ref, shift4_ref)):
            sums_ref[7 + index : 8 + index] = total(ref[...])
        dz_ref[...] = narrow(dz1_ref[...] + norm_back(unit, inverse, norm_ref[0:1], upstream))

    upstream = (
        mm_nt(dq3_ref[...], wq_ref[...])
        + mm_nt(dk1_ref[...], in_ref[1])
        + mm_nt(dv1_ref[...], in_ref[2])
    )
    unit, inverse = norm_parts(x_ref[...].astype(F32))
    gain_ref[...] += fold_rows(upstream * unit)
    shift_ref[...] += fold_rows(upstream)
    dx_ref[...] = narrow(dx1_ref[...] + norm_back(unit, inverse, norm_ref[1:2], upstream))

    @pl.when(step == pl.num_programs(0) - 1)
    def _():
        sums_ref[1:2] = total(gain_ref[...])
        sums_ref[6:7] = total(shift_ref[...])


def bits_of(count):
    bits = count.bit_length() - 1
    if 1 << bits != count:
        raise ValueError("axis size")
    return bits


def swap(tensor, axis, bit, count):
    return lax.ppermute(tensor, axis, [(i, i ^ (1 << bit)) for i in range(count)])


def own_bit(bit, axis="blk"):
    return (lax.axis_index(axis) >> bit) & 1


def gather_rows(tensor, count, line, fill):
    bits = bits_of(count)
    step = 0
    for bit in range(bits - 1, 1, -1):
        other = swap(line.gate(tensor), "blk", bit, count)
        beside = fill(step)
        line.note((other, beside) if beside is not None else other)
        tensor = jnp.stack([tensor, other], step)
        step += 1
    rows = tensor.shape[-2]
    left, right = tensor[..., : rows // 2, :], tensor[..., rows // 2 :, :]
    for bit_left, bit_right in ((1, 0), (0, 1)):
        got_left = swap(line.gate(left), "blk", bit_left, count)
        got_right = swap(line.gate(right), "blk", bit_right, count)
        beside = fill(step)
        line.note((got_left, got_right) + (() if beside is None else (beside,)))
        if bit_left == 1:
            left = jnp.stack([left, got_left], step)
            right = jnp.stack([right, got_right], step)
        step += 1
    return [piece.reshape(count // 2, -1, piece.shape[-1]) for piece in (left, got_left, right, got_right)]


def gather_places(count, groups):
    bits = bits_of(count)

    def spans(order):
        distances = [0]
        for bit in order:
            distances = [d | (on << bit) for d in distances for on in (0, 1)]
        return distances

    high = list(range(bits - 1, 1, -1))
    distance, place = [], []
    half = groups // 2
    for order, last, first in ((high + [1], 0, 0), (high + [0], 1, half)):
        for on in (0, 1):
            for d in spans(order):
                for group in range(first, first + half):
                    distance.append(d | (on << last))
                    place.append(group)
    return distance, place


def scatter_orders(bits):
    if bits < 3:
        return [list(range(bits))] * 3
    low, high = [0, 1], list(range(2, bits))
    return [
        low + high,
        [1] + high[:1] + [0] + high[1:],
        high[:1] + low + high[1:],
    ]


class Line:
    def __init__(self):
        self.last = None

    def gate(self, tensors):
        if self.last is None:
            return tensors
        tensors, _ = lax.optimization_barrier((tensors, self.last))
        return tensors

    def note(self, tensor):
        self.last = tensor


class Scatter:
    def __init__(self, line, count, orders):
        self.line, self.count, self.orders = line, count, orders
        self.left = [list(range(bits_of(count) - 1, -1, -1)) for _ in orders]
        self.step = 0

    def cut(self, parts):
        lead = self.count // 2
        picks, in_specs, operands, out_specs, out_shape = [], [], [], [], []
        for (kept, got, rows, block), order in zip(parts, self.orders):
            inner = 1 << order[0]
            after = [bit for bit in range(bits_of(self.count) - 1, -1, -1) if bit != order[0]]
            near = (lead // 2) >> after.index(order[1])
            picks.append(own_bit(order[0]))
            spec = pl.BlockSpec(
                (None, 2, None, rows, D),
                lambda i, inner=inner, block=block: (i // inner, 0, i % inner, block, 0),
            )
            in_specs += [spec, spec]
            kept, got = (t.reshape(lead // inner, 2, inner, -1, D) for t in (kept, got))
            operands += [in_hbm(kept), got]
            out_specs += [
                pl.BlockSpec((None, rows, D), lambda i: (i, 0, 0)),
                pl.BlockSpec(
                    (None, None, None, rows, D),
                    lambda i, near=near: (i // (2 * near), (i // near) % 2, i % near, 0, 0),
                ),
            ]
            out_shape += [
                shaped((lead, rows, D), BF), pltpu.HBM((lead // (2 * near), 2, near, rows, D), BF)
            ]
        out = call(
            functools.partial(stage_kernel, len(parts)), (lead,),
            [pl.BlockSpec(memory_space=pltpu.SMEM)] + in_specs, out_specs, out_shape, 0, 0, vmem=10,
        )(*self.line.gate((jnp.stack(picks).astype(jnp.int32), *operands)))
        self.line.note(out)
        return [(sent, stay, part[2]) for sent, stay, part in zip(out[::2], out[1::2], parts)]

    def begin_cut(self, parts):
        self.parts = []
        for (sent, stay, rows), left, order in zip(parts, self.left, self.orders):
            bit = order[0]
            left.remove(bit)
            self.parts.append((stay, swap(self.line.gate(sent), "blk", bit, self.count), rows, 0))
        self.step += 1

    def send(self, pin=lambda tensor: tensor, far=False):
        if self.step == len(self.orders[0]) - 1 and len({order[-1] for order in self.orders}) == 1:
            self.send_last(pin)
            return
        lead = (self.count >> self.step) // 2
        picks, in_specs, operands, out_specs, out_shape, bits = [], [], [], [], [], []
        for left, order in zip(self.left, self.orders):
            bits.append((order[self.step], left.index(order[self.step])))
            left.remove(order[self.step])
        for (kept, got, rows, block), (bit, place) in zip(self.parts, bits):
            inner = lead >> place
            picks.append(own_bit(bit))
            spec = pl.BlockSpec(
                (None, 2, None, rows, D),
                lambda i, inner=inner, block=block: (i // inner, 0, i % inner, block, 0),
            )
            in_specs += [spec, spec]
            got = got.reshape(lead // inner, 2, inner, -1, D)
            kept = in_hbm(kept) if kept.ndim == 5 else kept.reshape(got.shape)
            operands += [kept, got]
            out_specs += [pl.BlockSpec((None, rows, D), lambda i: (i, 0, 0))] * 2
            out_shape += [shaped((lead, rows, D), BF), (pltpu.HBM if far else shaped)((lead, rows, D), BF)]
        moved = sum(3 * 4 * lead * part[2] * D for part in self.parts)
        out = call(
            functools.partial(stage_kernel, len(self.parts)), (lead,),
            [pl.BlockSpec(memory_space=pltpu.SMEM)] + in_specs, out_specs, out_shape, 0, moved, vmem=10,
        )(*self.line.gate((jnp.stack(picks).astype(jnp.int32), *operands)))
        cut = [(sent, stay, part[2]) for sent, stay, part in zip(out[::2], out[1::2], self.parts)]
        self.line.note(out)
        self.parts = [
            (stay, swap(sent, "blk", bit, self.count), rows, 0)
            for (sent, stay, rows), (bit, _) in zip(cut, bits)
        ]
        self.step += 1

    def send_last(self, pin=lambda tensor: tensor):
        bit = self.orders[0][-1]
        rows = [part[2] for part in self.parts]
        operands = [pin(t) for kept, got, _, _ in self.parts for t in (kept, got)]
        shape = (sum(rows), D)
        send, stay = call(
            functools.partial(last_stage_kernel, len(rows)), (1,),
            [pl.BlockSpec(memory_space=pltpu.SMEM)] + [whole(t.shape) for t in operands], [whole(shape)] * 2,
            [shaped(shape, BF)] * 2, 0, 12 * shape[0] * D,
        )(*self.line.gate((own_bit(bit).reshape(1).astype(jnp.int32), *operands)))
        self.line.note(stay)
        self.parts = [(stay, swap(send, "blk", bit, self.count), shape[0], 0)]
        self.step += 1

    def flying(self):
        return [part[1] for part in self.parts]

    def result(self):
        ((stay, got, rows, _),) = self.parts
        return call(
            sum_kernel, (1,), [whole((rows, D))] * 2, whole((rows, D)), shaped((rows, D), BF), 0, 6 * rows * D,
        )(*self.line.gate((stay, got)))


def make_body(n_blk, n_rep):
    rep_bits = bits_of(n_rep)
    orders = scatter_orders(bits_of(n_blk))
    rows = D // n_blk

    def body(
        patches, latents, norm_gain, norm_bias, read_in, read_out, self_in, self_out,
        write_in, write_out, feed_up, feed_down, group_image, cot_patches, cot_latents,
    ):
        x, z, cot, cot_z = patches[0], latents[0], cot_patches[0], cot_latents[0]
        tokens, lat = x.shape[0], z.shape[0]
        groups = lat // LAT
        size = tokens // groups
        total = lat * n_blk
        hidden = feed_up.shape[1]
        feed_rows = hidden // n_blk
        core = lax.axis_index("rep") & 1
        core_at = core.reshape(1).astype(jnp.int32)
        other_at = 1 - core_at
        norms = jnp.concatenate([norm_gain, norm_bias, jnp.zeros((6, D), BF)], 0).astype(F32)
        norm_spec = whole((16, D))
        square = whole((D, D))
        three = whole((3, D, D))
        lat_spec = whole((lat, D))
        fold_spec = whole((8, D))
        patch_spec = rows_of((size, D))
        smem = pl.BlockSpec(memory_space=pltpu.SMEM)
        share_spec = pl.BlockSpec((None, HL, size), lambda g: (g, 0, 0))
        grid = (groups,)
        unit_flops = 2 * tokens * D * D
        low_lat, full_lat, fold = shaped((lat, D), BF), shaped((lat, D), F32), shaped((8, D), F32)
        low_patch = shaped((tokens, D), BF)
        far_patch, far_lat, far_full = pltpu.HBM((tokens, D), BF), pltpu.HBM((lat, D), BF), pltpu.HBM((lat, D), F32)
        far_fold = pltpu.HBM((8, D), F32)
        line = Line()

        a1, q1, b1, k1, v1, p1, o1, z1, a2 = call(
            read_forward_kernel, grid,
            [patch_spec, lat_spec, norm_spec, three, square],
            [lat_spec, lat_spec, patch_spec, patch_spec, patch_spec, share_spec, lat_spec, lat_spec, lat_spec],
            [far_lat, far_full, low_patch, far_patch, far_patch, pltpu.HBM((groups, HL, size), F32),
             far_lat, full_lat, low_lat],
            2 * unit_flops, 12 * tokens * D,
            [pltpu.VMEM((lat, D), F32)],
        )(in_hbm(x), z, norms, in_hbm(read_in), in_hbm(read_out))

        q3 = []

        def fill_first(step):
            if step == 0:
                q3.append(narrow(mm(b1, write_in[0])))
                return q3[0]
            return None

        pieces = gather_rows(a2, n_blk, line, fill_first)
        q3 = q3[0]

        me = lax.axis_index("blk")
        distance, place = gather_places(n_blk, groups)
        places = (me ^ jnp.array(distance, jnp.int32)) * groups + jnp.array(place, jnp.int32)
        own_at = me * groups + jnp.arange(groups, dtype=jnp.int32)
        piece_shape = (n_blk // 2, lat // 2)
        hl2 = HEADS * lat
        a2_all, allowed, k2, v2, p2, l2, o2, z2, out_latents, b3, k3, v3 = call(
            self_forward_kernel, (1,),
            [smem] * 3 + [whole(piece_shape + (D,))] * 4 + [lat_spec, lat_spec, norm_spec, three, square,
             one_of(1), one_of(2)],
            [whole((total, D)), whole((hl2, total)), whole((total, D)), whole((total, D)), whole((hl2, total)),
             whole((hl2, 1))] + [lat_spec] * 6,
            [pltpu.HBM((total, D), BF), pltpu.HBM((hl2, total), F32), shaped((total, D), BF), shaped((total, D), BF),
             shaped((hl2, total), F32), shaped((hl2, 1), F32),
             far_lat, full_lat, low_lat, low_lat, full_lat, full_lat],
            unit_flops * 2, 10 * D * D * 2,
        )(group_image, places, own_at, *pieces, a2, z1, norms, self_in, self_out, write_in, write_in)

        resident = pl.BlockSpec(memory_space=pltpu.VMEM)
        pair_spec = pl.BlockSpec((2, size, D), lambda g: (0, g, 0))
        early_shape = (n_blk, 2 * rows, D)
        each = 1
        spans = rows_of((each * size, D))
        out_patches, h, gd, dq3, dx1, dk3, dv3, early_other, early_mine, gain4, shift4 = call(
            functools.partial(patch_kernel, D, size), (groups // each,),
            [smem] + [spans, spans, spans, lat_spec, lat_spec, norm_spec, square,
             resident, resident, whole((tokens, D)), lat_spec],
            [spans, spans,
             pl.BlockSpec((2, each * size, hidden), lambda g: (0, g, 0), pipeline_mode=pl.Buffered(1 if each > 1 else 2)),
             whole((tokens, D)), spans, lat_spec, lat_spec, whole(early_shape), whole(early_shape), fold_spec, fold_spec],
            [low_patch, far_patch, pltpu.HBM((2, tokens, hidden), BF),
             far_patch, pltpu.HBM((tokens, D), F32), full_lat, full_lat, shaped(early_shape, BF), shaped(early_shape, BF),
             far_fold, far_fold],
            unit_flops * 22, 40 * tokens * D, [pltpu.VMEM((tokens, D), BF)] * 2, vmem=46,
        )(core_at, in_hbm(x), in_hbm(q3), in_hbm(cot), k3, v3, norms, write_out, feed_up, feed_down, in_hbm(b1), b3)

        width = D + 128
        dz2, e2, payload, dq2, gain3, shift3 = call(
            latent_back_kernel, (1,),
            [lat_spec] * 4 + [whole((total, D))] * 2
            + [whole((hl2, total)), whole((hl2, 1)), norm_spec, one_of(1), one_of(2), square],
            [lat_spec] * 2 + [whole((lat, width)), lat_spec, fold_spec, fold_spec],
            [far_full, far_lat, shaped((lat, width), BF), far_lat, far_fold, far_fold],
            unit_flops, 10 * D * D,
        )(dk3, dv3, z2, cot_z, k2, v2, p2, l2, norms, write_in, write_in, self_out)
        line.note(payload)

        feed_specs = [
            pl.BlockSpec((None, tokens, D), lambda j, w: (w[0], 0, j)),
            pl.BlockSpec((tokens, D), lambda j, w: (0, 0), pipeline_mode=pl.Buffered(1)),
            pl.BlockSpec((tokens, D), lambda j, w: (0, 0), pipeline_mode=pl.Buffered(1)),
        ]

        def feed_call(kernel, in_specs, out_specs, out_shape, operands):
            return pl.pallas_call(
                kernel,
                grid_spec=pltpu.PrefetchScalarGridSpec(
                    num_scalar_prefetch=1, grid=(hidden // D,), in_specs=in_specs, out_specs=out_specs
                ),
                out_shape=out_shape,
                compiler_params=pltpu.CompilerParams(
                    vmem_limit_bytes=24 << 20, dimension_semantics=("arbitrary",)
                ),
                cost_estimate=pl.CostEstimate(
                    flops=unit_flops * 4, bytes_accessed=20 * tokens * D, transcendentals=0
                ),
            )(*line.gate(operands))

        def once(shape):
            return pl.BlockSpec(shape, lambda j, w: (0,) * len(shape), pipeline_mode=pl.Buffered(1))

        gd, h, e4 = in_hbm(gd), in_hbm(h), in_hbm(cot)
        half = feed_rows // 2
        first = Scatter(line, n_blk, orders)
        firsts = (orders[0][0], orders[1][0])

        def feed_other():
            shape = (n_blk, feed_rows, D)
            return feed_call(feed_kernel, feed_specs, once(shape), shaped(shape, BF), (other_at, gd, h, e4))

        def feed_mine(got):
            which = jnp.stack([core, own_bit(firsts[0]), own_bit(firsts[1])]).astype(jnp.int32)
            near = D // feed_rows
            shape = (n_blk // 2, half, D)
            return feed_call(
                functools.partial(feed_sum_kernel, firsts),
                feed_specs
                + [pl.BlockSpec((n_blk, rows, D), lambda j, w: (0, j, 0)),
                   pl.BlockSpec((near, feed_rows, D), lambda j, w: (j, 0, 0))],
                [once(shape)] * 4, [shaped(shape, BF)] * 4, (which, gd, h, e4, got, got),
            )

        whole_patch = whole((tokens, D))

        def core_swap(tensor):
            return swap(line.gate(tensor), "rep", 0, n_rep)

        early = {}

        def fill_second(step):
            if step == 0:
                early["got"] = core_swap(early_other)
                early["feed_other"] = feed_other()
                return early["feed_other"], early["got"]
            if step == 1:
                early["feed_got"] = core_swap(early["feed_other"])
                bit = orders[2][0]
                shape = (n_blk // 2, 2 * rows, D)
                early["sum"] = call(
                    functools.partial(cut_kernel, bit), (1,), [smem] + [whole(early_shape)] * 2,
                    [whole(shape)] * 2, [shaped(shape, BF)] * 2, 0, 12 * tokens * D,
                )(*line.gate((own_bit(bit).reshape(1).astype(jnp.int32), in_hbm(early_mine), in_hbm(early["got"]))))
                return early["sum"]
            if step == 3:
                early["feed"] = feed_mine(early["feed_got"])
                return early["feed"]
            return None

        spread_pieces = gather_rows(payload, n_blk, line, fill_second)
        feed0, feed1, feed2, feed3 = early["feed"]
        first.begin_cut([(feed0, feed1, half), (feed2, feed3, half), (*early["sum"], 2 * rows)])

        late_shape = (n_blk, 4 * rows, D)
        late_other, late_mine, dk1, dv1, dq1, dz1, gain2, shift2 = call(
            tail_kernel, grid,
            [smem] + [whole(piece_shape + (width,))] * 4
            + [whole((total, D)), whole((hl2, total)), whole((total, D)), whole((total, D))] + [lat_spec] * 3
            + [norm_spec, three, square, lat_spec, share_spec, patch_spec, patch_spec, whole_patch] + [lat_spec] * 5,
            [whole(late_shape)] * 2 + [whole_patch] * 2 + [lat_spec] * 2 + [fold_spec] * 2,
            [shaped(late_shape, BF), shaped(late_shape, BF), far_patch, far_patch, far_full, far_full, far_fold, far_fold],
            4 * unit_flops, 30 * tokens * D,
            [pltpu.VMEM((lat, D), F32)] + [pltpu.VMEM((lat, D), BF)] * 3,
            vmem=40,
        )(*line.gate((core_at, *spread_pieces, in_hbm(a2_all), in_hbm(allowed), k2, v2, in_hbm(dq2), in_hbm(z1), in_hbm(dz2), norms, self_in,
                      read_out, in_hbm(q1), in_hbm(p1), in_hbm(k1), in_hbm(v1), in_hbm(b1), in_hbm(a1), in_hbm(o1), in_hbm(a2),
                      in_hbm(o2), in_hbm(e2))))
        line.note((late_other, first.flying()))
        late_got = core_swap(late_other)
        first.send()
        line.note(late_got)
        last = Scatter(line, n_blk, orders)
        last_rows = 4 * rows // 3
        last_parts = last.cut([(late_mine, late_got, last_rows, i) for i in range(3)])
        line.note((last_parts, first.flying()))
        bits = bits_of(n_blk)
        first.send(far=first.step == bits - 2)
        line.note(first.flying())
        first.send(in_hbm)
        last.begin_cut(last_parts)
        dx, dz, norm_grads = call(
            input_back_kernel, grid,
            [patch_spec] * 5 + [lat_spec] * 3 + [norm_spec, three, one_of(0)] + [fold_spec] * 6,
            [patch_spec, lat_spec, norm_spec],
            [low_patch, low_lat, shaped((16, D), F32)],
            unit_flops * 3, 14 * tokens * D,
            [pltpu.VMEM((8, D), F32)] * 2,
        )(*line.gate((in_hbm(x), in_hbm(dx1), in_hbm(dq3), in_hbm(dk1), in_hbm(dv1), z, in_hbm(dz1), in_hbm(dq1), norms, read_in, write_in,
                      in_hbm(gain2), in_hbm(shift2), in_hbm(gain3), in_hbm(shift3), in_hbm(gain4), in_hbm(shift4))))
        line.note(dx)
        for bit in range(rep_bits):
            norm_grads = norm_grads + swap(line.gate(norm_grads), "rep", bit, n_rep)
        bits = bits_of(n_blk)

        def finish(flat):
            for bit in range(1, rep_bits):
                flat = narrow(flat.astype(F32) + swap(flat, "rep", bit, n_rep).astype(F32))
            return flat, swap(flat, "rep", 0, n_rep)

        def outputs(kernel, flat, partner, shapes):
            return call(
                kernel, (1,), [smem, whole(flat.shape), whole(flat.shape)], [whole(t) for t in shapes],
                [shaped(t, F32) for t in shapes], 0, 12 * flat.shape[0] * D,
            )(*line.gate((core_at, flat, partner)))

        for step in range(bits):
            got = swap(line.gate(norm_grads), "blk", step, n_blk)
            if step == 0:
                line.note((last.flying(), first.flying(), got))
            elif step == 1:
                last.send()
                while first.step < bits:
                    line.note(first.flying())
                    first.send()
                flat, partner = finish(first.result())
                up, down, wo, write_in_grad = outputs(
                    early_out_kernel, flat, partner, [(rows, hidden), (feed_rows, D), (rows, D), (3, rows, D)]
                )
                line.note((last.flying(), got, up))
            else:
                if last.step < bits:
                    last.send()
                line.note((last.flying(), got))
            norm_grads = norm_grads + got
        while last.step < bits:
            last.send()
            line.note(last.flying())
        flat, partner = finish(last.result())
        read_in_grad, read_out_grad, self_in_grad, self_out_grad = outputs(
            late_out_kernel, flat, partner, [(3, rows, D), (rows, D), (3, rows, D), (rows, D)]
        )
        norm_own = lax.dynamic_slice_in_dim(norm_grads, lax.axis_index("blk") * rows, rows, 1)
        return (
            out_patches[None], out_latents[None], dx[None], dz[None], norm_own[:5], norm_own[5:10],
            read_in_grad, read_out_grad, self_in_grad, self_out_grad, write_in_grad, wo, up, down,
        )

    return body


def solution(mesh):
    return jax.shard_map(
        make_body(mesh.shape["blk"], mesh.shape["rep"]),
        mesh=mesh,
        in_specs=(
            P("rep", "blk", None), P("rep", "blk", None), P(), P(), P(), P(), P(), P(), P(), P(), P(), P(),
            P("rep", None), P("rep", "blk", None), P("rep", "blk", None),
        ),
        out_specs=(
            P("rep", "blk", None), P("rep", "blk", None), P("rep", "blk", None), P("rep", "blk", None),
            P(None, "blk"), P(None, "blk"), P(None, "blk", None), P("blk", None), P(None, "blk", None),
            P("blk", None), P(None, "blk", None), P("blk", None), P("blk", None), P("blk", None),
        ),
        check_vma=False,
    )
```

```python
import functools

import jax
import jax.numpy as jnp
from jax import lax
from jax.experimental import pallas as pl
from jax.experimental.pallas import tpu as pltpu
from jax.sharding import PartitionSpec as P

D = 768
HEADS = 12
HEAD = 64
LAT = 8
FACTOR = HEAD ** (-0.5)
HL = HEADS * LAT
LANES = 768
BF = jnp.bfloat16
F32 = jnp.float32


def narrow(tensor):
    return tensor.astype(BF)


def mm(left, right):
    return lax.dot_general(left, right, (((1,), (0,)), ((), ())), preferred_element_type=F32)


def mm_tn(left, right):
    return lax.dot_general(left, right, (((0,), (0,)), ((), ())), preferred_element_type=F32)


def mm_nt(left, right):
    return lax.dot_general(left, right, (((1,), (1,)), ((), ())), preferred_element_type=F32)


def norm_parts(tensor):
    center = tensor - jnp.mean(tensor, axis=-1, keepdims=True)
    spread = jnp.mean(center * center, axis=-1, keepdims=True)
    inverse = lax.rsqrt(spread + 1e-06)
    return center * inverse, inverse


def norm_forward(tensor, gain, shift):
    unit, _ = norm_parts(tensor)
    return unit * gain + shift


def norm_back(unit, inverse, gain, upstream):
    scaled = upstream * gain
    return inverse * (
        scaled
        - jnp.mean(scaled, axis=-1, keepdims=True)
        - unit * jnp.mean(scaled * unit, axis=-1, keepdims=True)
    )


def fold_rows(tensor):
    rows, cols = tensor.shape
    return jnp.sum(tensor.reshape(rows // 8, 8, cols), axis=0)


def head_mask():
    head = lax.broadcasted_iota(jnp.int32, (HEADS, 1, D), 0)
    feature = lax.broadcasted_iota(jnp.int32, (HEADS, 1, D), 2)
    return (feature >= head * HEAD) & (feature < head * HEAD + HEAD)


def expand(rows):
    count = rows.shape[0]
    return narrow(jnp.where(head_mask(), rows[None], 0.0).reshape(HEADS * count, D))


def collapse(rows):
    count = rows.shape[0] // HEADS
    return jnp.sum(jnp.where(head_mask(), rows.reshape(HEADS, count, D), 0.0), axis=0)


def whole(shape):
    return pl.BlockSpec(shape, lambda *_: (0,) * len(shape), pipeline_mode=pl.Buffered(1))


def rows_of(shape):
    return pl.BlockSpec(shape, lambda g: (g,) + (0,) * (len(shape) - 1))


def one_of(index):
    return pl.BlockSpec(
        (None, D, D), lambda *_: (index, 0, 0), pipeline_mode=pl.Buffered(1)
    )


def shaped(shape, dtype):
    return jax.ShapeDtypeStruct(shape, dtype)


def in_hbm(tensor):
    return pltpu.with_memory_space_constraint(tensor, pltpu.HBM)


def image_marks(image_ref, places_ref, shape, axis, rows):
    index = lax.broadcasted_iota(jnp.int32, shape, axis)
    marks = jnp.zeros(shape, jnp.int32)
    for group in range(shape[axis] // rows):
        inside = (index >= group * rows) & (index < (group + 1) * rows)
        marks = jnp.where(inside, image_ref[0, places_ref[group]], marks)
    return marks


def gathered(refs):
    pieces = [ref[...] for ref in refs]
    return jnp.concatenate([piece.reshape(-1, piece.shape[-1]) for piece in pieces], 0)


def call(body, grid, in_specs, out_specs, out_shape, flops, moved, scratch=(), vmem=20):
    return pl.pallas_call(
        body,
        grid=grid,
        in_specs=in_specs,
        out_specs=out_specs,
        out_shape=out_shape,
        scratch_shapes=scratch,
        compiler_params=pltpu.CompilerParams(
            vmem_limit_bytes=vmem << 20, dimension_semantics=("arbitrary",) * len(grid)
        ),
        cost_estimate=pl.CostEstimate(
            flops=int(flops), bytes_accessed=int(moved), transcendentals=0
        ),
    )


def read_forward_kernel(
    x_ref, z_ref, norm_ref, in_ref, out_w_ref,
    a1_ref, q1_ref, b1_ref, k1_ref, v1_ref, p1_ref, o1_ref, z1_ref, a2_ref,
    mix_ref,
):
    step = pl.program_id(0)
    last = pl.num_programs(0) - 1

    @pl.when(step == 0)
    def _():
        a1 = narrow(norm_forward(z_ref[...].astype(F32), norm_ref[0:1], norm_ref[5:6]))
        a1_ref[...] = a1
        q1_ref[...] = narrow(mm(a1, in_ref[0])).astype(F32)

    b1 = narrow(norm_forward(x_ref[...].astype(F32), norm_ref[1:2], norm_ref[6:7]))
    b1_ref[...] = b1
    k1 = narrow(mm(b1, in_ref[1]))
    v1 = narrow(mm(b1, in_ref[2]))
    k1_ref[...] = k1
    v1_ref[...] = v1
    own = pl.ds(pl.multiple_of(step * LAT, LAT), LAT)
    scores = mm_nt(expand(q1_ref[own, :]), k1) * FACTOR
    powers = jnp.exp(scores - jnp.max(scores, axis=-1, keepdims=True))
    shares = powers / jnp.sum(powers, axis=-1, keepdims=True)
    p1_ref[...] = shares
    mix_ref[own, :] = collapse(mm(narrow(shares), v1))

    @pl.when(step == last)
    def _():
        o1 = narrow(mix_ref[...])
        o1_ref[...] = o1
        z1 = z_ref[...].astype(F32) + mm(o1, out_w_ref[...])
        z1_ref[...] = z1
        a2_ref[...] = narrow(norm_forward(z1, norm_ref[2:3], norm_ref[7:8]))


def self_forward_kernel(
    image_ref, places_ref, own_at_ref, piece0_ref, piece1_ref, piece2_ref, piece3_ref,
    a2_ref, z1_ref, norm_ref, in_ref, out_w_ref, wk_ref, wv_ref,
    all_ref, allowed_ref, k2_ref, v2_ref, p2_ref, l2_ref, o2_ref, z2_ref, out_ref, b3_ref, k3_ref, v3_ref,
):
    everyone = gathered((piece0_ref, piece1_ref, piece2_ref, piece3_ref))
    all_ref[...] = everyone
    k2 = narrow(mm(everyone, in_ref[1]))
    v2 = narrow(mm(everyone, in_ref[2]))
    k2_ref[...] = k2
    v2_ref[...] = v2
    q2 = narrow(mm(a2_ref[...], in_ref[0])).astype(F32)
    scores = mm_nt(expand(q2), k2) * FACTOR
    total, count = everyone.shape[0], q2.shape[0]
    owners = image_marks(image_ref, places_ref, (1, total), 1, LAT)
    own = jnp.concatenate([image_marks(image_ref, own_at_ref, (count, 1), 0, LAT)] * HEADS, 0)
    allowed = own == owners
    allowed_ref[...] = jnp.where(allowed, 1.0, 0.0)
    scores = jnp.where(allowed, scores, -1e30)
    highest = jnp.max(scores, axis=-1, keepdims=True)
    powers = jnp.exp(scores - highest)
    totals = jnp.sum(powers, axis=-1, keepdims=True)
    shares = powers / totals
    p2_ref[...] = shares
    l2_ref[...] = highest + jnp.log(totals)
    o2 = narrow(collapse(mm(narrow(shares), v2)))
    o2_ref[...] = o2
    z2 = z1_ref[...] + mm(o2, out_w_ref[...])
    z2_ref[...] = z2
    out_ref[...] = narrow(z2)
    b3 = narrow(norm_forward(z2, norm_ref[3:4], norm_ref[8:9]))
    b3_ref[...] = b3
    k3_ref[...] = narrow(mm(b3, wk_ref[...])).astype(F32)
    v3_ref[...] = narrow(mm(b3, wv_ref[...])).astype(F32)


ROOT_HALF = 0.7071067811865476
DENSITY = 0.3989422804014327


def patch_kernel(
    chunk, size, core_ref, x_ref, q3_ref, cot_ref, k3_ref, v3_ref, norm_ref, wo_ref, up_ref, down_ref, b1_ref, b3_ref,
    near_ref, far_ref, out_ref, h_ref, gd_ref, dq3_ref, dx1_ref, dk3_ref, dv3_ref, other_ref, mine_ref,
    gain_ref, shift_ref, o3_ref, e3_ref, b1_all_ref, dq3_all_ref,
):
    step = pl.program_id(0)
    tokens = x_ref.shape[0]
    each = tokens // size
    here = pl.ds(pl.multiple_of(step * tokens, tokens), tokens)
    keys, values, weights = [], [], []
    for index in range(each):
        own = pl.ds(pl.multiple_of((step * each + index) * LAT, LAT), LAT)
        kx, vx = expand(k3_ref[own, :]), expand(v3_ref[own, :])
        rows = slice(index * size, (index + 1) * size)
        scores = (mm_nt(kx, q3_ref[rows]) * FACTOR).reshape(HEADS, LAT, size)
        powers = jnp.exp(scores - jnp.max(scores, axis=1, keepdims=True))
        shares = powers / jnp.sum(powers, axis=1, keepdims=True)
        keys.append(kx)
        values.append(vx)
        weights.append(shares)
    mixed = [narrow(mm_tn(narrow(w.reshape(HL, size)), v)) for w, v in zip(weights, values)]
    o3 = jnp.concatenate(mixed, 0) if each > 1 else mixed[0]
    o3_ref[here, :] = o3
    b1_all_ref[here, :] = b1_ref[...]
    x1 = x_ref[...].astype(F32) + mm(o3, wo_ref[...])
    unit, inverse = norm_parts(x1)
    gain = norm_ref[4:5]
    h = narrow(unit * gain + norm_ref[9:10])
    h_ref[...] = h
    e4 = cot_ref[...]
    x2 = x1
    dh = jnp.zeros((tokens, D), F32)
    hidden = up_ref.shape[1]
    for start in range(0, hidden, chunk):
        part = slice(start, start + chunk)
        u = mm(h, up_ref[:, part])
        cdf = 0.5 + 0.5 * lax.erf(u * ROOT_HALF)
        g = narrow(u * cdf)
        gd_ref[1, :, part] = g
        x2 = x2 + mm(g, down_ref[part, :])
        slope = cdf + u * (jnp.exp(-0.5 * u * u) * DENSITY)
        pulled = near_ref if start < hidden // 2 else far_ref
        begin = start % (hidden // 2)
        du = narrow(pulled[:, begin : begin + chunk].astype(F32) * slope)
        gd_ref[0, :, part] = du
        dh = dh + mm_nt(du, up_ref[:, part])
    out_ref[...] = narrow(x2)

    @pl.when(step == 0)
    def _():
        gain_ref[...] = jnp.zeros_like(gain_ref)
        shift_ref[...] = jnp.zeros_like(shift_ref)

    gain_ref[...] += fold_rows(dh * unit)
    shift_ref[...] += fold_rows(dh)
    dx1 = e4.astype(F32) + norm_back(unit, inverse, gain, dh)
    dx1_ref[...] = dx1
    e3 = narrow(dx1)
    e3_ref[here, :] = e3
    do3 = narrow(mm_nt(e3, wo_ref[...]))
    for index in range(each):
        own = pl.ds(pl.multiple_of((step * each + index) * LAT, LAT), LAT)
        place = pl.ds(pl.multiple_of((step * each + index) * size, size), size)
        rows = slice(index * size, (index + 1) * size)
        kx, vx, shares = keys[index], values[index], weights[index]
        grad = do3[rows]
        dshares = mm_nt(vx, grad).reshape(HEADS, LAT, size)
        inner = jnp.sum(shares * dshares, axis=1, keepdims=True)
        dscores = narrow((shares * (dshares - inner)).reshape(HL, size))
        dq3 = narrow(mm_tn(dscores, kx) * FACTOR)
        dq3_ref[rows] = dq3
        dq3_all_ref[place, :] = dq3
        dv3_ref[own, :] = narrow(collapse(mm(narrow(shares.reshape(HL, size)), grad))).astype(F32)
        dk3_ref[own, :] = narrow(collapse(mm(dscores, q3_ref[rows])) * FACTOR).astype(F32)

    @pl.when(step == pl.num_programs(0) - 1)
    def _():
        b3 = b3_ref[...]
        put_units(core_ref, other_ref, mine_ref,
                  [[(o3_ref, e3_ref), (b3, narrow(dk3_ref[...]))], [(b1_all_ref, dq3_all_ref), (b3, narrow(dv3_ref[...]))]])


STAT = 2 * HEADS


def latent_back_kernel(
    dk3_ref, dv3_ref, z2_ref, cot_ref, k2_ref, v2_ref, p2_ref, l2_ref, norm_ref, wk_ref, wv_ref, out_w_ref,
    dz2_ref, e2_ref, send_ref, dq2_ref, gain_ref, shift_ref,
):
    dk3 = narrow(dk3_ref[...])
    dv3 = narrow(dv3_ref[...])
    upstream = mm_nt(dk3, wk_ref[...]) + mm_nt(dv3, wv_ref[...])
    unit, inverse = norm_parts(z2_ref[...])
    gain_ref[...] = fold_rows(upstream * unit)
    shift_ref[...] = fold_rows(upstream)
    dz2 = cot_ref[...].astype(F32) + norm_back(unit, inverse, norm_ref[3:4], upstream)
    dz2_ref[...] = dz2
    e2 = narrow(dz2)
    e2_ref[...] = e2
    do2 = narrow(mm_nt(e2, out_w_ref[...]))
    send_ref[:, :D] = do2
    shares = p2_ref[...]
    dshares = mm_nt(expand(do2.astype(F32)), v2_ref[...])
    inner = jnp.sum(shares * dshares, axis=-1, keepdims=True)
    count = do2.shape[0]
    lane = lax.broadcasted_iota(jnp.int32, (count, 128), 1)
    stats = jnp.zeros((count, 128), F32)
    for slot, columns in ((0, l2_ref[...]), (HEADS, inner)):
        for head in range(HEADS):
            place = slot + head
            chosen = (lane == place) | (lane == place + STAT) | (lane == place + 2 * STAT)
            stats = jnp.where(chosen, columns[head * count : (head + 1) * count], stats)
    top = narrow(stats)
    rest = stats - top.astype(F32)
    middle = narrow(rest)
    bottom = narrow(rest - middle.astype(F32))
    send_ref[:, D:] = narrow(
        jnp.where(lane < STAT, top.astype(F32), jnp.where(lane < 2 * STAT, middle.astype(F32), bottom.astype(F32)))
    )
    dscores = narrow(shares * (dshares - inner))
    dq2_ref[...] = narrow(collapse(mm(dscores, k2_ref[...])) * FACTOR)


def spread_stat(stats, slot, count):
    shape = (HEADS * count, 128)
    place = lax.broadcasted_iota(jnp.int32, shape, 1)
    column = lax.broadcasted_iota(jnp.int32, shape, 0)
    chosen = jnp.zeros(shape, jnp.bool_)
    for term in range(3):
        head = place - (slot + term * STAT)
        chosen |= (head >= 0) & (head < HEADS) & (column >= head * count) & (column < (head + 1) * count)
    return mm_nt(narrow(jnp.where(chosen, 1.0, 0.0)), stats)


def unit_grad(left, right, count):
    return mm_tn(left[...], right[...]).reshape(count, D // count, D)


def put_units(core_ref, other_ref, mine_ref, units):
    count = mine_ref.shape[0]
    rows = D // count
    for core in range(2):
        @pl.when(core_ref[0] == core)
        def _():
            for ref, pairs in ((other_ref, units[1 - core]), (mine_ref, units[core])):
                for index, (left, right) in enumerate(pairs):
                    ref[:, index * rows : (index + 1) * rows, :] = narrow(unit_grad(left, right, count))


def cut_kernel(bit, pick_ref, keep_ref, got_ref, send_ref, stay_ref):
    zero, one = halves(keep_ref[...].astype(F32) + got_ref[...].astype(F32), bit)
    mine = pick_ref[0] == 0
    send_ref[...] = narrow(jnp.where(mine, one, zero))
    stay_ref[...] = narrow(jnp.where(mine, zero, one))


def stage_kernel(parts, pick_ref, *refs):
    for index in range(parts):
        keep_ref, got_ref = refs[2 * index : 2 * index + 2]
        send_ref, stay_ref = refs[2 * parts + 2 * index : 2 * parts + 2 * index + 2]
        mine = pick_ref[index]
        send_ref[...] = narrow(keep_ref[1 - mine].astype(F32) + got_ref[1 - mine].astype(F32))
        stay_ref[...] = narrow(keep_ref[mine].astype(F32) + got_ref[mine].astype(F32))


def last_stage_kernel(parts, pick_ref, *refs):
    send_ref, stay_ref = refs[2 * parts :]
    mine = pick_ref[0]
    start = 0
    for index in range(parts):
        keep_ref, got_ref = refs[2 * index : 2 * index + 2]
        rows = keep_ref.shape[1]
        span = slice(start, start + rows)
        send_ref[span] = narrow(keep_ref[1 - mine].astype(F32) + got_ref[1 - mine].astype(F32))
        stay_ref[span] = narrow(keep_ref[mine].astype(F32) + got_ref[mine].astype(F32))
        start += rows


def sum_kernel(keep_ref, got_ref, out_ref):
    out_ref[...] = narrow(keep_ref[...].astype(F32) + got_ref[...].astype(F32))


def early_out_kernel(core_ref, mine_ref, partner_ref, up_ref, down_ref, wo_ref, in_ref):
    rows = wo_ref.shape[0]
    feed_rows = down_ref.shape[0]
    for core in range(2):
        @pl.when(core_ref[0] == core)
        def _():
            zero, one = (mine_ref, partner_ref) if core == 0 else (partner_ref, mine_ref)
            for index in range(feed_rows // rows):
                up_ref[:, index * D : (index + 1) * D] = zero[index * rows : (index + 1) * rows].astype(F32)
            down_ref[...] = one[:feed_rows].astype(F32)
            wo_ref[...] = zero[feed_rows : feed_rows + rows].astype(F32)
            in_ref[0] = one[feed_rows : feed_rows + rows].astype(F32)
            in_ref[1] = zero[feed_rows + rows :].astype(F32)
            in_ref[2] = one[feed_rows + rows :].astype(F32)


def late_out_kernel(core_ref, mine_ref, partner_ref, read_in_ref, read_out_ref, self_in_ref, self_out_ref):
    rows = read_out_ref.shape[0]
    for core in range(2):
        @pl.when(core_ref[0] == core)
        def _():
            zero, one = (mine_ref, partner_ref) if core == 0 else (partner_ref, mine_ref)

            def unit(ref, index):
                return ref[index * rows : (index + 1) * rows].astype(F32)

            read_in_ref[0] = unit(zero, 1)
            read_in_ref[1] = unit(zero, 0)
            read_in_ref[2] = unit(one, 0)
            read_out_ref[...] = unit(one, 1)
            self_in_ref[0] = unit(zero, 2)
            self_in_ref[1] = unit(one, 2)
            self_in_ref[2] = unit(one, 3)
            self_out_ref[...] = unit(zero, 3)


def lane_spans():
    return [slice(start, start + LANES) for start in range(0, D, LANES)]


def feed_kernel(which_ref, gd_ref, h_ref, e4_ref, out_ref):
    part = pl.program_id(0)
    count, rows, _ = out_ref.shape
    slab = D // count
    near = D // rows

    @pl.when(which_ref[0] == 0)
    def _():
        for lanes in lane_spans():
            grad = narrow(mm_tn(h_ref[...], gd_ref[:, lanes]).reshape(count, slab, LANES))
            out_ref[:, pl.ds(pl.multiple_of(part * slab, 8), slab), lanes] = grad

    @pl.when(which_ref[0] == 1)
    def _():
        for lanes in lane_spans():
            grad = narrow(mm_tn(gd_ref[...], e4_ref[:, lanes]).reshape(near, rows, LANES))
            out_ref[pl.ds(part * near, near), :, lanes] = grad


def halves(tensor, bit):
    count, rows, cols = tensor.shape
    cut = tensor.reshape(count >> (bit + 1), 2, 1 << bit, rows, cols)
    return cut[:, 0].reshape(count // 2, rows, cols), cut[:, 1].reshape(count // 2, rows, cols)


def feed_sum_kernel(
    bits, which_ref, gd_ref, h_ref, e4_ref, got_up_ref, got_down_ref, send0_ref, stay0_ref, send1_ref, stay1_ref
):
    part = pl.program_id(0)
    count, slab, _ = got_up_ref.shape
    near, rows, _ = got_down_ref.shape
    half = rows // 2
    per_part = half // slab

    def store(index, place, value):
        zero, one = halves(value, bits[index])
        mine = which_ref[1 + index] == 0
        send, stay = ((send0_ref, stay0_ref), (send1_ref, stay1_ref))[index]
        send[place] = narrow(jnp.where(mine, one, zero))
        stay[place] = narrow(jnp.where(mine, zero, one))

    for index in range(2):
        @pl.when((which_ref[0] == 0) & (part // per_part == index))
        def _():
            rows_at = pl.ds(pl.multiple_of(lax.rem(part, per_part) * slab, 8), slab)
            for lanes in lane_spans():
                grad = mm_tn(h_ref[...], gd_ref[:, lanes]).reshape(count, slab, LANES)
                store(index, (slice(None), rows_at, lanes), grad + got_up_ref[:, :, lanes].astype(F32))

    @pl.when(which_ref[0] == 1)
    def _():
        place = pl.ds(part * (near // 2), near // 2)
        for lanes in lane_spans():
            grad = mm_tn(gd_ref[...], e4_ref[:, lanes]).reshape(near, rows, LANES)
            grad = grad + got_down_ref[:, :, lanes].astype(F32)
            for index in range(2):
                store(index, (place, slice(None), lanes), grad[:, index * half : (index + 1) * half])


def tail_kernel(
    core_ref, piece0_ref, piece1_ref, piece2_ref, piece3_ref, everyone_ref, allowed_ref, k2_ref, v2_ref,
    dq2_ref, z1_ref, dz2_ref, norm_ref, self_in_ref, read_out_ref, q1_ref, p1_ref, k1_ref, v1_ref,
    b1_ref, a1_ref, o1_ref, a2_ref, o2_ref, e2_ref,
    other_ref, mine_ref, dk1_ref, dv1_ref, dq1_ref, dz1_ref, gain_ref, shift_ref,
    do1_ref, e1_ref, dk2_ref, dv2_ref,
):
    step = pl.program_id(0)
    last = pl.num_programs(0) - 1

    @pl.when(step == 0)
    def _():
        count = dq2_ref.shape[0]
        half, everything = count // 2, everyone_ref.shape[0]

        def own_rows(ref):
            return jnp.concatenate([ref[:half], ref[everything // 2 : everything // 2 + half]], 0).astype(F32)

        q_all = narrow(mm(everyone_ref[...], self_in_ref[0]))
        spread = gathered((piece0_ref, piece1_ref, piece2_ref, piece3_ref))
        do_all = spread[:, :D]
        stats = spread[:, D:]
        scores = mm_nt(expand(own_rows(k2_ref)), q_all) * FACTOR
        allowed = allowed_ref[...] > 0.5
        log_total = spread_stat(stats, 0, count)
        shares = jnp.where(allowed, jnp.exp(jnp.where(allowed, scores - log_total, 0.0)), 0.0)
        dv2 = narrow(collapse(mm(narrow(shares), do_all)))
        dshares = mm_nt(expand(own_rows(v2_ref)), do_all)
        dscores = narrow(shares * (dshares - spread_stat(stats, HEADS, count)))
        dk2 = narrow(collapse(mm(dscores, q_all)) * FACTOR)
        dk2_ref[...] = dk2
        dv2_ref[...] = dv2
        upstream = (
            mm_nt(dq2_ref[...], self_in_ref[0]) + mm_nt(dk2, self_in_ref[1]) + mm_nt(dv2, self_in_ref[2])
        )
        unit, inverse = norm_parts(z1_ref[...])
        gain_ref[...] = fold_rows(upstream * unit)
        shift_ref[...] = fold_rows(upstream)
        dz1 = dz2_ref[...] + norm_back(unit, inverse, norm_ref[2:3], upstream)
        dz1_ref[...] = dz1
        e1 = narrow(dz1)
        e1_ref[...] = e1
        do1_ref[...] = narrow(mm_nt(e1, read_out_ref[...])).astype(F32)

    own = pl.ds(pl.multiple_of(step * LAT, LAT), LAT)
    qx = expand(q1_ref[own, :])
    dox = expand(do1_ref[own, :])
    shares = p1_ref[...]
    dshares = mm_nt(dox, v1_ref[...])
    inner = jnp.sum(shares * dshares, axis=-1, keepdims=True)
    dscores = narrow(shares * (dshares - inner))
    size = k1_ref.shape[0]
    here = pl.ds(pl.multiple_of(step * size, size), size)
    dv1 = narrow(mm_tn(narrow(shares), dox))
    dk1 = narrow(mm_tn(dscores, qx) * FACTOR)
    dv1_ref[here, :] = dv1
    dk1_ref[here, :] = dk1
    dq1_ref[own, :] = collapse(mm(dscores, k1_ref[...])) * FACTOR

    @pl.when(step == last)
    def _():
        dq1 = narrow(dq1_ref[...])
        put_units(core_ref, other_ref, mine_ref,
                  [[(b1_ref, dk1_ref), (a1_ref, dq1), (a2_ref, dq2_ref), (o2_ref, e2_ref)],
                   [(b1_ref, dv1_ref), (o1_ref, e1_ref), (a2_ref, dk2_ref), (a2_ref, dv2_ref)]])


def input_back_kernel(
    x_ref, dx1_ref, dq3_ref, dk1_ref, dv1_ref, z_ref, dz1_ref, dq1_ref, norm_ref, in_ref, wq_ref,
    gain2_ref, shift2_ref, gain3_ref, shift3_ref, gain4_ref, shift4_ref,
    dx_ref, dz_ref, sums_ref, gain_ref, shift_ref,
):
    step = pl.program_id(0)

    def total(tensor):
        return jnp.sum(tensor, axis=0, keepdims=True)

    @pl.when(step == 0)
    def _():
        gain_ref[...] = jnp.zeros_like(gain_ref)
        shift_ref[...] = jnp.zeros_like(shift_ref)
        upstream = mm_nt(narrow(dq1_ref[...]), in_ref[0])
        unit, inverse = norm_parts(z_ref[...].astype(F32))
        sums_ref[...] = jnp.zeros_like(sums_ref)
        sums_ref[0:1] = total(upstream * unit)
        sums_ref[5:6] = total(upstream)
        for index, ref in enumerate((gain2_ref, gain3_ref, gain4_ref)):
            sums_ref[2 + index : 3 + index] = total(ref[...])
        for index, ref in enumerate((shift2_ref, shift3_ref, shift4_ref)):
            sums_ref[7 + index : 8 + index] = total(ref[...])
        dz_ref[...] = narrow(dz1_ref[...] + norm_back(unit, inverse, norm_ref[0:1], upstream))

    upstream = (
        mm_nt(dq3_ref[...], wq_ref[...])
        + mm_nt(dk1_ref[...], in_ref[1])
        + mm_nt(dv1_ref[...], in_ref[2])
    )
    unit, inverse = norm_parts(x_ref[...].astype(F32))
    gain_ref[...] += fold_rows(upstream * unit)
    shift_ref[...] += fold_rows(upstream)
    dx_ref[...] = narrow(dx1_ref[...] + norm_back(unit, inverse, norm_ref[1:2], upstream))

    @pl.when(step == pl.num_programs(0) - 1)
    def _():
        sums_ref[1:2] = total(gain_ref[...])
        sums_ref[6:7] = total(shift_ref[...])


def bits_of(count):
    bits = count.bit_length() - 1
    if 1 << bits != count:
        raise ValueError("axis size")
    return bits


def swap(tensor, axis, bit, count):
    return lax.ppermute(tensor, axis, [(i, i ^ (1 << bit)) for i in range(count)])


def own_bit(bit, axis="blk"):
    return (lax.axis_index(axis) >> bit) & 1


def gather_rows(tensor, count, line, fill):
    bits = bits_of(count)
    step = 0
    for bit in range(bits - 1, 1, -1):
        other = swap(line.gate(tensor), "blk", bit, count)
        beside = fill(step)
        line.note((other, beside) if beside is not None else other)
        tensor = jnp.stack([tensor, other], step)
        step += 1
    rows = tensor.shape[-2]
    left, right = tensor[..., : rows // 2, :], tensor[..., rows // 2 :, :]
    for bit_left, bit_right in ((1, 0), (0, 1)):
        got_left = swap(line.gate(left), "blk", bit_left, count)
        got_right = swap(line.gate(right), "blk", bit_right, count)
        beside = fill(step)
        line.note((got_left, got_right) + (() if beside is None else (beside,)))
        if bit_left == 1:
            left = jnp.stack([left, got_left], step)
            right = jnp.stack([right, got_right], step)
        step += 1
    return [piece.reshape(count // 2, -1, piece.shape[-1]) for piece in (left, got_left, right, got_right)]


def gather_places(count, groups):
    bits = bits_of(count)

    def spans(order):
        distances = [0]
        for bit in order:
            distances = [d | (on << bit) for d in distances for on in (0, 1)]
        return distances

    high = list(range(bits - 1, 1, -1))
    distance, place = [], []
    half = groups // 2
    for order, last, first in ((high + [1], 0, 0), (high + [0], 1, half)):
        for on in (0, 1):
            for d in spans(order):
                for group in range(first, first + half):
                    distance.append(d | (on << last))
                    place.append(group)
    return distance, place


def scatter_orders(bits):
    if bits < 3:
        return [list(range(bits))] * 3
    low, high = [0, 1], list(range(2, bits))
    return [
        low + high,
        [1] + high[:1] + [0] + high[1:],
        high[:1] + low + high[1:],
    ]


class Line:
    def __init__(self):
        self.last = None

    def gate(self, tensors):
        if self.last is None:
            return tensors
        tensors, _ = lax.optimization_barrier((tensors, self.last))
        return tensors

    def note(self, tensor):
        self.last = tensor


class Scatter:
    def __init__(self, line, count, orders):
        self.line, self.count, self.orders = line, count, orders
        self.left = [list(range(bits_of(count) - 1, -1, -1)) for _ in orders]
        self.step = 0

    def cut(self, parts):
        lead = self.count // 2
        picks, in_specs, operands, out_specs, out_shape = [], [], [], [], []
        for (kept, got, rows, block), order in zip(parts, self.orders):
            inner = 1 << order[0]
            after = [bit for bit in range(bits_of(self.count) - 1, -1, -1) if bit != order[0]]
            near = (lead // 2) >> after.index(order[1])
            picks.append(own_bit(order[0]))
            spec = pl.BlockSpec(
                (None, 2, None, rows, D),
                lambda i, inner=inner, block=block: (i // inner, 0, i % inner, block, 0),
            )
            in_specs += [spec, spec]
            kept, got = (t.reshape(lead // inner, 2, inner, -1, D) for t in (kept, got))
            operands += [in_hbm(kept), got]
            out_specs += [
                pl.BlockSpec((None, rows, D), lambda i: (i, 0, 0)),
                pl.BlockSpec(
                    (None, None, None, rows, D),
                    lambda i, near=near: (i // (2 * near), (i // near) % 2, i % near, 0, 0),
                ),
            ]
            out_shape += [
                shaped((lead, rows, D), BF), pltpu.HBM((lead // (2 * near), 2, near, rows, D), BF)
            ]
        out = call(
            functools.partial(stage_kernel, len(parts)), (lead,),
            [pl.BlockSpec(memory_space=pltpu.SMEM)] + in_specs, out_specs, out_shape, 0, 0, vmem=10,
        )(*self.line.gate((jnp.stack(picks).astype(jnp.int32), *operands)))
        self.line.note(out)
        return [(sent, stay, part[2]) for sent, stay, part in zip(out[::2], out[1::2], parts)]

    def begin_cut(self, parts):
        self.parts = []
        for (sent, stay, rows), left, order in zip(parts, self.left, self.orders):
            bit = order[0]
            left.remove(bit)
            self.parts.append((stay, swap(self.line.gate(sent), "blk", bit, self.count), rows, 0))
        self.step += 1

    def send(self, pin=lambda tensor: tensor, far=False):
        if self.step == len(self.orders[0]) - 1 and len({order[-1] for order in self.orders}) == 1:
            self.send_last(pin)
            return
        lead = (self.count >> self.step) // 2
        picks, in_specs, operands, out_specs, out_shape, bits = [], [], [], [], [], []
        for left, order in zip(self.left, self.orders):
            bits.append((order[self.step], left.index(order[self.step])))
            left.remove(order[self.step])
        for (kept, got, rows, block), (bit, place) in zip(self.parts, bits):
            inner = lead >> place
            picks.append(own_bit(bit))
            spec = pl.BlockSpec(
                (None, 2, None, rows, D),
                lambda i, inner=inner, block=block: (i // inner, 0, i % inner, block, 0),
            )
            in_specs += [spec, spec]
            got = got.reshape(lead // inner, 2, inner, -1, D)
            kept = in_hbm(kept) if kept.ndim == 5 else kept.reshape(got.shape)
            operands += [kept, got]
            out_specs += [pl.BlockSpec((None, rows, D), lambda i: (i, 0, 0))] * 2
            out_shape += [shaped((lead, rows, D), BF), (pltpu.HBM if far else shaped)((lead, rows, D), BF)]
        moved = sum(3 * 4 * lead * part[2] * D for part in self.parts)
        out = call(
            functools.partial(stage_kernel, len(self.parts)), (lead,),
            [pl.BlockSpec(memory_space=pltpu.SMEM)] + in_specs, out_specs, out_shape, 0, moved, vmem=10,
        )(*self.line.gate((jnp.stack(picks).astype(jnp.int32), *operands)))
        cut = [(sent, stay, part[2]) for sent, stay, part in zip(out[::2], out[1::2], self.parts)]
        self.line.note(out)
        self.parts = [
            (stay, swap(sent, "blk", bit, self.count), rows, 0)
            for (sent, stay, rows), (bit, _) in zip(cut, bits)
        ]
        self.step += 1

    def send_last(self, pin=lambda tensor: tensor):
        bit = self.orders[0][-1]
        rows = [part[2] for part in self.parts]
        operands = [pin(t) for kept, got, _, _ in self.parts for t in (kept, got)]
        shape = (sum(rows), D)
        send, stay = call(
            functools.partial(last_stage_kernel, len(rows)), (1,),
            [pl.BlockSpec(memory_space=pltpu.SMEM)] + [whole(t.shape) for t in operands], [whole(shape)] * 2,
            [shaped(shape, BF)] * 2, 0, 12 * shape[0] * D,
        )(*self.line.gate((own_bit(bit).reshape(1).astype(jnp.int32), *operands)))
        self.line.note(stay)
        self.parts = [(stay, swap(send, "blk", bit, self.count), shape[0], 0)]
        self.step += 1

    def flying(self):
        return [part[1] for part in self.parts]

    def result(self):
        ((stay, got, rows, _),) = self.parts
        return call(
            sum_kernel, (1,), [whole((rows, D))] * 2, whole((rows, D)), shaped((rows, D), BF), 0, 6 * rows * D,
        )(*self.line.gate((stay, got)))


def make_body(n_blk, n_rep):
    rep_bits = bits_of(n_rep)
    orders = scatter_orders(bits_of(n_blk))
    rows = D // n_blk

    def body(
        patches, latents, norm_gain, norm_bias, read_in, read_out, self_in, self_out,
        write_in, write_out, feed_up, feed_down, group_image, cot_patches, cot_latents,
    ):
        x, z, cot, cot_z = patches[0], latents[0], cot_patches[0], cot_latents[0]
        tokens, lat = x.shape[0], z.shape[0]
        groups = lat // LAT
        size = tokens // groups
        total = lat * n_blk
        hidden = feed_up.shape[1]
        feed_rows = hidden // n_blk
        core = lax.axis_index("rep") & 1
        core_at = core.reshape(1).astype(jnp.int32)
        other_at = 1 - core_at
        norms = jnp.concatenate([norm_gain, norm_bias, jnp.zeros((6, D), BF)], 0).astype(F32)
        norm_spec = whole((16, D))
        square = whole((D, D))
        three = whole((3, D, D))
        lat_spec = whole((lat, D))
        fold_spec = whole((8, D))
        patch_spec = rows_of((size, D))
        smem = pl.BlockSpec(memory_space=pltpu.SMEM)
        share_spec = pl.BlockSpec((None, HL, size), lambda g: (g, 0, 0))
        grid = (groups,)
        unit_flops = 2 * tokens * D * D
        low_lat, full_lat, fold = shaped((lat, D), BF), shaped((lat, D), F32), shaped((8, D), F32)
        low_patch = shaped((tokens, D), BF)
        far_patch, far_lat, far_full = pltpu.HBM((tokens, D), BF), pltpu.HBM((lat, D), BF), pltpu.HBM((lat, D), F32)
        far_fold = pltpu.HBM((8, D), F32)
        line = Line()

        a1, q1, b1, k1, v1, p1, o1, z1, a2 = call(
            read_forward_kernel, grid,
            [patch_spec, lat_spec, norm_spec, three, square],
            [lat_spec, lat_spec, patch_spec, patch_spec, patch_spec, share_spec, lat_spec, lat_spec, lat_spec],
            [far_lat, far_full, low_patch, far_patch, far_patch, pltpu.HBM((groups, HL, size), F32),
             far_lat, full_lat, low_lat],
            2 * unit_flops, 12 * tokens * D,
            [pltpu.VMEM((lat, D), F32)],
        )(in_hbm(x), in_hbm(z), norms, in_hbm(read_in), in_hbm(read_out))

        q3, pulled = [], []

        def fill_first(step):
            if step == 0:
                q3.append(narrow(mm(b1, write_in[0])))
                return q3[0]
            if step < 3:
                span = slice((step - 1) * hidden // 2, step * hidden // 2)
                pulled.append(narrow(mm_nt(line.gate(cot), feed_down[span])))
                return pulled[-1]
            return None

        pieces = gather_rows(a2, n_blk, line, fill_first)
        q3 = q3[0]

        me = lax.axis_index("blk")
        distance, place = gather_places(n_blk, groups)
        places = (me ^ jnp.array(distance, jnp.int32)) * groups + jnp.array(place, jnp.int32)
        own_at = me * groups + jnp.arange(groups, dtype=jnp.int32)
        piece_shape = (n_blk // 2, lat // 2)
        hl2 = HEADS * lat
        a2_all, allowed, k2, v2, p2, l2, o2, z2, out_latents, b3, k3, v3 = call(
            self_forward_kernel, (1,),
            [smem] * 3 + [whole(piece_shape + (D,))] * 4 + [lat_spec, lat_spec, norm_spec, three, square,
             one_of(1), one_of(2)],
            [whole((total, D)), whole((hl2, total)), whole((total, D)), whole((total, D)), whole((hl2, total)),
             whole((hl2, 1))] + [lat_spec] * 6,
            [pltpu.HBM((total, D), BF), pltpu.HBM((hl2, total), F32), shaped((total, D), BF), shaped((total, D), BF),
             shaped((hl2, total), F32), shaped((hl2, 1), F32),
             far_lat, full_lat, low_lat, low_lat, full_lat, full_lat],
            unit_flops * 2, 10 * D * D * 2,
        )(group_image, places, own_at, *pieces, a2, z1, norms, self_in, self_out, write_in, write_in)

        resident = pl.BlockSpec(memory_space=pltpu.VMEM)
        pair_spec = pl.BlockSpec((2, size, D), lambda g: (0, g, 0))
        early_shape = (n_blk, 2 * rows, D)
        each = 1
        spans = rows_of((each * size, D))
        out_patches, h, gd, dq3, dx1, dk3, dv3, early_other, early_mine, gain4, shift4 = call(
            functools.partial(patch_kernel, D, size), (groups // each,),
            [smem] + [spans, spans, spans, lat_spec, lat_spec, norm_spec, square,
             resident, resident, spans, lat_spec] + [rows_of((each * size, hidden // 2))] * 2,
            [spans, spans,
             pl.BlockSpec((2, each * size, hidden), lambda g: (0, g, 0), pipeline_mode=pl.Buffered(1 if each > 1 else 2)),
             spans, spans, lat_spec, lat_spec, whole(early_shape), whole(early_shape), fold_spec, fold_spec],
            [low_patch, far_patch, pltpu.HBM((2, tokens, hidden), BF),
             far_patch, pltpu.HBM((tokens, D), F32), full_lat, full_lat, shaped(early_shape, BF), shaped(early_shape, BF),
             far_fold, far_fold],
            unit_flops * 22, 40 * tokens * D, [pltpu.VMEM((tokens, D), BF)] * 4, vmem=51,
        )(core_at, in_hbm(x), in_hbm(q3), in_hbm(cot), k3, v3, norms, write_out, feed_up, feed_down, in_hbm(b1), b3,
          *[in_hbm(t) for t in pulled])

        width = D + 128
        dz2, e2, payload, dq2, gain3, shift3 = call(
            latent_back_kernel, (1,),
            [lat_spec] * 4 + [whole((total, D))] * 2
            + [whole((hl2, total)), whole((hl2, 1)), norm_spec, one_of(1), one_of(2), square],
            [lat_spec] * 2 + [whole((lat, width)), lat_spec, fold_spec, fold_spec],
            [far_full, far_lat, shaped((lat, width), BF), far_lat, far_fold, far_fold],
            unit_flops, 10 * D * D,
        )(dk3, dv3, z2, cot_z, k2, v2, p2, l2, norms, write_in, write_in, self_out)
        line.note(payload)

        feed_specs = [
            pl.BlockSpec((None, tokens, D), lambda j, w: (w[0], 0, j)),
            pl.BlockSpec((tokens, D), lambda j, w: (0, 0), pipeline_mode=pl.Buffered(1)),
            pl.BlockSpec((tokens, D), lambda j, w: (0, 0), pipeline_mode=pl.Buffered(1)),
        ]

        def feed_call(kernel, in_specs, out_specs, out_shape, operands):
            return pl.pallas_call(
                kernel,
                grid_spec=pltpu.PrefetchScalarGridSpec(
                    num_scalar_prefetch=1, grid=(hidden // D,), in_specs=in_specs, out_specs=out_specs
                ),
                out_shape=out_shape,
                compiler_params=pltpu.CompilerParams(
                    vmem_limit_bytes=24 << 20, dimension_semantics=("arbitrary",)
                ),
                cost_estimate=pl.CostEstimate(
                    flops=unit_flops * 4, bytes_accessed=20 * tokens * D, transcendentals=0
                ),
            )(*line.gate(operands))

        def once(shape):
            return pl.BlockSpec(shape, lambda j, w: (0,) * len(shape), pipeline_mode=pl.Buffered(1))

        gd, h, e4 = in_hbm(gd), in_hbm(h), in_hbm(cot)
        half = feed_rows // 2
        first = Scatter(line, n_blk, orders)
        firsts = (orders[0][0], orders[1][0])

        def feed_other():
            shape = (n_blk, feed_rows, D)
            return feed_call(feed_kernel, feed_specs, once(shape), shaped(shape, BF), (other_at, gd, h, e4))

        def feed_mine(got):
            which = jnp.stack([core, own_bit(firsts[0]), own_bit(firsts[1])]).astype(jnp.int32)
            near = D // feed_rows
            shape = (n_blk // 2, half, D)
            return feed_call(
                functools.partial(feed_sum_kernel, firsts),
                feed_specs
                + [pl.BlockSpec((n_blk, rows, D), lambda j, w: (0, j, 0)),
                   pl.BlockSpec((near, feed_rows, D), lambda j, w: (j, 0, 0))],
                [once(shape)] * 4, [shaped(shape, BF)] * 4, (which, gd, h, e4, got, got),
            )

        whole_patch = whole((tokens, D))

        def core_swap(tensor):
            return swap(line.gate(tensor), "rep", 0, n_rep)

        early = {}

        def fill_second(step):
            if step == 0:
                early["got"] = core_swap(early_other)
                early["feed_other"] = feed_other()
                return early["feed_other"], early["got"]
            if step == 1:
                early["feed_got"] = core_swap(early["feed_other"])
                bit = orders[2][0]
                shape = (n_blk // 2, 2 * rows, D)
                early["sum"] = call(
                    functools.partial(cut_kernel, bit), (1,), [smem] + [whole(early_shape)] * 2,
                    [whole(shape)] * 2, [shaped(shape, BF)] * 2, 0, 12 * tokens * D,
                )(*line.gate((own_bit(bit).reshape(1).astype(jnp.int32), in_hbm(early_mine), in_hbm(early["got"]))))
                return early["sum"]
            if step == 3:
                early["feed"] = feed_mine(early["feed_got"])
                return early["feed"]
            return None

        spread_pieces = gather_rows(payload, n_blk, line, fill_second)
        feed0, feed1, feed2, feed3 = early["feed"]
        first.begin_cut([(feed0, feed1, half), (feed2, feed3, half), (*early["sum"], 2 * rows)])

        late_shape = (n_blk, 4 * rows, D)
        late_other, late_mine, dk1, dv1, dq1, dz1, gain2, shift2 = call(
            tail_kernel, grid,
            [smem] + [whole(piece_shape + (width,))] * 4
            + [whole((total, D)), whole((hl2, total)), whole((total, D)), whole((total, D))] + [lat_spec] * 3
            + [norm_spec, three, square, lat_spec, share_spec, patch_spec, patch_spec, whole_patch] + [lat_spec] * 5,
            [whole(late_shape)] * 2 + [whole_patch] * 2 + [lat_spec] * 2 + [fold_spec] * 2,
            [shaped(late_shape, BF), shaped(late_shape, BF), far_patch, far_patch, far_full, far_full, far_fold, far_fold],
            4 * unit_flops, 30 * tokens * D,
            [pltpu.VMEM((lat, D), F32)] + [pltpu.VMEM((lat, D), BF)] * 3,
            vmem=40,
        )(*line.gate((core_at, *spread_pieces, in_hbm(a2_all), in_hbm(allowed), k2, v2, in_hbm(dq2), in_hbm(z1), in_hbm(dz2), norms, self_in,
                      read_out, in_hbm(q1), in_hbm(p1), in_hbm(k1), in_hbm(v1), in_hbm(b1), in_hbm(a1), in_hbm(o1), in_hbm(a2),
                      in_hbm(o2), in_hbm(e2))))
        line.note((late_other, first.flying()))
        late_got = core_swap(late_other)
        first.send()
        line.note(late_got)
        last = Scatter(line, n_blk, orders)
        last_rows = 4 * rows // 3
        last_parts = last.cut([(late_mine, late_got, last_rows, i) for i in range(3)])
        line.note((last_parts, first.flying()))
        bits = bits_of(n_blk)
        first.send(far=first.step == bits - 2)
        line.note(first.flying())
        first.send(in_hbm)
        last.begin_cut(last_parts)
        dx, dz, norm_grads = call(
            input_back_kernel, grid,
            [patch_spec] * 5 + [lat_spec] * 3 + [norm_spec, three, one_of(0)] + [fold_spec] * 6,
            [patch_spec, lat_spec, norm_spec],
            [low_patch, low_lat, shaped((16, D), F32)],
            unit_flops * 3, 14 * tokens * D,
            [pltpu.VMEM((8, D), F32)] * 2,
        )(*line.gate((in_hbm(x), in_hbm(dx1), in_hbm(dq3), in_hbm(dk1), in_hbm(dv1), z, in_hbm(dz1), in_hbm(dq1), norms, read_in, write_in,
                      in_hbm(gain2), in_hbm(shift2), in_hbm(gain3), in_hbm(shift3), in_hbm(gain4), in_hbm(shift4))))
        line.note(dx)
        for bit in range(rep_bits):
            norm_grads = norm_grads + swap(line.gate(norm_grads), "rep", bit, n_rep)
        bits = bits_of(n_blk)

        def finish(flat):
            for bit in range(1, rep_bits):
                flat = narrow(flat.astype(F32) + swap(flat, "rep", bit, n_rep).astype(F32))
            return flat, swap(flat, "rep", 0, n_rep)

        def outputs(kernel, flat, partner, shapes):
            return call(
                kernel, (1,), [smem, whole(flat.shape), whole(flat.shape)], [whole(t) for t in shapes],
                [shaped(t, F32) for t in shapes], 0, 12 * flat.shape[0] * D,
            )(*line.gate((core_at, flat, partner)))

        for step in range(bits):
            got = swap(line.gate(norm_grads), "blk", step, n_blk)
            if step == 0:
                line.note((last.flying(), first.flying(), got))
            elif step == 1:
                last.send()
                while first.step < bits:
                    line.note(first.flying())
                    first.send()
                flat, partner = finish(first.result())
                up, down, wo, write_in_grad = outputs(
                    early_out_kernel, flat, partner, [(rows, hidden), (feed_rows, D), (rows, D), (3, rows, D)]
                )
                line.note((last.flying(), got, up))
            else:
                if last.step < bits:
                    last.send()
                line.note((last.flying(), got))
            norm_grads = norm_grads + got
        while last.step < bits:
            last.send()
            line.note(last.flying())
        flat, partner = finish(last.result())
        read_in_grad, read_out_grad, self_in_grad, self_out_grad = outputs(
            late_out_kernel, flat, partner, [(3, rows, D), (rows, D), (3, rows, D), (rows, D)]
        )
        norm_own = lax.dynamic_slice_in_dim(norm_grads, lax.axis_index("blk") * rows, rows, 1)
        return (
            out_patches[None], out_latents[None], dx[None], dz[None], norm_own[:5], norm_own[5:10],
            read_in_grad, read_out_grad, self_in_grad, self_out_grad, write_in_grad, wo, up, down,
        )

    return body


def solution(mesh):
    return jax.shard_map(
        make_body(mesh.shape["blk"], mesh.shape["rep"]),
        mesh=mesh,
        in_specs=(
            P("rep", "blk", None), P("rep", "blk", None), P(), P(), P(), P(), P(), P(), P(), P(), P(), P(),
            P("rep", None), P("rep", "blk", None), P("rep", "blk", None),
        ),
        out_specs=(
            P("rep", "blk", None), P("rep", "blk", None), P("rep", "blk", None), P("rep", "blk", None),
            P(None, "blk"), P(None, "blk"), P(None, "blk", None), P("blk", None), P(None, "blk", None),
            P("blk", None), P(None, "blk", None), P("blk", None), P("blk", None), P("blk", None),
        ),
        check_vma=False,
    )
```

```python
import functools

import jax
import jax.numpy as jnp
from jax import lax
from jax.experimental import pallas as pl
from jax.experimental.pallas import tpu as pltpu
from jax.sharding import PartitionSpec as P

D = 768
HEADS = 12
HEAD = 64
LAT = 8
FACTOR = HEAD ** (-0.5)
HL = HEADS * LAT
LANES = 768
BF = jnp.bfloat16
F32 = jnp.float32


def narrow(tensor):
    return tensor.astype(BF)


def mm(left, right):
    return lax.dot_general(left, right, (((1,), (0,)), ((), ())), preferred_element_type=F32)


def mm_tn(left, right):
    return lax.dot_general(left, right, (((0,), (0,)), ((), ())), preferred_element_type=F32)


def mm_nt(left, right):
    return lax.dot_general(left, right, (((1,), (1,)), ((), ())), preferred_element_type=F32)


def norm_parts(tensor):
    center = tensor - jnp.mean(tensor, axis=-1, keepdims=True)
    spread = jnp.mean(center * center, axis=-1, keepdims=True)
    inverse = lax.rsqrt(spread + 1e-06)
    return center * inverse, inverse


def norm_forward(tensor, gain, shift):
    unit, _ = norm_parts(tensor)
    return unit * gain + shift


def norm_back(unit, inverse, gain, upstream):
    scaled = upstream * gain
    return inverse * (
        scaled
        - jnp.mean(scaled, axis=-1, keepdims=True)
        - unit * jnp.mean(scaled * unit, axis=-1, keepdims=True)
    )


def fold_rows(tensor):
    rows, cols = tensor.shape
    return jnp.sum(tensor.reshape(rows // 8, 8, cols), axis=0)


def head_mask():
    head = lax.broadcasted_iota(jnp.int32, (HEADS, 1, D), 0)
    feature = lax.broadcasted_iota(jnp.int32, (HEADS, 1, D), 2)
    return (feature >= head * HEAD) & (feature < head * HEAD + HEAD)


def expand(rows):
    count = rows.shape[0]
    return narrow(jnp.where(head_mask(), rows[None], 0.0).reshape(HEADS * count, D))


def collapse(rows):
    count = rows.shape[0] // HEADS
    return jnp.sum(jnp.where(head_mask(), rows.reshape(HEADS, count, D), 0.0), axis=0)


def whole(shape):
    return pl.BlockSpec(shape, lambda *_: (0,) * len(shape), pipeline_mode=pl.Buffered(1))


def rows_of(shape):
    return pl.BlockSpec(shape, lambda g: (g,) + (0,) * (len(shape) - 1))


def one_of(index):
    return pl.BlockSpec(
        (None, D, D), lambda *_: (index, 0, 0), pipeline_mode=pl.Buffered(1)
    )


def shaped(shape, dtype):
    return jax.ShapeDtypeStruct(shape, dtype)


def in_hbm(tensor):
    return pltpu.with_memory_space_constraint(tensor, pltpu.HBM)


def image_marks(image_ref, places_ref, shape, axis, rows):
    index = lax.broadcasted_iota(jnp.int32, shape, axis)
    marks = jnp.zeros(shape, jnp.int32)
    for group in range(shape[axis] // rows):
        inside = (index >= group * rows) & (index < (group + 1) * rows)
        marks = jnp.where(inside, image_ref[0, places_ref[group]], marks)
    return marks


def gathered(refs):
    pieces = [ref[...] for ref in refs]
    return jnp.concatenate([piece.reshape(-1, piece.shape[-1]) for piece in pieces], 0)


def call(body, grid, in_specs, out_specs, out_shape, flops, moved, scratch=(), vmem=20):
    return pl.pallas_call(
        body,
        grid=grid,
        in_specs=in_specs,
        out_specs=out_specs,
        out_shape=out_shape,
        scratch_shapes=scratch,
        compiler_params=pltpu.CompilerParams(
            vmem_limit_bytes=vmem << 20, dimension_semantics=("arbitrary",) * len(grid)
        ),
        cost_estimate=pl.CostEstimate(
            flops=int(flops), bytes_accessed=int(moved), transcendentals=0
        ),
    )


def read_forward_kernel(
    x_ref, z_ref, norm_ref, in_ref, out_w_ref,
    a1_ref, q1_ref, b1_ref, k1_ref, v1_ref, p1_ref, o1_ref, z1_ref, a2_ref,
    mix_ref,
):
    step = pl.program_id(0)
    last = pl.num_programs(0) - 1

    @pl.when(step == 0)
    def _():
        a1 = narrow(norm_forward(z_ref[...].astype(F32), norm_ref[0:1], norm_ref[5:6]))
        a1_ref[...] = a1
        q1_ref[...] = narrow(mm(a1, in_ref[0])).astype(F32)

    b1 = narrow(norm_forward(x_ref[...].astype(F32), norm_ref[1:2], norm_ref[6:7]))
    b1_ref[...] = b1
    k1 = narrow(mm(b1, in_ref[1]))
    v1 = narrow(mm(b1, in_ref[2]))
    k1_ref[...] = k1
    v1_ref[...] = v1
    own = pl.ds(pl.multiple_of(step * LAT, LAT), LAT)
    scores = mm_nt(expand(q1_ref[own, :]), k1) * FACTOR
    powers = jnp.exp(scores - jnp.max(scores, axis=-1, keepdims=True))
    shares = powers / jnp.sum(powers, axis=-1, keepdims=True)
    p1_ref[...] = shares
    mix_ref[own, :] = collapse(mm(narrow(shares), v1))

    @pl.when(step == last)
    def _():
        o1 = narrow(mix_ref[...])
        o1_ref[...] = o1
        z1 = z_ref[...].astype(F32) + mm(o1, out_w_ref[...])
        z1_ref[...] = z1
        a2_ref[...] = narrow(norm_forward(z1, norm_ref[2:3], norm_ref[7:8]))


def self_forward_kernel(
    image_ref, places_ref, own_at_ref, piece0_ref, piece1_ref, piece2_ref, piece3_ref,
    a2_ref, z1_ref, norm_ref, in_ref, out_w_ref, wk_ref, wv_ref,
    all_ref, allowed_ref, k2_ref, v2_ref, p2_ref, l2_ref, o2_ref, z2_ref, out_ref, b3_ref, k3_ref, v3_ref,
):
    everyone = gathered((piece0_ref, piece1_ref, piece2_ref, piece3_ref))
    all_ref[...] = everyone
    k2 = narrow(mm(everyone, in_ref[1]))
    v2 = narrow(mm(everyone, in_ref[2]))
    k2_ref[...] = k2
    v2_ref[...] = v2
    q2 = narrow(mm(a2_ref[...], in_ref[0])).astype(F32)
    scores = mm_nt(expand(q2), k2) * FACTOR
    total, count = everyone.shape[0], q2.shape[0]
    owners = image_marks(image_ref, places_ref, (1, total), 1, LAT)
    own = jnp.concatenate([image_marks(image_ref, own_at_ref, (count, 1), 0, LAT)] * HEADS, 0)
    allowed = own == owners
    allowed_ref[...] = jnp.where(allowed, 1.0, 0.0)
    scores = jnp.where(allowed, scores, -1e30)
    highest = jnp.max(scores, axis=-1, keepdims=True)
    powers = jnp.exp(scores - highest)
    totals = jnp.sum(powers, axis=-1, keepdims=True)
    shares = powers / totals
    p2_ref[...] = shares
    l2_ref[...] = highest + jnp.log(totals)
    o2 = narrow(collapse(mm(narrow(shares), v2)))
    o2_ref[...] = o2
    z2 = z1_ref[...] + mm(o2, out_w_ref[...])
    z2_ref[...] = z2
    out_ref[...] = narrow(z2)
    b3 = narrow(norm_forward(z2, norm_ref[3:4], norm_ref[8:9]))
    b3_ref[...] = b3
    k3_ref[...] = narrow(mm(b3, wk_ref[...])).astype(F32)
    v3_ref[...] = narrow(mm(b3, wv_ref[...])).astype(F32)


ROOT_HALF = 0.7071067811865476
DENSITY = 0.3989422804014327


def patch_kernel(
    chunk, size, core_ref, x_ref, q3_ref, cot_ref, k3_ref, v3_ref, norm_ref, wo_ref, up_ref, down_ref, b1_ref, b3_ref,
    out_ref, h_ref, gd_ref, dq3_ref, dx1_ref, dk3_ref, dv3_ref, other_ref, mine_ref,
    gain_ref, shift_ref, o3_ref, e3_ref, b1_all_ref, dq3_all_ref,
):
    step = pl.program_id(0)
    tokens = x_ref.shape[0]
    each = tokens // size
    here = pl.ds(pl.multiple_of(step * tokens, tokens), tokens)
    keys, values, weights = [], [], []
    for index in range(each):
        own = pl.ds(pl.multiple_of((step * each + index) * LAT, LAT), LAT)
        kx, vx = expand(k3_ref[own, :]), expand(v3_ref[own, :])
        rows = slice(index * size, (index + 1) * size)
        scores = (mm_nt(kx, q3_ref[rows]) * FACTOR).reshape(HEADS, LAT, size)
        powers = jnp.exp(scores - jnp.max(scores, axis=1, keepdims=True))
        shares = powers / jnp.sum(powers, axis=1, keepdims=True)
        keys.append(kx)
        values.append(vx)
        weights.append(shares)
    mixed = [narrow(mm_tn(narrow(w.reshape(HL, size)), v)) for w, v in zip(weights, values)]
    o3 = jnp.concatenate(mixed, 0) if each > 1 else mixed[0]
    o3_ref[here, :] = o3
    b1_all_ref[here, :] = b1_ref[...]
    x1 = x_ref[...].astype(F32) + mm(o3, wo_ref[...])
    unit, inverse = norm_parts(x1)
    gain = norm_ref[4:5]
    h = narrow(unit * gain + norm_ref[9:10])
    h_ref[...] = h
    e4 = cot_ref[...]
    x2 = x1
    dh = jnp.zeros((tokens, D), F32)
    hidden = up_ref.shape[1]
    for start in range(0, hidden, chunk):
        part = slice(start, start + chunk)
        u = mm(h, up_ref[:, part])
        cdf = 0.5 + 0.5 * lax.erf(u * ROOT_HALF)
        g = narrow(u * cdf)
        gd_ref[1, :, part] = g
        x2 = x2 + mm(g, down_ref[part, :])
        slope = cdf + u * (jnp.exp(-0.5 * u * u) * DENSITY)
        du = narrow(mm_nt(e4, down_ref[part, :]) * slope)
        gd_ref[0, :, part] = du
        dh = dh + mm_nt(du, up_ref[:, part])
    out_ref[...] = narrow(x2)

    @pl.when(step == 0)
    def _():
        gain_ref[...] = jnp.zeros_like(gain_ref)
        shift_ref[...] = jnp.zeros_like(shift_ref)

    gain_ref[...] += fold_rows(dh * unit)
    shift_ref[...] += fold_rows(dh)
    dx1 = e4.astype(F32) + norm_back(unit, inverse, gain, dh)
    dx1_ref[...] = dx1
    e3 = narrow(dx1)
    e3_ref[here, :] = e3
    do3 = narrow(mm_nt(e3, wo_ref[...]))
    for index in range(each):
        own = pl.ds(pl.multiple_of((step * each + index) * LAT, LAT), LAT)
        place = pl.ds(pl.multiple_of((step * each + index) * size, size), size)
        rows = slice(index * size, (index + 1) * size)
        kx, vx, shares = keys[index], values[index], weights[index]
        grad = do3[rows]
        dshares = mm_nt(vx, grad).reshape(HEADS, LAT, size)
        inner = jnp.sum(shares * dshares, axis=1, keepdims=True)
        dscores = narrow((shares * (dshares - inner)).reshape(HL, size))
        dq3 = narrow(mm_tn(dscores, kx) * FACTOR)
        dq3_ref[rows] = dq3
        dq3_all_ref[place, :] = dq3
        dv3_ref[own, :] = narrow(collapse(mm(narrow(shares.reshape(HL, size)), grad))).astype(F32)
        dk3_ref[own, :] = narrow(collapse(mm(dscores, q3_ref[rows])) * FACTOR).astype(F32)

    @pl.when(step == pl.num_programs(0) - 1)
    def _():
        b3 = b3_ref[...]
        put_units(core_ref, other_ref, mine_ref,
                  [[(o3_ref, e3_ref), (b3, narrow(dk3_ref[...]))], [(b1_all_ref, dq3_all_ref), (b3, narrow(dv3_ref[...]))]])


STAT = 2 * HEADS


def latent_back_kernel(
    dk3_ref, dv3_ref, z2_ref, cot_ref, k2_ref, v2_ref, p2_ref, l2_ref, norm_ref, wk_ref, wv_ref, out_w_ref,
    dz2_ref, e2_ref, send_ref, dq2_ref, gain_ref, shift_ref,
):
    dk3 = narrow(dk3_ref[...])
    dv3 = narrow(dv3_ref[...])
    upstream = mm_nt(dk3, wk_ref[...]) + mm_nt(dv3, wv_ref[...])
    unit, inverse = norm_parts(z2_ref[...])
    gain_ref[...] = fold_rows(upstream * unit)
    shift_ref[...] = fold_rows(upstream)
    dz2 = cot_ref[...].astype(F32) + norm_back(unit, inverse, norm_ref[3:4], upstream)
    dz2_ref[...] = dz2
    e2 = narrow(dz2)
    e2_ref[...] = e2
    do2 = narrow(mm_nt(e2, out_w_ref[...]))
    send_ref[:, :D] = do2
    shares = p2_ref[...]
    dshares = mm_nt(expand(do2.astype(F32)), v2_ref[...])
    inner = jnp.sum(shares * dshares, axis=-1, keepdims=True)
    count = do2.shape[0]
    lane = lax.broadcasted_iota(jnp.int32, (count, 128), 1)
    stats = jnp.zeros((count, 128), F32)
    for slot, columns in ((0, l2_ref[...]), (HEADS, inner)):
        for head in range(HEADS):
            place = slot + head
            chosen = (lane == place) | (lane == place + STAT) | (lane == place + 2 * STAT)
            stats = jnp.where(chosen, columns[head * count : (head + 1) * count], stats)
    top = narrow(stats)
    rest = stats - top.astype(F32)
    middle = narrow(rest)
    bottom = narrow(rest - middle.astype(F32))
    send_ref[:, D:] = narrow(
        jnp.where(lane < STAT, top.astype(F32), jnp.where(lane < 2 * STAT, middle.astype(F32), bottom.astype(F32)))
    )
    dscores = narrow(shares * (dshares - inner))
    dq2_ref[...] = narrow(collapse(mm(dscores, k2_ref[...])) * FACTOR)


def spread_stat(stats, slot, count):
    shape = (HEADS * count, 128)
    place = lax.broadcasted_iota(jnp.int32, shape, 1)
    column = lax.broadcasted_iota(jnp.int32, shape, 0)
    chosen = jnp.zeros(shape, jnp.bool_)
    for term in range(3):
        head = place - (slot + term * STAT)
        chosen |= (head >= 0) & (head < HEADS) & (column >= head * count) & (column < (head + 1) * count)
    return mm_nt(narrow(jnp.where(chosen, 1.0, 0.0)), stats)


def unit_grad(left, right, count):
    return mm_tn(left[...], right[...]).reshape(count, D // count, D)


def put_units(core_ref, other_ref, mine_ref, units):
    count = mine_ref.shape[0]
    rows = D // count
    for core in range(2):
        @pl.when(core_ref[0] == core)
        def _():
            for ref, pairs in ((other_ref, units[1 - core]), (mine_ref, units[core])):
                for index, (left, right) in enumerate(pairs):
                    ref[:, index * rows : (index + 1) * rows, :] = narrow(unit_grad(left, right, count))


def cut_kernel(bit, pick_ref, keep_ref, got_ref, send_ref, stay_ref):
    zero, one = halves(keep_ref[...].astype(F32) + got_ref[...].astype(F32), bit)
    mine = pick_ref[0] == 0
    send_ref[...] = narrow(jnp.where(mine, one, zero))
    stay_ref[...] = narrow(jnp.where(mine, zero, one))


def stage_kernel(parts, pick_ref, *refs):
    for index in range(parts):
        keep_ref, got_ref = refs[2 * index : 2 * index + 2]
        send_ref, stay_ref = refs[2 * parts + 2 * index : 2 * parts + 2 * index + 2]
        mine = pick_ref[index]
        send_ref[...] = narrow(keep_ref[1 - mine].astype(F32) + got_ref[1 - mine].astype(F32))
        stay_ref[...] = narrow(keep_ref[mine].astype(F32) + got_ref[mine].astype(F32))


def last_stage_kernel(parts, pick_ref, *refs):
    send_ref, stay_ref = refs[2 * parts :]
    mine = pick_ref[0]
    start = 0
    for index in range(parts):
        keep_ref, got_ref = refs[2 * index : 2 * index + 2]
        rows = keep_ref.shape[1]
        span = slice(start, start + rows)
        send_ref[span] = narrow(keep_ref[1 - mine].astype(F32) + got_ref[1 - mine].astype(F32))
        stay_ref[span] = narrow(keep_ref[mine].astype(F32) + got_ref[mine].astype(F32))
        start += rows


def sum_kernel(keep_ref, got_ref, out_ref):
    out_ref[...] = narrow(keep_ref[...].astype(F32) + got_ref[...].astype(F32))


def early_out_kernel(core_ref, mine_ref, partner_ref, up_ref, down_ref, wo_ref, in_ref):
    rows = wo_ref.shape[0]
    feed_rows = down_ref.shape[0]
    for core in range(2):
        @pl.when(core_ref[0] == core)
        def _():
            zero, one = (mine_ref, partner_ref) if core == 0 else (partner_ref, mine_ref)
            for index in range(feed_rows // rows):
                up_ref[:, index * D : (index + 1) * D] = zero[index * rows : (index + 1) * rows].astype(F32)
            down_ref[...] = one[:feed_rows].astype(F32)
            wo_ref[...] = zero[feed_rows : feed_rows + rows].astype(F32)
            in_ref[0] = one[feed_rows : feed_rows + rows].astype(F32)
            in_ref[1] = zero[feed_rows + rows :].astype(F32)
            in_ref[2] = one[feed_rows + rows :].astype(F32)


def late_out_kernel(core_ref, mine_ref, partner_ref, read_in_ref, read_out_ref, self_in_ref, self_out_ref):
    rows = read_out_ref.shape[0]
    for core in range(2):
        @pl.when(core_ref[0] == core)
        def _():
            zero, one = (mine_ref, partner_ref) if core == 0 else (partner_ref, mine_ref)

            def unit(ref, index):
                return ref[index * rows : (index + 1) * rows].astype(F32)

            read_in_ref[0] = unit(zero, 1)
            read_in_ref[1] = unit(zero, 0)
            read_in_ref[2] = unit(one, 0)
            read_out_ref[...] = unit(one, 1)
            self_in_ref[0] = unit(zero, 2)
            self_in_ref[1] = unit(one, 2)
            self_in_ref[2] = unit(one, 3)
            self_out_ref[...] = unit(zero, 3)


def lane_spans():
    return [slice(start, start + LANES) for start in range(0, D, LANES)]


def feed_kernel(which_ref, gd_ref, h_ref, e4_ref, out_ref):
    part = pl.program_id(0)
    count, rows, _ = out_ref.shape
    slab = D // count
    near = D // rows

    @pl.when(which_ref[0] == 0)
    def _():
        for lanes in lane_spans():
            grad = narrow(mm_tn(h_ref[...], gd_ref[:, lanes]).reshape(count, slab, LANES))
            out_ref[:, pl.ds(pl.multiple_of(part * slab, 8), slab), lanes] = grad

    @pl.when(which_ref[0] == 1)
    def _():
        for lanes in lane_spans():
            grad = narrow(mm_tn(gd_ref[...], e4_ref[:, lanes]).reshape(near, rows, LANES))
            out_ref[pl.ds(part * near, near), :, lanes] = grad


def halves(tensor, bit):
    count, rows, cols = tensor.shape
    cut = tensor.reshape(count >> (bit + 1), 2, 1 << bit, rows, cols)
    return cut[:, 0].reshape(count // 2, rows, cols), cut[:, 1].reshape(count // 2, rows, cols)


def feed_sum_kernel(
    bits, which_ref, gd_ref, h_ref, e4_ref, got_up_ref, got_down_ref, send0_ref, stay0_ref, send1_ref, stay1_ref
):
    part = pl.program_id(0)
    count, slab, _ = got_up_ref.shape
    near, rows, _ = got_down_ref.shape
    half = rows // 2
    per_part = half // slab

    def store(index, place, value):
        zero, one = halves(value, bits[index])
        mine = which_ref[1 + index] == 0
        send, stay = ((send0_ref, stay0_ref), (send1_ref, stay1_ref))[index]
        send[place] = narrow(jnp.where(mine, one, zero))
        stay[place] = narrow(jnp.where(mine, zero, one))

    for index in range(2):
        @pl.when((which_ref[0] == 0) & (part // per_part == index))
        def _():
            rows_at = pl.ds(pl.multiple_of(lax.rem(part, per_part) * slab, 8), slab)
            for lanes in lane_spans():
                grad = mm_tn(h_ref[...], gd_ref[:, lanes]).reshape(count, slab, LANES)
                store(index, (slice(None), rows_at, lanes), grad + got_up_ref[:, :, lanes].astype(F32))

    @pl.when(which_ref[0] == 1)
    def _():
        place = pl.ds(part * (near // 2), near // 2)
        for lanes in lane_spans():
            grad = mm_tn(gd_ref[...], e4_ref[:, lanes]).reshape(near, rows, LANES)
            grad = grad + got_down_ref[:, :, lanes].astype(F32)
            for index in range(2):
                store(index, (place, slice(None), lanes), grad[:, index * half : (index + 1) * half])


def tail_kernel(
    core_ref, piece0_ref, piece1_ref, piece2_ref, piece3_ref, everyone_ref, allowed_ref, k2_ref, v2_ref,
    dq2_ref, z1_ref, dz2_ref, norm_ref, self_in_ref, read_out_ref, q1_ref, p1_ref, k1_ref, v1_ref,
    b1_ref, a1_ref, o1_ref, a2_ref, o2_ref, e2_ref,
    other_ref, mine_ref, dk1_ref, dv1_ref, dq1_ref, dz1_ref, gain_ref, shift_ref,
    do1_ref, e1_ref, dk2_ref, dv2_ref,
):
    step = pl.program_id(0)
    last = pl.num_programs(0) - 1

    @pl.when(step == 0)
    def _():
        count = dq2_ref.shape[0]
        half, everything = count // 2, everyone_ref.shape[0]

        def own_rows(ref):
            return jnp.concatenate([ref[:half], ref[everything // 2 : everything // 2 + half]], 0).astype(F32)

        q_all = narrow(mm(everyone_ref[...], self_in_ref[0]))
        spread = gathered((piece0_ref, piece1_ref, piece2_ref, piece3_ref))
        do_all = spread[:, :D]
        stats = spread[:, D:]
        scores = mm_nt(expand(own_rows(k2_ref)), q_all) * FACTOR
        allowed = allowed_ref[...] > 0.5
        log_total = spread_stat(stats, 0, count)
        shares = jnp.where(allowed, jnp.exp(jnp.where(allowed, scores - log_total, 0.0)), 0.0)
        dv2 = narrow(collapse(mm(narrow(shares), do_all)))
        dshares = mm_nt(expand(own_rows(v2_ref)), do_all)
        dscores = narrow(shares * (dshares - spread_stat(stats, HEADS, count)))
        dk2 = narrow(collapse(mm(dscores, q_all)) * FACTOR)
        dk2_ref[...] = dk2
        dv2_ref[...] = dv2
        upstream = (
            mm_nt(dq2_ref[...], self_in_ref[0]) + mm_nt(dk2, self_in_ref[1]) + mm_nt(dv2, self_in_ref[2])
        )
        unit, inverse = norm_parts(z1_ref[...])
        gain_ref[...] = fold_rows(upstream * unit)
        shift_ref[...] = fold_rows(upstream)
        dz1 = dz2_ref[...] + norm_back(unit, inverse, norm_ref[2:3], upstream)
        dz1_ref[...] = dz1
        e1 = narrow(dz1)
        e1_ref[...] = e1
        do1_ref[...] = narrow(mm_nt(e1, read_out_ref[...])).astype(F32)

    own = pl.ds(pl.multiple_of(step * LAT, LAT), LAT)
    qx = expand(q1_ref[own, :])
    dox = expand(do1_ref[own, :])
    shares = p1_ref[...]
    dshares = mm_nt(dox, v1_ref[...])
    inner = jnp.sum(shares * dshares, axis=-1, keepdims=True)
    dscores = narrow(shares * (dshares - inner))
    size = k1_ref.shape[0]
    here = pl.ds(pl.multiple_of(step * size, size), size)
    dv1 = narrow(mm_tn(narrow(shares), dox))
    dk1 = narrow(mm_tn(dscores, qx) * FACTOR)
    dv1_ref[here, :] = dv1
    dk1_ref[here, :] = dk1
    dq1_ref[own, :] = collapse(mm(dscores, k1_ref[...])) * FACTOR

    @pl.when(step == last)
    def _():
        dq1 = narrow(dq1_ref[...])
        put_units(core_ref, other_ref, mine_ref,
                  [[(b1_ref, dk1_ref), (a1_ref, dq1), (a2_ref, dq2_ref), (o2_ref, e2_ref)],
                   [(b1_ref, dv1_ref), (o1_ref, e1_ref), (a2_ref, dk2_ref), (a2_ref, dv2_ref)]])


def input_back_kernel(
    x_ref, dx1_ref, dq3_ref, dk1_ref, dv1_ref, z_ref, dz1_ref, dq1_ref, norm_ref, in_ref, wq_ref,
    gain2_ref, shift2_ref, gain3_ref, shift3_ref, gain4_ref, shift4_ref,
    dx_ref, dz_ref, sums_ref, gain_ref, shift_ref,
):
    step = pl.program_id(0)

    def total(tensor):
        return jnp.sum(tensor, axis=0, keepdims=True)

    @pl.when(step == 0)
    def _():
        gain_ref[...] = jnp.zeros_like(gain_ref)
        shift_ref[...] = jnp.zeros_like(shift_ref)
        upstream = mm_nt(narrow(dq1_ref[...]), in_ref[0])
        unit, inverse = norm_parts(z_ref[...].astype(F32))
        sums_ref[...] = jnp.zeros_like(sums_ref)
        sums_ref[0:1] = total(upstream * unit)
        sums_ref[5:6] = total(upstream)
        for index, ref in enumerate((gain2_ref, gain3_ref, gain4_ref)):
            sums_ref[2 + index : 3 + index] = total(ref[...])
        for index, ref in enumerate((shift2_ref, shift3_ref, shift4_ref)):
            sums_ref[7 + index : 8 + index] = total(ref[...])
        dz_ref[...] = narrow(dz1_ref[...] + norm_back(unit, inverse, norm_ref[0:1], upstream))

    upstream = (
        mm_nt(dq3_ref[...], wq_ref[...])
        + mm_nt(dk1_ref[...], in_ref[1])
        + mm_nt(dv1_ref[...], in_ref[2])
    )
    unit, inverse = norm_parts(x_ref[...].astype(F32))
    gain_ref[...] += fold_rows(upstream * unit)
    shift_ref[...] += fold_rows(upstream)
    dx_ref[...] = narrow(dx1_ref[...] + norm_back(unit, inverse, norm_ref[1:2], upstream))

    @pl.when(step == pl.num_programs(0) - 1)
    def _():
        sums_ref[1:2] = total(gain_ref[...])
        sums_ref[6:7] = total(shift_ref[...])


def bits_of(count):
    bits = count.bit_length() - 1
    if 1 << bits != count:
        raise ValueError("axis size")
    return bits


def swap(tensor, axis, bit, count):
    return lax.ppermute(tensor, axis, [(i, i ^ (1 << bit)) for i in range(count)])


def own_bit(bit, axis="blk"):
    return (lax.axis_index(axis) >> bit) & 1


def gather_rows(tensor, count, line, fill):
    bits = bits_of(count)
    step = 0
    for bit in range(bits - 1, 1, -1):
        other = swap(line.gate(tensor), "blk", bit, count)
        beside = fill(step)
        line.note((other, beside) if beside is not None else other)
        tensor = jnp.stack([tensor, other], step)
        step += 1
    rows = tensor.shape[-2]
    left, right = tensor[..., : rows // 2, :], tensor[..., rows // 2 :, :]
    for bit_left, bit_right in ((1, 0), (0, 1)):
        got_left = swap(line.gate(left), "blk", bit_left, count)
        got_right = swap(line.gate(right), "blk", bit_right, count)
        beside = fill(step)
        line.note((got_left, got_right) + (() if beside is None else (beside,)))
        if bit_left == 1:
            left = jnp.stack([left, got_left], step)
            right = jnp.stack([right, got_right], step)
        step += 1
    return [piece.reshape(count // 2, -1, piece.shape[-1]) for piece in (left, got_left, right, got_right)]


def gather_places(count, groups):
    bits = bits_of(count)

    def spans(order):
        distances = [0]
        for bit in order:
            distances = [d | (on << bit) for d in distances for on in (0, 1)]
        return distances

    high = list(range(bits - 1, 1, -1))
    distance, place = [], []
    half = groups // 2
    for order, last, first in ((high + [1], 0, 0), (high + [0], 1, half)):
        for on in (0, 1):
            for d in spans(order):
                for group in range(first, first + half):
                    distance.append(d | (on << last))
                    place.append(group)
    return distance, place


def scatter_orders(bits):
    if bits < 3:
        return [list(range(bits))] * 3
    low, high = [0, 1], list(range(2, bits))
    return [
        low + high,
        [1] + high[:1] + [0] + high[1:],
        high[:1] + low + high[1:],
    ]


class Line:
    def __init__(self):
        self.last = None

    def gate(self, tensors):
        if self.last is None:
            return tensors
        tensors, _ = lax.optimization_barrier((tensors, self.last))
        return tensors

    def note(self, tensor):
        self.last = tensor


class Scatter:
    def __init__(self, line, count, orders):
        self.line, self.count, self.orders = line, count, orders
        self.left = [list(range(bits_of(count) - 1, -1, -1)) for _ in orders]
        self.step = 0

    def cut(self, parts):
        lead = self.count // 2
        picks, in_specs, operands, out_specs, out_shape = [], [], [], [], []
        for (kept, got, rows, block), order in zip(parts, self.orders):
            inner = 1 << order[0]
            after = [bit for bit in range(bits_of(self.count) - 1, -1, -1) if bit != order[0]]
            near = (lead // 2) >> after.index(order[1])
            picks.append(own_bit(order[0]))
            spec = pl.BlockSpec(
                (None, 2, None, rows, D),
                lambda i, inner=inner, block=block: (i // inner, 0, i % inner, block, 0),
            )
            in_specs += [spec, spec]
            kept, got = (t.reshape(lead // inner, 2, inner, -1, D) for t in (kept, got))
            operands += [in_hbm(kept), got]
            out_specs += [
                pl.BlockSpec((None, rows, D), lambda i: (i, 0, 0)),
                pl.BlockSpec(
                    (None, None, None, rows, D),
                    lambda i, near=near: (i // (2 * near), (i // near) % 2, i % near, 0, 0),
                ),
            ]
            out_shape += [
                shaped((lead, rows, D), BF), pltpu.HBM((lead // (2 * near), 2, near, rows, D), BF)
            ]
        out = call(
            functools.partial(stage_kernel, len(parts)), (lead,),
            [pl.BlockSpec(memory_space=pltpu.SMEM)] + in_specs, out_specs, out_shape, 0, 0, vmem=10,
        )(*self.line.gate((jnp.stack(picks).astype(jnp.int32), *operands)))
        self.line.note(out)
        return [(sent, stay, part[2]) for sent, stay, part in zip(out[::2], out[1::2], parts)]

    def begin_cut(self, parts):
        self.parts = []
        for (sent, stay, rows), left, order in zip(parts, self.left, self.orders):
            bit = order[0]
            left.remove(bit)
            self.parts.append((stay, swap(self.line.gate(sent), "blk", bit, self.count), rows, 0))
        self.step += 1

    def send(self, pin=lambda tensor: tensor, far=False):
        if self.step == len(self.orders[0]) - 1 and len({order[-1] for order in self.orders}) == 1:
            self.send_last(pin)
            return
        lead = (self.count >> self.step) // 2
        picks, in_specs, operands, out_specs, out_shape, bits = [], [], [], [], [], []
        for left, order in zip(self.left, self.orders):
            bits.append((order[self.step], left.index(order[self.step])))
            left.remove(order[self.step])
        for (kept, got, rows, block), (bit, place) in zip(self.parts, bits):
            inner = lead >> place
            picks.append(own_bit(bit))
            spec = pl.BlockSpec(
                (None, 2, None, rows, D),
                lambda i, inner=inner, block=block: (i // inner, 0, i % inner, block, 0),
            )
            in_specs += [spec, spec]
            got = got.reshape(lead // inner, 2, inner, -1, D)
            kept = in_hbm(kept) if kept.ndim == 5 else kept.reshape(got.shape)
            operands += [kept, got]
            out_specs += [pl.BlockSpec((None, rows, D), lambda i: (i, 0, 0))] * 2
            out_shape += [shaped((lead, rows, D), BF), (pltpu.HBM if far else shaped)((lead, rows, D), BF)]
        moved = sum(3 * 4 * lead * part[2] * D for part in self.parts)
        out = call(
            functools.partial(stage_kernel, len(self.parts)), (lead,),
            [pl.BlockSpec(memory_space=pltpu.SMEM)] + in_specs, out_specs, out_shape, 0, moved, vmem=10,
        )(*self.line.gate((jnp.stack(picks).astype(jnp.int32), *operands)))
        cut = [(sent, stay, part[2]) for sent, stay, part in zip(out[::2], out[1::2], self.parts)]
        self.line.note(out)
        self.parts = [
            (stay, swap(sent, "blk", bit, self.count), rows, 0)
            for (sent, stay, rows), (bit, _) in zip(cut, bits)
        ]
        self.step += 1

    def send_last(self, pin=lambda tensor: tensor):
        bit = self.orders[0][-1]
        rows = [part[2] for part in self.parts]
        operands = [pin(t) for kept, got, _, _ in self.parts for t in (kept, got)]
        shape = (sum(rows), D)
        send, stay = call(
            functools.partial(last_stage_kernel, len(rows)), (1,),
            [pl.BlockSpec(memory_space=pltpu.SMEM)] + [whole(t.shape) for t in operands], [whole(shape)] * 2,
            [shaped(shape, BF)] * 2, 0, 12 * shape[0] * D,
        )(*self.line.gate((own_bit(bit).reshape(1).astype(jnp.int32), *operands)))
        self.line.note(stay)
        self.parts = [(stay, swap(send, "blk", bit, self.count), shape[0], 0)]
        self.step += 1

    def flying(self):
        return [part[1] for part in self.parts]

    def result(self):
        ((stay, got, rows, _),) = self.parts
        return call(
            sum_kernel, (1,), [whole((rows, D))] * 2, whole((rows, D)), shaped((rows, D), BF), 0, 6 * rows * D,
        )(*self.line.gate((stay, got)))


def make_body(n_blk, n_rep):
    rep_bits = bits_of(n_rep)
    orders = scatter_orders(bits_of(n_blk))
    rows = D // n_blk

    def body(
        patches, latents, norm_gain, norm_bias, read_in, read_out, self_in, self_out,
        write_in, write_out, feed_up, feed_down, group_image, cot_patches, cot_latents,
    ):
        x, z, cot, cot_z = patches[0], latents[0], cot_patches[0], cot_latents[0]
        tokens, lat = x.shape[0], z.shape[0]
        groups = lat // LAT
        size = tokens // groups
        total = lat * n_blk
        hidden = feed_up.shape[1]
        feed_rows = hidden // n_blk
        core = lax.axis_index("rep") & 1
        core_at = core.reshape(1).astype(jnp.int32)
        other_at = 1 - core_at
        norms = jnp.concatenate([norm_gain, norm_bias, jnp.zeros((6, D), BF)], 0).astype(F32)
        norm_spec = whole((16, D))
        square = whole((D, D))
        three = whole((3, D, D))
        lat_spec = whole((lat, D))
        fold_spec = whole((8, D))
        patch_spec = rows_of((size, D))
        smem = pl.BlockSpec(memory_space=pltpu.SMEM)
        share_spec = pl.BlockSpec((None, HL, size), lambda g: (g, 0, 0))
        grid = (groups,)
        unit_flops = 2 * tokens * D * D
        low_lat, full_lat, fold = shaped((lat, D), BF), shaped((lat, D), F32), shaped((8, D), F32)
        low_patch = shaped((tokens, D), BF)
        far_patch, far_lat, far_full = pltpu.HBM((tokens, D), BF), pltpu.HBM((lat, D), BF), pltpu.HBM((lat, D), F32)
        far_fold = pltpu.HBM((8, D), F32)
        line = Line()

        a1, q1, b1, k1, v1, p1, o1, z1, a2 = call(
            read_forward_kernel, grid,
            [patch_spec, lat_spec, norm_spec, three, square],
            [lat_spec, lat_spec, patch_spec, patch_spec, patch_spec, share_spec, lat_spec, lat_spec, lat_spec],
            [far_lat, far_full, low_patch, far_patch, far_patch, pltpu.HBM((groups, HL, size), F32),
             far_lat, full_lat, low_lat],
            2 * unit_flops, 12 * tokens * D,
            [pltpu.VMEM((lat, D), F32)],
        )(in_hbm(x), in_hbm(z), norms, in_hbm(read_in), in_hbm(read_out))

        q3 = []

        def fill_first(step):
            if step == 0:
                q3.append(narrow(mm(b1, write_in[0])))
                return q3[0]
            return None

        pieces = gather_rows(a2, n_blk, line, fill_first)
        q3 = q3[0]

        me = lax.axis_index("blk")
        distance, place = gather_places(n_blk, groups)
        places = (me ^ jnp.array(distance, jnp.int32)) * groups + jnp.array(place, jnp.int32)
        own_at = me * groups + jnp.arange(groups, dtype=jnp.int32)
        piece_shape = (n_blk // 2, lat // 2)
        hl2 = HEADS * lat
        a2_all, allowed, k2, v2, p2, l2, o2, z2, out_latents, b3, k3, v3 = call(
            self_forward_kernel, (1,),
            [smem] * 3 + [whole(piece_shape + (D,))] * 4 + [lat_spec, lat_spec, norm_spec, three, square,
             one_of(1), one_of(2)],
            [whole((total, D)), whole((hl2, total)), whole((total, D)), whole((total, D)), whole((hl2, total)),
             whole((hl2, 1))] + [lat_spec] * 6,
            [pltpu.HBM((total, D), BF), pltpu.HBM((hl2, total), F32), shaped((total, D), BF), shaped((total, D), BF),
             shaped((hl2, total), F32), shaped((hl2, 1), F32),
             far_lat, full_lat, low_lat, low_lat, full_lat, full_lat],
            unit_flops * 2, 10 * D * D * 2,
        )(group_image, places, own_at, *pieces, a2, z1, norms, self_in, self_out, write_in, write_in)

        resident = pl.BlockSpec(memory_space=pltpu.VMEM)
        pair_spec = pl.BlockSpec((2, size, D), lambda g: (0, g, 0))
        early_shape = (n_blk, 2 * rows, D)
        each = 1
        spans = rows_of((each * size, D))
        out_patches, h, gd, dq3, dx1, dk3, dv3, early_other, early_mine, gain4, shift4 = call(
            functools.partial(patch_kernel, D, size), (groups // each,),
            [smem] + [spans, spans, spans, lat_spec, lat_spec, norm_spec, square,
             resident, resident, spans, lat_spec],
            [spans, spans,
             pl.BlockSpec((2, each * size, hidden), lambda g: (0, g, 0), pipeline_mode=pl.Buffered(1 if each > 1 else 2)),
             spans, spans, lat_spec, lat_spec, whole(early_shape), whole(early_shape), fold_spec, fold_spec],
            [low_patch, far_patch, pltpu.HBM((2, tokens, hidden), BF),
             far_patch, pltpu.HBM((tokens, D), F32), full_lat, full_lat, shaped(early_shape, BF), shaped(early_shape, BF),
             far_fold, far_fold],
            unit_flops * 22, 40 * tokens * D, [pltpu.VMEM((tokens, D), BF)] * 4, vmem=48,
        )(core_at, in_hbm(x), in_hbm(q3), in_hbm(cot), k3, v3, norms, write_out, feed_up, feed_down, in_hbm(b1), b3)

        width = D + 128
        dz2, e2, payload, dq2, gain3, shift3 = call(
            latent_back_kernel, (1,),
            [lat_spec] * 4 + [whole((total, D))] * 2
            + [whole((hl2, total)), whole((hl2, 1)), norm_spec, one_of(1), one_of(2), square],
            [lat_spec] * 2 + [whole((lat, width)), lat_spec, fold_spec, fold_spec],
            [far_full, far_lat, shaped((lat, width), BF), far_lat, far_fold, far_fold],
            unit_flops, 10 * D * D,
        )(dk3, dv3, z2, cot_z, k2, v2, p2, l2, norms, write_in, write_in, self_out)
        line.note(payload)

        feed_specs = [
            pl.BlockSpec((None, tokens, D), lambda j, w: (w[0], 0, j)),
            pl.BlockSpec((tokens, D), lambda j, w: (0, 0), pipeline_mode=pl.Buffered(1)),
            pl.BlockSpec((tokens, D), lambda j, w: (0, 0), pipeline_mode=pl.Buffered(1)),
        ]

        def feed_call(kernel, in_specs, out_specs, out_shape, operands):
            return pl.pallas_call(
                kernel,
                grid_spec=pltpu.PrefetchScalarGridSpec(
                    num_scalar_prefetch=1, grid=(hidden // D,), in_specs=in_specs, out_specs=out_specs
                ),
                out_shape=out_shape,
                compiler_params=pltpu.CompilerParams(
                    vmem_limit_bytes=24 << 20, dimension_semantics=("arbitrary",)
                ),
                cost_estimate=pl.CostEstimate(
                    flops=unit_flops * 4, bytes_accessed=20 * tokens * D, transcendentals=0
                ),
            )(*line.gate(operands))

        def once(shape):
            return pl.BlockSpec(shape, lambda j, w: (0,) * len(shape), pipeline_mode=pl.Buffered(1))

        gd, h, e4 = in_hbm(gd), in_hbm(h), in_hbm(cot)
        half = feed_rows // 2
        first = Scatter(line, n_blk, orders)
        firsts = (orders[0][0], orders[1][0])

        def feed_other():
            shape = (n_blk, feed_rows, D)
            return feed_call(feed_kernel, feed_specs, once(shape), shaped(shape, BF), (other_at, gd, h, e4))

        def feed_mine(got):
            which = jnp.stack([core, own_bit(firsts[0]), own_bit(firsts[1])]).astype(jnp.int32)
            near = D // feed_rows
            shape = (n_blk // 2, half, D)
            return feed_call(
                functools.partial(feed_sum_kernel, firsts),
                feed_specs
                + [pl.BlockSpec((n_blk, rows, D), lambda j, w: (0, j, 0)),
                   pl.BlockSpec((near, feed_rows, D), lambda j, w: (j, 0, 0))],
                [once(shape)] * 4, [shaped(shape, BF)] * 4, (which, gd, h, e4, got, got),
            )

        whole_patch = whole((tokens, D))

        def core_swap(tensor):
            return swap(line.gate(tensor), "rep", 0, n_rep)

        early = {}

        def fill_second(step):
            if step == 0:
                early["got"] = core_swap(early_other)
                early["feed_other"] = feed_other()
                return early["feed_other"], early["got"]
            if step == 1:
                early["feed_got"] = core_swap(early["feed_other"])
                bit = orders[2][0]
                shape = (n_blk // 2, 2 * rows, D)
                early["sum"] = call(
                    functools.partial(cut_kernel, bit), (1,), [smem] + [whole(early_shape)] * 2,
                    [whole(shape)] * 2, [shaped(shape, BF)] * 2, 0, 12 * tokens * D,
                )(*line.gate((own_bit(bit).reshape(1).astype(jnp.int32), in_hbm(early_mine), in_hbm(early["got"]))))
                return early["sum"]
            if step == 3:
                early["feed"] = feed_mine(early["feed_got"])
                return early["feed"]
            return None

        spread_pieces = gather_rows(payload, n_blk, line, fill_second)
        feed0, feed1, feed2, feed3 = early["feed"]
        first.begin_cut([(feed0, feed1, half), (feed2, feed3, half), (*early["sum"], 2 * rows)])

        late_shape = (n_blk, 4 * rows, D)
        late_other, late_mine, dk1, dv1, dq1, dz1, gain2, shift2 = call(
            tail_kernel, grid,
            [smem] + [whole(piece_shape + (width,))] * 4
            + [whole((total, D)), whole((hl2, total)), whole((total, D)), whole((total, D))] + [lat_spec] * 3
            + [norm_spec, three, square, lat_spec, share_spec, patch_spec, patch_spec, whole_patch] + [lat_spec] * 5,
            [whole(late_shape)] * 2 + [whole_patch] * 2 + [lat_spec] * 2 + [fold_spec] * 2,
            [shaped(late_shape, BF), shaped(late_shape, BF), far_patch, far_patch, far_full, far_full, far_fold, far_fold],
            4 * unit_flops, 30 * tokens * D,
            [pltpu.VMEM((lat, D), F32)] + [pltpu.VMEM((lat, D), BF)] * 3,
            vmem=40,
        )(*line.gate((core_at, *spread_pieces, in_hbm(a2_all), in_hbm(allowed), k2, v2, in_hbm(dq2), in_hbm(z1), in_hbm(dz2), norms, self_in,
                      read_out, in_hbm(q1), in_hbm(p1), in_hbm(k1), in_hbm(v1), in_hbm(b1), in_hbm(a1), in_hbm(o1), in_hbm(a2),
                      in_hbm(o2), in_hbm(e2))))
        line.note((late_other, first.flying()))
        late_got = core_swap(late_other)
        first.send()
        line.note(late_got)
        last = Scatter(line, n_blk, orders)
        last_rows = 4 * rows // 3
        last_parts = last.cut([(late_mine, late_got, last_rows, i) for i in range(3)])
        line.note((last_parts, first.flying()))
        bits = bits_of(n_blk)
        first.send(far=first.step == bits - 2)
        line.note(first.flying())
        first.send(in_hbm)
        last.begin_cut(last_parts)
        dx, dz, norm_grads = call(
            input_back_kernel, grid,
            [patch_spec] * 5 + [lat_spec] * 3 + [norm_spec, three, one_of(0)] + [fold_spec] * 6,
            [patch_spec, lat_spec, norm_spec],
            [low_patch, low_lat, shaped((16, D), F32)],
            unit_flops * 3, 14 * tokens * D,
            [pltpu.VMEM((8, D), F32)] * 2,
        )(*line.gate((in_hbm(x), in_hbm(dx1), in_hbm(dq3), in_hbm(dk1), in_hbm(dv1), z, in_hbm(dz1), in_hbm(dq1), norms, read_in, write_in,
                      in_hbm(gain2), in_hbm(shift2), in_hbm(gain3), in_hbm(shift3), in_hbm(gain4), in_hbm(shift4))))
        line.note(dx)
        for bit in range(rep_bits):
            norm_grads = norm_grads + swap(line.gate(norm_grads), "rep", bit, n_rep)
        bits = bits_of(n_blk)

        def finish(flat):
            for bit in range(1, rep_bits):
                flat = narrow(flat.astype(F32) + swap(flat, "rep", bit, n_rep).astype(F32))
            return flat, swap(flat, "rep", 0, n_rep)

        def outputs(kernel, flat, partner, shapes):
            return call(
                kernel, (1,), [smem, whole(flat.shape), whole(flat.shape)], [whole(t) for t in shapes],
                [shaped(t, F32) for t in shapes], 0, 12 * flat.shape[0] * D,
            )(*line.gate((core_at, flat, partner)))

        for step in range(bits):
            got = swap(line.gate(norm_grads), "blk", step, n_blk)
            if step == 0:
                line.note((last.flying(), first.flying(), got))
            elif step == 1:
                last.send()
                while first.step < bits:
                    line.note(first.flying())
                    first.send()
                flat, partner = finish(first.result())
                up, down, wo, write_in_grad = outputs(
                    early_out_kernel, flat, partner, [(rows, hidden), (feed_rows, D), (rows, D), (3, rows, D)]
                )
                line.note((last.flying(), got, up))
            else:
                if last.step < bits:
                    last.send()
                line.note((last.flying(), got))
            norm_grads = norm_grads + got
        while last.step < bits:
            last.send()
            line.note(last.flying())
        flat, partner = finish(last.result())
        read_in_grad, read_out_grad, self_in_grad, self_out_grad = outputs(
            late_out_kernel, flat, partner, [(3, rows, D), (rows, D), (3, rows, D), (rows, D)]
        )
        norm_own = lax.dynamic_slice_in_dim(norm_grads, lax.axis_index("blk") * rows, rows, 1)
        return (
            out_patches[None], out_latents[None], dx[None], dz[None], norm_own[:5], norm_own[5:10],
            read_in_grad, read_out_grad, self_in_grad, self_out_grad, write_in_grad, wo, up, down,
        )

    return body


def solution(mesh):
    return jax.shard_map(
        make_body(mesh.shape["blk"], mesh.shape["rep"]),
        mesh=mesh,
        in_specs=(
            P("rep", "blk", None), P("rep", "blk", None), P(), P(), P(), P(), P(), P(), P(), P(), P(), P(),
            P("rep", None), P("rep", "blk", None), P("rep", "blk", None),
        ),
        out_specs=(
            P("rep", "blk", None), P("rep", "blk", None), P("rep", "blk", None), P("rep", "blk", None),
            P(None, "blk"), P(None, "blk"), P(None, "blk", None), P("blk", None), P(None, "blk", None),
            P("blk", None), P(None, "blk", None), P("blk", None), P("blk", None), P("blk", None),
        ),
        check_vma=False,
    )
```
